32 devices in a mesh: clips: 8 (over y, x, core), slab: 4 (over z).
Axes of the slice: x: 2, y: 2, z: 4, core: 2. Of those that a mesh axis runs over, the one named last changes fastest.
Arguments:
- video: bfloat16 [16, 6, 4, 16, 256], P('clips', None, 'slab'), may hold values from -6 to 6
- clip_blocks: int32 [16], replicated, may hold values from 1 to 3, 32 in all
- deal_order: int32 [8], replicated, may hold values from 0 to 7, each once
- kernel: bfloat16 [256, 3456], P('clips', 'slab'), may hold values from -0.078125 to 0.078125
- gain: float32 [128], replicated, may hold values from 0.25 to 1.75
- bias: float32 [128], replicated, may hold values from -3 to 3
- cotangent: bfloat16 [32, 2, 4, 16, 128], P('clips', None, 'slab'), may hold values from -6 to 6
Outputs:
- activations: bfloat16 [32, 2, 4, 16, 128], P('clips', None, 'slab')
- video_grad: bfloat16 [16, 6, 4, 16, 256], P('clips', None, 'slab')
- kernel_grad: float32 [256, 3456], P('clips', 'slab')
- gain_grad: float32 [128], replicated
- bias_grad: float32 [128], replicated
The draws below stay inside these ranges and needn't reach their ends.
Inputs may be any that keep to these rules, and one draw needn't show every extreme that they name: `clip_blocks`: the blocks of all clips add up to 4 times the number of devices along clips, so every device receives exactly 4 blocks; some clip has 3 blocks. `deal_order`: a permutation of the devices along clips.
All inputs are finite; a program needn't handle non-finite values.
Results may differ from the reference program's by a relative error of at most 0.0049.
Values may be sent and summed in bfloat16 or wider, within the bound.
No kernel may reach another device: no remote copies, remote signals or barrier semaphores. Data moves between devices by JAX's collectives and lax.ppermute only.
A program may use at most 64 MiB of HBM per device.

```python
import math
import jax
import jax.numpy as jnp
import numpy as np
from jax import lax

C_IN = 256
C_OUT = 128
GROUPS = 16
TAPS = 27
FB = 2
BMAX = 3
W = 16
CSL = 4
NCLIP = 16
FRAMES = 6
H = 4
N_CLIPS = 8


def level_of(rng, shape, split, least, largest):
    loudness = 1.0
    for dim, parts in split:
        heights = jax.random.uniform(jax.random.fold_in(jax.random.fold_in(rng, 6), dim), (parts,), jnp.float32, least / len(split), largest / len(split))
        loudness = loudness * jnp.repeat(jnp.exp(heights), shape[dim] // parts).reshape((-1,) + (1,) * (len(shape) - 1 - dim))
    return loudness


def length_profile(count, total, most, slope):
    loads = [(1 << 20) // math.isqrt(grade ** slope) + 1 for grade in range(2, count + 1)]
    surplus, given = total - most - (count - 1), [1] * (count - 1)
    while surplus > 0:
        movable = [i for i in range(count - 1) if given[i] < most]
        pool, left = sum([loads[i] for i in movable]), surplus
        for i in movable:
            extra = min(most - given[i], max(1, left * loads[i] // pool), surplus)
            given[i] = given[i] + extra
            surplus = surplus - extra
    return np.array([most] + given)


def ragged(rng, number_of, total, reach, slope):
    if number_of == 2:
        one = jax.random.randint(rng, (), max(1, total - reach), min(reach, total - 1) + 1)
        return jnp.stack([one, total - one])
    sizes = jnp.asarray(length_profile(number_of, total, reach, slope), jnp.int32)
    couples = (number_of - 1) // 2
    donor, sink = sizes[1:1 + 2 * couples:2], sizes[2:2 + 2 * couples:2]
    margin = jnp.minimum(donor - 1, reach - sink)
    moved = jax.random.randint(jax.random.fold_in(rng, 1), (couples,), 0, 1 << 20) % (margin + 1)
    sizes = sizes.at[1:1 + 2 * couples:2].set(donor - moved).at[2:2 + 2 * couples:2].set(sink + moved)
    return sizes[jax.random.permutation(jax.random.fold_in(rng, 2), number_of)]


def normal_values(stream_key, extent, scale, reach, split=(), kind=jnp.bfloat16):
    array = jax.random.normal(stream_key, extent, jnp.float32) * scale
    if len(split) > 0:
        array = level_of(stream_key, extent, split, -0.22, 0.18) * array
    return jnp.clip(array, min=-reach, max=reach).astype(kind)


def setup_inputs(seed: int = 0) -> dict:
    streams_of = jax.random.split(jax.random.key(seed), 8)
    video = normal_values(streams_of[0], (NCLIP, FRAMES, H, W, C_IN), 1.0, 6.0, ((0, 8), (2, 4)))
    clip_blocks = ragged(streams_of[1], NCLIP, CSL * N_CLIPS, BMAX, 2).astype(jnp.int32)
    deal_order = jax.random.permutation(streams_of[2], N_CLIPS).astype(jnp.int32)
    kernel = normal_values(streams_of[3], (C_IN, C_OUT * TAPS), (TAPS * C_IN) ** -0.5, 0.078125, ((0, 8), (1, 4)))
    gain = jnp.clip(1.0 + 0.15 * jax.random.normal(streams_of[4], (C_OUT,), jnp.float32), 0.25, 1.75)
    bias = normal_values(streams_of[5], (C_OUT,), 0.5, 3.0, (), jnp.float32)
    cotangent = normal_values(streams_of[6], (N_CLIPS * CSL, FB, H, W, C_OUT), 1.0, 6.0, ((0, 8), (2, 4)))
    return dict(video=video, clip_blocks=clip_blocks, deal_order=deal_order, kernel=kernel, gain=gain, bias=bias, cotangent=cotangent)


def clip_index(block_id, block_ends):
    return lax.optimization_barrier(jnp.sum((block_ends[None, :] <= block_id[:, None]).astype(jnp.int32), axis=1)).astype(jnp.int32)

def reference(video, clip_blocks, deal_order, kernel, gain, bias, cotangent):
    per_group = C_OUT // GROUPS
    kernel_taps = kernel.reshape(C_IN, C_OUT, TAPS).transpose(2, 0, 1)

    def conv_clip(clip):
        padded = jnp.pad(clip, ((2, 0), (1, 1), (1, 1), (0, 0)))
        totals = jnp.zeros((FRAMES * H * W, C_OUT), jnp.float32)
        for step_a in range(3):
            for step_b in range(3):
                for step_c in range(3):
                    tap_rows = padded[step_a:step_a + FRAMES, step_b:step_b + H, step_c:step_c + W].reshape(-1, C_IN)
                    totals = totals + jnp.dot(tap_rows, kernel_taps[(step_a * 3 + step_b) * 3 + step_c], preferred_element_type=jnp.float32)
        return totals.reshape(FRAMES, H, W, C_OUT)
    conv_out = lax.map(conv_clip, video)
    block_ends = jnp.cumsum(clip_blocks).astype(jnp.int32)
    block_starts = (block_ends - clip_blocks).astype(jnp.int32)
    frame_alive = jnp.arange(FRAMES, dtype=jnp.int32)[None, :] < (clip_blocks * FB)[:, None]
    alive_mask = frame_alive[:, :, None, None, None, None]
    grouped = conv_out.reshape(NCLIP, FRAMES, H, W, GROUPS, per_group)
    counts = (clip_blocks * (FB * H * W * per_group)).astype(jnp.float32)
    sum_first = lax.optimization_barrier(jnp.sum(jnp.where(alive_mask, grouped, 0.0), axis=(1, 2, 3, 5)))
    sum_second = lax.optimization_barrier(jnp.sum(jnp.where(alive_mask, grouped * grouped, 0.0), axis=(1, 2, 3, 5)))
    group_mean = sum_first / counts[:, None]
    group_var = sum_second / counts[:, None] - group_mean * group_mean
    inv_std = lax.rsqrt(group_var + 1e-05)

    def spread(stat):
        return stat[:, None, None, None, :, None]
    normed_groups = (grouped - spread(group_mean)) * spread(inv_std)
    normed = normed_groups.reshape(NCLIP, FRAMES, H, W, C_OUT)
    affine = normed * gain + bias
    act = jax.nn.silu(affine).astype(jnp.bfloat16)
    device_ids = jnp.arange(N_CLIPS, dtype=jnp.int32)
    deal_slot = lax.optimization_barrier(jnp.sum(jnp.where(deal_order[:, None] == device_ids[None, :], device_ids[:, None], 0), axis=0)).astype(jnp.int32)
    row_ids = jnp.arange(N_CLIPS * CSL, dtype=jnp.int32)
    block_id = row_ids % CSL * N_CLIPS + deal_slot[row_ids // CSL]
    clip_of = clip_index(block_id, block_ends)
    block_of = block_id - block_starts[clip_of]
    activations = act.reshape(NCLIP, BMAX, FB, H, W, C_OUT)[clip_of, block_of]
    block_range = jnp.arange(BMAX, dtype=jnp.int32)
    clip_block_id = block_starts[:, None] + block_range[None, :]
    block_alive = block_range[None, :] < clip_blocks[:, None]
    row_of = deal_order[clip_block_id % N_CLIPS] * CSL + clip_block_id // N_CLIPS
    row_of = jnp.where(block_alive, row_of, 0).astype(jnp.int32)
    grad_act = jnp.where(block_alive[:, :, None, None, None, None], cotangent[row_of].astype(jnp.float32), 0.0)
    grad_act = grad_act.reshape(NCLIP, FRAMES, H, W, C_OUT)
    sigmoid = jax.nn.sigmoid(affine)
    grad_affine = grad_act * sigmoid * (1.0 + affine * (1.0 - sigmoid))
    gain_grad = lax.optimization_barrier(jnp.sum(grad_affine * normed, axis=(0, 1, 2, 3)))
    bias_grad = lax.optimization_barrier(jnp.sum(grad_affine, axis=(0, 1, 2, 3)))
    grad_normed = (grad_affine * gain).reshape(NCLIP, FRAMES, H, W, GROUPS, per_group)
    sum_grad = lax.optimization_barrier(jnp.sum(jnp.where(alive_mask, grad_normed, 0.0), axis=(1, 2, 3, 5)))
    sum_cross = lax.optimization_barrier(jnp.sum(jnp.where(alive_mask, grad_normed * normed_groups, 0.0), axis=(1, 2, 3, 5)))
    mean_grad = sum_grad / counts[:, None]
    mean_cross = sum_cross / counts[:, None]
    grad_conv = spread(inv_std) * (grad_normed - spread(mean_grad) - normed_groups * spread(mean_cross))
    grad_conv = jnp.where(alive_mask, grad_conv, 0.0).reshape(NCLIP, FRAMES, H, W, C_OUT).astype(jnp.bfloat16)

    def backward_clip(carry, inputs):
        clip, grad_clip = inputs
        padded = jnp.pad(clip, ((2, 0), (1, 1), (1, 1), (0, 0)))
        grad_padded = jnp.pad(grad_clip, ((0, 2), (1, 1), (1, 1), (0, 0)))
        grad_flat = grad_clip.reshape(-1, C_OUT)
        totals = jnp.zeros((FRAMES * H * W, C_IN), jnp.float32)
        tap_terms = []
        for step_a in range(3):
            for step_b in range(3):
                for step_c in range(3):
                    tap = (step_a * 3 + step_b) * 3 + step_c
                    tap_rows = padded[step_a:step_a + FRAMES, step_b:step_b + H, step_c:step_c + W].reshape(-1, C_IN)
                    tap_terms.append(lax.dot_general(tap_rows, grad_flat, (((0,), (0,)), ((), ())), preferred_element_type=jnp.float32))
                    moved = grad_padded[2 - step_a:2 - step_a + FRAMES, 2 - step_b:2 - step_b + H, 2 - step_c:2 - step_c + W].reshape(-1, C_OUT)
                    totals = totals + lax.dot_general(moved, kernel_taps[tap], (((1,), (1,)), ((), ())), preferred_element_type=jnp.float32)
        return (carry + jnp.stack(tap_terms, axis=0), totals.reshape(FRAMES, H, W, C_IN).astype(jnp.bfloat16))
    kernel_sums, video_grad = lax.scan(backward_clip, jnp.zeros((TAPS, C_IN, C_OUT), jnp.float32), (video, grad_conv))
    kernel_grad = kernel_sums.transpose(1, 2, 0).reshape(C_IN, C_OUT * TAPS)
    return (activations, video_grad, kernel_grad, gain_grad, bias_grad)
```

```python
import functools

import jax
import jax.numpy as jnp
import numpy as np
from jax import lax
from jax.experimental import pallas as pl
from jax.experimental.pallas import tpu as pltpu
from jax.sharding import PartitionSpec as P

GROUPS = 16
TAPS = 27
FB = 2
BMAX = 3
LANES = 128
F32 = jnp.float32
BF16 = jnp.bfloat16
SMEM = pl.BlockSpec(memory_space=pltpu.SMEM)
VMEM = pl.BlockSpec(memory_space=pltpu.VMEM)
PARAMS = pltpu.CompilerParams(vmem_limit_bytes=48 * 1024 * 1024)


def round_up(value, unit):
    return -(-value // unit) * unit


def column_table(och, width):
    table = np.zeros((width, 9 * LANES), np.float32)
    for o in range(och):
        for a in range(3):
            for b in range(3):
                for e in range(3):
                    table[27 * o + 9 * a + 3 * b + e, (3 * b + e) * LANES + (2 - a) * och + o] = 1
    return table.astype(BF16)


def fold(values, slice_index, och):
    groups = LANES // och
    rows = round_up(-(-values.shape[0] // groups), 16)
    short = rows * groups - values.shape[0]
    if short:
        values = jnp.concatenate([values, jnp.zeros((short, LANES), values.dtype)], axis=0)
    lane_group = lax.broadcasted_iota(jnp.int32, (rows, LANES), 1) // och
    total = jnp.zeros((rows, LANES), F32)
    for g in range(groups):
        shift = jnp.mod((g - slice_index) * och + LANES, LANES)
        moved = pltpu.roll(values[g * rows : (g + 1) * rows], shift, 1)
        total = total + jnp.where(lane_group == g, moved, 0.0)
    return total


def first_block_of(blocks_ref, first_clip, clips):
    start = jnp.int32(0)
    for k in range(clips):
        start = start + jnp.where(k < first_clip, blocks_ref[k], 0)
    return start


def slot_holders(blocks_ref, order_ref, me, slots, clips, held, devs):
    residue = jnp.int32(0)
    for r in range(devs):
        residue = jnp.where(order_ref[r] == me, r, residue)
    clip_of = [jnp.int32(0)] * slots
    end = jnp.int32(0)
    for k in range(clips):
        end = end + blocks_ref[k]
        for q in range(slots):
            clip_of[q] = clip_of[q] + jnp.where(end <= q * devs + residue, 1, 0)
    return [jnp.minimum(c, clips - 1) // held for c in clip_of]


def pack_kernel(dims, blocks_ref, order_ref, kernel_ref, cot_ref, out_ref):
    devs, slots, clips, held, rows_in, cols, lane0 = dims
    me = lax.axis_index("clips")
    holders = slot_holders(blocks_ref, order_ref, me, slots, clips, held, devs)
    rows = out_ref.shape[1]
    weights = kernel_ref[...].astype(F32)
    weights = jnp.concatenate([weights, jnp.zeros((rows_in, lane0 - cols), F32)], axis=1)
    if rows > rows_in:
        weights = jnp.concatenate([weights, jnp.zeros((rows - rows_in, lane0), F32)], axis=0)
    weights = weights.astype(BF16)
    for d in range(devs):
        out_ref[d, :, 0:lane0] = weights
    for q in range(slots):
        out_ref[holders[q], :, lane0 : lane0 + LANES] = cot_ref[q]


def spread_kernel(dims, blocks_ref, order_ref, table_ref, received_ref, *outs):
    devs, slab, clips, held, rows_in, lane0, och = dims
    weights_ref, payload_refs = outs[0], outs[1:]
    me, own = lax.axis_index("clips"), lax.axis_index("slab")
    start = first_block_of(blocks_ref, me * held, clips)
    pieces = []
    for k in range(held):
        count = blocks_ref[me * held + k]
        for b in range(BMAX):
            source = order_ref[jnp.mod(start + b, devs)]
            piece = received_ref[source, :, lane0 : lane0 + LANES].astype(F32)
            pieces.append(jnp.where(b < count, piece, 0.0))
        start = start + count
    cot = jnp.concatenate(pieces, axis=0)
    for i, ref in enumerate(payload_refs):
        ref[...] = fold(cot, jnp.mod(own + i, slab), och).astype(BF16)
    weights = received_ref[:, :, 0:lane0]
    if weights.shape[1] > rows_in:
        weights = weights.astype(F32)[:, :rows_in].reshape(devs * rows_in, lane0).astype(BF16)
    else:
        weights = weights.reshape(devs * rows_in, lane0)
    weights_ref[...] = jnp.dot(weights, table_ref[...], preferred_element_type=F32).astype(BF16)


def split3(values):
    high = values.astype(BF16).astype(F32)
    rest = values - high
    middle = rest.astype(BF16).astype(F32)
    return [high, middle, rest - middle]


def main_kernel(dims, blocks_ref, order_ref, gain_ref, bias_ref, table_ref, weights_ref, *refs):
    devs, slab, clips, held, frames, columns, rows_in, cols, lane0, och, per_group = dims
    video_refs, cot_refs = refs[:slab], refs[slab : 2 * slab]
    out_ref, grad_ref, video_pad, cot_rows = refs[2 * slab :]
    me, own = lax.axis_index("clips"), lax.axis_index("slab")
    places = held * frames * columns
    per_clip = frames * columns
    c_in = video_pad.shape[2]
    groups = LANES // och
    video_pad[0] = jnp.zeros((places, c_in), BF16)
    video_pad[slab + 1] = jnp.zeros((places, c_in), BF16)
    for i in range(slab):
        row = jnp.mod(own - i + slab, slab)
        video_pad[row + 1] = video_refs[i][...]
        folded = cot_refs[i][...].astype(F32)
        parts = [folded[:, g * och : (g + 1) * och] for g in range(groups)]
        cot_rows[row] = jnp.concatenate(parts, axis=0)[:places]

    total = None
    for b in range(3):
        rows = video_pad[b : b + slab].reshape(slab * places, c_in)
        term = jnp.dot(rows, weights_ref[:, 384 * b : 384 * (b + 1)], preferred_element_type=F32)
        total = term if total is None else total + term
    column = lax.broadcasted_iota(jnp.int32, (slab * places, LANES), 0) % columns
    many = slab * places

    def from_left(values):
        return jnp.where(column > 0, pltpu.roll(values, 1, 0), 0.0)

    def from_right(values):
        return jnp.where(column < columns - 1, pltpu.roll(values, many - 1, 0), 0.0)

    mixed = (
        from_left(total[:, 0:LANES])
        + total[:, LANES : 2 * LANES]
        + from_right(total[:, 2 * LANES :])
    ).reshape(slab, places, LANES)
    frame_shifts = [mixed[:, :, a * och : (a + 1) * och] for a in range(3)]

    shift = jnp.mod(LANES - own * och, LANES)
    gain = pltpu.roll(jnp.broadcast_to(gain_ref[...], (8, LANES)), shift, 1)[0:1, :och]
    bias = pltpu.roll(jnp.broadcast_to(bias_ref[...], (8, LANES)), shift, 1)[0:1, :och]
    same = lax.broadcasted_iota(jnp.int32, (och, och), 0) // per_group
    same = (same == lax.broadcasted_iota(jnp.int32, (och, och), 1) // per_group).astype(F32)

    def group_mean_of(values, count):
        sums = jnp.sum(jnp.sum(values, axis=0), axis=0, keepdims=True)
        sums = jnp.broadcast_to(sums, (8, och))
        sums = jnp.dot(sums, same, precision=lax.Precision.HIGHEST, preferred_element_type=F32)
        return (sums[0:1] / count)[None]

    frame_of = lax.broadcasted_iota(jnp.int32, (slab, per_clip, och), 1) // columns
    gain_part = jnp.zeros((1, och), F32)
    bias_part = jnp.zeros((1, och), F32)
    start = first_block_of(blocks_ref, me * held, clips)
    conv_grads = []
    act_blocks = []
    for k in range(held):
        blocks = blocks_ref[me * held + k]
        conv = frame_shifts[0][:, k * per_clip : (k + 1) * per_clip]
        for a in (1, 2):
            part = frame_shifts[a][:, k * per_clip : (k + 1) * per_clip - a * columns]
            conv = conv + jnp.concatenate([jnp.zeros((slab, a * columns, och), F32), part], axis=1)
        alive = frame_of < blocks * FB
        count = (blocks * (FB * slab * columns * per_group)).astype(F32)
        kept = jnp.where(alive, conv, 0.0)
        mean = group_mean_of(kept, count)
        var = group_mean_of(kept * conv, count) - mean * mean
        inv_std = lax.rsqrt(var + 1e-05)
        normed = (conv - mean) * inv_std
        affine = normed * gain[None] + bias[None]
        sigmoid = jax.nn.sigmoid(affine)
        act = affine * sigmoid
        cot = cot_rows[:, k * per_clip : (k + 1) * per_clip, :]
        grad_affine = jnp.where(alive, cot * sigmoid * (1.0 + affine * (1.0 - sigmoid)), 0.0)
        gain_part += jnp.sum(jnp.sum(grad_affine * normed, axis=0), axis=0, keepdims=True)
        bias_part += jnp.sum(jnp.sum(grad_affine, axis=0), axis=0, keepdims=True)
        grad_normed = grad_affine * gain[None]
        mean_grad = group_mean_of(grad_normed, count)
        mean_cross = group_mean_of(grad_normed * normed, count)
        grad_conv = inv_std * (grad_normed - mean_grad - normed * mean_cross)
        grad_conv = jnp.where(alive, grad_conv, 0.0).astype(BF16).astype(F32)
        lanes = [grad_conv]
        for a in (1, 2):
            zeros = jnp.zeros((slab, a * columns, och), F32)
            lanes.append(jnp.concatenate([grad_conv[:, a * columns :], zeros], axis=1))
        if LANES > 3 * och:
            lanes.append(jnp.zeros((slab, per_clip, LANES - 3 * och), F32))
        conv_grads.append(jnp.concatenate(lanes, axis=2))
        rows = FB * columns
        for b in range(BMAX):
            block = [act[h, b * rows : (b + 1) * rows] for h in range(slab)]
            dest = order_ref[jnp.mod(start + b, devs)]
            act_blocks.append((b < blocks, dest, jnp.concatenate(block, axis=1).astype(BF16)))
        start = start + blocks

    grads = jnp.concatenate(conv_grads, axis=1).reshape(many, LANES)
    grad_ref[0] = jnp.zeros((places, 3 * LANES), BF16)
    grad_ref[slab + 1] = jnp.zeros((places, 3 * LANES), BF16)
    for e, shifted in enumerate((from_right(grads), grads, from_left(grads))):
        shifted = shifted.astype(BF16).reshape(slab, places, LANES)
        grad_ref[1 : slab + 1, :, e * LANES : (e + 1) * LANES] = shifted

    video_t = jnp.transpose(video_pad[1 : slab + 1].reshape(many, c_in))
    parts = []
    for b in range(3):
        moved = grad_ref[2 - b : 2 - b + slab].reshape(many, 3 * LANES)
        parts.append(jnp.dot(video_t, moved, preferred_element_type=F32).astype(BF16))
    native = lax.dot_general(
        jnp.concatenate(parts, axis=1),
        table_ref[...],
        (((1,), (1,)), ((), ())),
        preferred_element_type=F32,
    ).reshape(devs, rows_in, lane0)
    out_rows = out_ref.shape[1]
    if out_rows > rows_in:
        zeros = jnp.zeros((devs, out_rows - rows_in, lane0), F32)
        native = jnp.concatenate([native, zeros], axis=1)
    sums = split3(gain_part) + split3(bias_part)
    sums = jnp.concatenate(sums + [jnp.zeros((out_rows - 6, och), F32)], axis=0)
    fill = jnp.zeros((out_rows, LANES - och), F32)
    sums = jnp.concatenate([fill, sums], axis=1)
    out_ref[:, :, 0 : lane0 - LANES] = native[:, :, 0 : lane0 - LANES].astype(BF16)
    last = native[:, :, lane0 - LANES : lane0] + sums[None]
    out_ref[:, :, lane0 - LANES : lane0] = last.astype(BF16)
    for alive, dest, block in act_blocks:

        @pl.when(alive)
        def _(dest=dest, block=block):
            out_ref[dest, :, lane0 : lane0 + LANES] = block


def video_grad_kernel(slab, grad_ref, weights_ref, *outs):
    own = lax.axis_index("slab")
    for i, ref in enumerate(outs):
        row = jnp.mod(own + i, slab)
        total = None
        for b in range(3):
            term = lax.dot_general(
                grad_ref[row + 2 - b],
                weights_ref[:, 384 * b : 384 * (b + 1)],
                (((1,), (1,)), ((), ())),
                preferred_element_type=F32,
            )
            total = term if total is None else total + term
        ref[...] = total.astype(ref.dtype)


def settle_kernel(dims, blocks_ref, order_ref, received_ref, kernel_grad_ref, *payload_refs):
    devs, slab, slots, clips, held, rows_in, cols, lane0, och = dims
    me, own = lax.axis_index("clips"), lax.axis_index("slab")
    total = received_ref[0, :, 0:lane0].astype(F32)
    for d in range(1, devs):
        total = total + received_ref[d, :, 0:lane0].astype(F32)
    kernel_grad_ref[...] = total[:rows_in, :cols]
    sums = total[:, lane0 - och : lane0]
    pair = [sums[0:1] + (sums[1:2] + sums[2:3]), sums[3:4] + (sums[4:5] + sums[5:6])]
    sums = jnp.concatenate(split3(pair[0]) + split3(pair[1]) + [jnp.zeros((10, och), F32)], axis=0)
    sums = jnp.concatenate([sums, jnp.zeros((16, LANES - och), F32)], axis=1)
    holders = slot_holders(blocks_ref, order_ref, me, slots, clips, held, devs)
    acts = [received_ref[h, :, lane0 : lane0 + LANES].astype(F32) for h in holders]
    acts = jnp.concatenate(acts, axis=0)
    for i, ref in enumerate(payload_refs):
        folded = fold(acts, jnp.mod(own + i, slab), och)
        ref[...] = jnp.concatenate([folded, sums], axis=0).astype(BF16)


def finish_kernel(slab, och, *refs):
    grad_refs, payload_refs = refs[:slab], refs[slab : 2 * slab]
    video_grad_ref, act_ref, gain_ref, bias_ref = refs[2 * slab :]
    own = lax.axis_index("slab")
    total = grad_refs[0][...]
    for ref in grad_refs[1:]:
        total = total + ref[...].astype(F32)
    video_grad_ref[...] = total.astype(BF16)
    groups = LANES // och
    rows = payload_refs[0].shape[0] - 16
    lane_group = lax.broadcasted_iota(jnp.int32, (rows, LANES), 1) // och
    acts = [jnp.zeros((rows, LANES), F32)] * groups
    sums = jnp.zeros((16, LANES), F32)
    for i, ref in enumerate(payload_refs):
        source = jnp.mod(own - i + slab, slab)
        payload = ref[...].astype(F32)
        for g in range(groups):
            shift = jnp.mod((source - g) * och + LANES, LANES)
            moved = pltpu.roll(payload[:rows], shift, 1)
            acts[g] = acts[g] + jnp.where(lane_group == source, moved, 0.0)
        moved = pltpu.roll(payload[rows:], source * och, 1)
        sums = sums + jnp.where(lane_group[:16] == source, moved, 0.0)
    act_ref[...] = jnp.concatenate(acts, axis=0)[: act_ref.shape[0]].astype(BF16)
    gain_ref[...] = sums[0:1] + (sums[1:2] + sums[2:3])
    bias_ref[...] = sums[3:4] + (sums[4:5] + sums[5:6])


def call(kernel, outs, specs, scratch=()):
    return pl.pallas_call(
        kernel,
        out_shape=outs,
        in_specs=specs,
        out_specs=[VMEM] * len(outs),
        scratch_shapes=list(scratch),
        compiler_params=PARAMS,
    )


def shifts(arrays, axis):
    size = lax.axis_size(axis)
    moved = [arrays[0]]
    for i in range(1, size):
        moved.append(lax.ppermute(arrays[i], axis, [(j, (j + i) % size) for j in range(size)]))
    return moved


def body(video, clip_blocks, deal_order, kernel, gain, bias, cotangent):
    devs, slab = lax.axis_size("clips"), lax.axis_size("slab")
    held, frames, _, columns, c_in = video.shape
    slots, clips = cotangent.shape[0], clip_blocks.shape[0]
    c_out = gain.shape[0]
    rows_in, cols = kernel.shape
    och = c_out // slab
    per_group = c_out // GROUPS
    lane0 = round_up(cols, LANES)
    places = held * frames * columns
    block_rows = FB * columns
    out_rows = max(rows_in, block_rows)
    shape = jax.ShapeDtypeStruct
    table = jnp.asarray(column_table(och, lane0))
    gain, bias = gain.reshape(1, c_out), bias.reshape(1, c_out)

    packed = call(
        functools.partial(pack_kernel, (devs, slots, clips, held, rows_in, cols, lane0)),
        [shape((devs, out_rows, lane0 + LANES), BF16)],
        [SMEM, SMEM, VMEM, VMEM],
    )(clip_blocks, deal_order, kernel, cotangent.reshape(slots, block_rows, c_out))[0]
    received = lax.all_to_all(packed, "clips", split_axis=0, concat_axis=0, tiled=True)
    videos = shifts([video.reshape(places, c_in)] * slab, "slab")

    fold_rows = round_up(-(-places // (LANES // och)), 16)
    weights, *cots = call(
        functools.partial(spread_kernel, (devs, slab, clips, held, rows_in, lane0, och)),
        [shape((c_in, 9 * LANES), BF16)] + [shape((fold_rows, LANES), BF16)] * slab,
        [SMEM, SMEM, VMEM, VMEM],
    )(clip_blocks, deal_order, table, received)
    cots = shifts(cots, "slab")

    dims = (devs, slab, clips, held, frames, columns, rows_in, cols, lane0, och, per_group)
    packed, grads = call(
        functools.partial(main_kernel, dims),
        [
            shape((devs, out_rows, lane0 + LANES), BF16),
            shape((slab + 2, places, 3 * LANES), BF16),
        ],
        [SMEM, SMEM] + [VMEM] * (4 + 2 * slab),
        [
            pltpu.VMEM((slab + 2, places, c_in), BF16),
            pltpu.VMEM((slab, places, och), F32),
        ],
    )(clip_blocks, deal_order, gain, bias, table, weights, *videos, *cots)
    received = lax.all_to_all(packed, "clips", split_axis=0, concat_axis=0, tiled=True)

    video_grads = call(
        functools.partial(video_grad_kernel, slab),
        [shape((places, c_in), F32 if i == 0 else BF16) for i in range(slab)],
        [VMEM, VMEM],
    )(grads, weights)
    video_grads = shifts(video_grads, "slab")

    fold_rows = round_up(-(-slots * block_rows // (LANES // och)), 16)
    kernel_grad, *payloads = call(
        functools.partial(
            settle_kernel, (devs, slab, slots, clips, held, rows_in, cols, lane0, och)
        ),
        [shape((rows_in, cols), F32)] + [shape((fold_rows + 16, LANES), BF16)] * slab,
        [SMEM, SMEM, VMEM],
    )(clip_blocks, deal_order, received)
    payloads = shifts(payloads, "slab")

    video_grad, act, gain_grad, bias_grad = call(
        functools.partial(finish_kernel, slab, och),
        [
            shape((places, c_in), BF16),
            shape((slots * block_rows, c_out), BF16),
            shape((1, c_out), F32),
            shape((1, c_out), F32),
        ],
        [VMEM] * (2 * slab),
    )(*video_grads, *payloads)
    return (
        act.reshape(cotangent.shape),
        video_grad.reshape(video.shape),
        kernel_grad,
        gain_grad.reshape(c_out),
        bias_grad.reshape(c_out),
    )


def solution(mesh):
    return jax.shard_map(
        body,
        mesh=mesh,
        in_specs=(
            P("clips", None, "slab", None, None),
            P(),
            P(),
            P("clips", "slab"),
            P(),
            P(),
            P("clips", None, "slab", None, None),
        ),
        out_specs=(
            P("clips", None, "slab", None, None),
            P("clips", None, "slab", None, None),
            P("clips", "slab"),
            P(),
            P(),
        ),
        check_vma=False,
    )
```

```python
import functools

import jax
import jax.numpy as jnp
from jax import lax
from jax.experimental import pallas as pl
from jax.experimental.pallas import tpu as pltpu
from jax.sharding import PartitionSpec as P

GROUPS = 16
TAPS = 27
FB = 2
BMAX = 3
LANES = 128
F32 = jnp.float32
BF16 = jnp.bfloat16
HBM = pl.BlockSpec(memory_space=pltpu.HBM)
VMEM = pl.BlockSpec(memory_space=pltpu.VMEM)
MIB = 1024 * 1024
FIRST = 10**6
STAGE = 10**10


def round_up(value, unit):
    return -(-value // unit) * unit


def fold(values, slice_index, och, unit):
    groups = LANES // och
    rows = round_up(-(-values.shape[0] // groups), unit)
    short = rows * groups - values.shape[0]
    if short:
        values = jnp.concatenate([values, jnp.zeros((short, LANES), values.dtype)], axis=0)
    lane_group = lax.broadcasted_iota(jnp.int32, (rows, LANES), 1) // och
    total = jnp.zeros((rows, LANES), F32)
    for g in range(groups):
        shift = (g - slice_index) * och % LANES
        moved = pltpu.roll(values[g * rows : (g + 1) * rows], shift, 1) if shift else values[g * rows : (g + 1) * rows]
        total = total + jnp.where(lane_group == g, moved, 0.0)
    return total


def first_block_of(blocks_ref, first_clip, clips):
    start = jnp.int32(0)
    for k in range(clips):
        start = start + jnp.where(k < first_clip, blocks_ref[k], 0)
    return start


def slot_holders(blocks_ref, order_ref, me, slots, clips, held, devs):
    residue = jnp.int32(0)
    for r in range(devs):
        residue = jnp.where(order_ref[r] == me, r, residue)
    clip_of = [jnp.int32(0)] * slots
    end = jnp.int32(0)
    for k in range(clips):
        end = end + blocks_ref[k]
        for q in range(slots):
            clip_of[q] = clip_of[q] + jnp.where(end <= q * devs + residue, 1, 0)
    return [jnp.minimum(c, clips - 1) // held for c in clip_of]


def split3(values):
    high = values.astype(BF16).astype(F32)
    rest = values - high
    middle = rest.astype(BF16).astype(F32)
    return [high, middle, rest - middle]


def fetch(pairs, sems):
    copies = [pltpu.make_async_copy(a, b, sems.at[i]) for i, (a, b) in enumerate(pairs)]
    for copy in copies:
        copy.start()
    return copies


def send_kernel(
    dims, blocks_hbm, order_hbm, cot_hbm, kernel_hbm, out_ref, shard_ref, blocks_ref, order_ref, cot_ref, sems
):
    devs, slab, slots, clips, held, och = dims
    pairs = [(blocks_hbm, blocks_ref), (order_hbm, order_ref), (cot_hbm, cot_ref), (kernel_hbm, shard_ref)]
    for copy in fetch(pairs, sems):
        copy.wait()
    me = lax.axis_index("clips")
    holders = slot_holders(blocks_ref, order_ref, me, slots, clips, held, devs)
    for q in range(slots):
        block = cot_ref[q].astype(F32)
        for s in range(slab):
            out_ref[holders[q] * slab + s] = fold(block, s, och, 8).astype(BF16)


def make_table(och, out_ref):
    rows = out_ref.shape[0]
    lane = lax.broadcasted_iota(jnp.int32, (8, LANES), 1)
    source = jnp.where(lane < 3 * och, 27 * (lane % och) + 9 * (2 - lane // och), -rows)
    ahead = source - lax.broadcasted_iota(jnp.int32, (8, LANES), 0)
    for group in range(9):
        for i in range(0, rows, 16):
            top = jnp.where(ahead == i - group, 1.0, 0.0)
            bottom = jnp.where(ahead == i + 8 - group, 1.0, 0.0)
            both = jnp.concatenate([top, bottom], axis=0).astype(BF16)
            out_ref[i : i + 16, group * LANES : (group + 1) * LANES] = both


def stage_kernel(slab, *refs):
    video_refs, video_pad = refs[:slab], refs[slab]
    own = lax.axis_index("slab")
    zeros = jnp.zeros(video_pad.shape[1:], BF16)
    video_pad[0] = zeros
    video_pad[slab + 1] = zeros
    for i in range(slab):
        video_pad[jnp.mod(own - i + slab, slab) + 1] = video_refs[i][...]


def forward_kernel(dims, blocks_hbm, *refs):
    devs, slab, clips, held, frames, columns, rows_in, cols, och, per_group = dims
    shard_refs, video_pad = refs[:devs], refs[devs]
    weights_ref, normed_ref, inv_ref, table_ref, shards, blocks_ref, sems = refs[devs + 1 :]
    make_table(och, table_ref)
    copy = fetch([(blocks_hbm, blocks_ref)], sems)[0]
    me = lax.axis_index("clips")
    places = held * frames * columns
    per_clip = frames * columns
    c_in = video_pad.shape[2]
    many = slab * places
    width = table_ref.shape[0]
    chips = devs // 2
    for t in range(chips):
        for e in range(2):
            source = 2 * partner(me // 2, t, chips) + (me % 2 + e) % 2
            shard = shard_refs[t + e * chips][...].astype(F32)
            shards[source] = jnp.concatenate([shard, jnp.zeros((rows_in, width - cols), F32)], axis=1)
    weights = shards[...].reshape(c_in, width).astype(BF16)
    weights_ref[...] = jnp.dot(weights, table_ref[...], preferred_element_type=F32).astype(BF16)

    total = None
    for b in range(3):
        rows = video_pad[b : b + slab].reshape(many, c_in)
        term = jnp.dot(rows, weights_ref[:, 384 * b : 384 * (b + 1)], preferred_element_type=F32)
        total = term if total is None else total + term
    mixed = (
        from_left(total[:, 0:LANES], columns)
        + total[:, LANES : 2 * LANES]
        + from_right(total[:, 2 * LANES :], columns)
    ).reshape(slab, places, LANES)
    frame_shifts = [mixed[:, :, a * och : (a + 1) * och] for a in range(3)]
    frame_of = lax.broadcasted_iota(jnp.int32, (slab, per_clip, och), 1) // columns
    copy.wait()
    for k in range(held):
        blocks = blocks_ref[me * held + k]
        conv = frame_shifts[0][:, k * per_clip : (k + 1) * per_clip]
        for a in (1, 2):
            part = frame_shifts[a][:, k * per_clip : (k + 1) * per_clip - a * columns]
            conv = conv + jnp.concatenate([jnp.zeros((slab, a * columns, och), F32), part], axis=1)
        alive = frame_of < blocks * FB
        count = (blocks * (FB * slab * columns * per_group)).astype(F32)
        kept = jnp.where(alive, conv, 0.0)
        mean = group_mean_of(kept, count, per_group)
        var = group_mean_of(kept * conv, count, per_group) - mean * mean
        inv_std = lax.rsqrt(var + 1e-05)
        normed_ref[:, k * per_clip : (k + 1) * per_clip, :] = (conv - mean) * inv_std
        inv_ref[k] = jnp.broadcast_to(inv_std[0], (8, och))


def from_left(values, columns):
    column = lax.broadcasted_iota(jnp.int32, values.shape, 0) % columns
    return jnp.where(column > 0, pltpu.roll(values, 1, 0), 0.0)


def from_right(values, columns):
    column = lax.broadcasted_iota(jnp.int32, values.shape, 0) % columns
    return jnp.where(column < columns - 1, pltpu.roll(values, values.shape[0] - 1, 0), 0.0)


def group_mean_of(values, count, per_group):
    och = values.shape[-1]
    same = lax.broadcasted_iota(jnp.int32, (och, och), 0) // per_group
    same = (same == lax.broadcasted_iota(jnp.int32, (och, och), 1) // per_group).astype(F32)
    sums = jnp.sum(jnp.sum(values, axis=0), axis=0, keepdims=True)
    sums = jnp.broadcast_to(sums, (8, och))
    sums = jnp.dot(sums, same, precision=lax.Precision.HIGHEST, preferred_element_type=F32)
    return (sums[0:1] / count)[None]


def backward_kernel(dims, blocks_hbm, order_hbm, gain_ref, bias_ref, weights_ref, *refs):
    devs, slab, clips, held, frames, columns, rows_in, cols, och, per_group = dims
    video_pad, normed_ref, inv_ref, cot_ref = refs[:4]
    act_hbm, keep_ref, send_ref = refs[4:7]
    video_grad_refs = refs[7 : 7 + slab]
    table_ref, act_ref, grad_ref, blocks_ref, order_ref, sems = refs[7 + slab :]
    copies = fetch([(blocks_hbm, blocks_ref), (order_hbm, order_ref)], sems)
    make_table(och, table_ref)
    me, own = lax.axis_index("clips"), lax.axis_index("slab")
    places = held * frames * columns
    per_clip = frames * columns
    block_rows = FB * columns
    c_in = video_pad.shape[2]
    groups = LANES // och
    many = slab * places
    shift = jnp.mod(LANES - own * och, LANES)
    gain = pltpu.roll(jnp.broadcast_to(gain_ref[...], (8, LANES)), shift, 1)[0:1, :och]
    bias = pltpu.roll(jnp.broadcast_to(bias_ref[...], (8, LANES)), shift, 1)[0:1, :och]
    frame_of = lax.broadcasted_iota(jnp.int32, (slab, per_clip, och), 1) // columns
    gain_part = jnp.zeros((1, och), F32)
    bias_part = jnp.zeros((1, och), F32)
    for copy in copies:
        copy.wait()
    start = first_block_of(blocks_ref, me * held, clips)
    conv_grads = []
    act_blocks = []
    for k in range(held):
        blocks = blocks_ref[me * held + k]
        cot = []
        for b in range(BMAX):
            device = order_ref[jnp.mod(start + b, devs)]
            rows = []
            for s in range(slab):
                folded = cot_ref[device * slab + s].astype(F32)
                parts = [folded[:, g * och : (g + 1) * och] for g in range(groups)]
                rows.append(jnp.concatenate(parts, axis=0)[:block_rows])
            cot.append(jnp.stack(rows, axis=0))
        cot = jnp.concatenate(cot, axis=1)
        alive = frame_of < blocks * FB
        count = (blocks * (FB * slab * columns * per_group)).astype(F32)
        inv_std = inv_ref[k][None, 0:1]
        normed = normed_ref[:, k * per_clip : (k + 1) * per_clip, :]
        affine = normed * gain[None] + bias[None]
        sigmoid = jax.nn.sigmoid(affine)
        act = affine * sigmoid
        grad_affine = jnp.where(alive, cot * sigmoid * (1.0 + affine * (1.0 - sigmoid)), 0.0)
        gain_part += jnp.sum(jnp.sum(grad_affine * normed, axis=0), axis=0, keepdims=True)
        bias_part += jnp.sum(jnp.sum(grad_affine, axis=0), axis=0, keepdims=True)
        grad_normed = grad_affine * gain[None]
        mean_grad = group_mean_of(grad_normed, count, per_group)
        mean_cross = group_mean_of(grad_normed * normed, count, per_group)
        grad_conv = inv_std * (grad_normed - mean_grad - normed * mean_cross)
        grad_conv = jnp.where(alive, grad_conv, 0.0).astype(BF16).astype(F32)
        lanes = [grad_conv]
        for a in (1, 2):
            zeros = jnp.zeros((slab, a * columns, och), F32)
            lanes.append(jnp.concatenate([grad_conv[:, a * columns :], zeros], axis=1))
        if LANES > 3 * och:
            lanes.append(jnp.zeros((slab, per_clip, LANES - 3 * och), F32))
        conv_grads.append(jnp.concatenate(lanes, axis=2))
        for b in range(BMAX):
            device = order_ref[jnp.mod(start + b, devs)]
            for h in range(slab):
                block = unfolded_to_lanes(act[h, b * block_rows : (b + 1) * block_rows], 8)
                act_blocks.append((b < blocks, device * slab + h, block))
        start = start + blocks

    sums = split3(gain_part) + split3(bias_part) + [jnp.zeros((2, och), F32)]
    sums = jnp.concatenate(sums, axis=0)
    sums = jnp.concatenate([sums, jnp.zeros((8, LANES - och), F32)], axis=1)
    nothing = jnp.concatenate([jnp.zeros_like(act_blocks[0][2]), sums], axis=0).astype(BF16)
    for d in range(devs * slab):
        act_ref[d] = nothing
    for alive, dest, block in act_blocks:

        @pl.when(alive)
        def _(dest=dest, block=block):
            act_ref[dest] = jnp.concatenate([block, sums], axis=0).astype(BF16)

    act_copy = pltpu.make_async_copy(act_ref, act_hbm, sems.at[2])
    act_copy.start()

    grads = jnp.concatenate(conv_grads, axis=1).reshape(many, LANES)
    grad_ref[0] = jnp.zeros((places, 3 * LANES), BF16)
    grad_ref[slab + 1] = jnp.zeros((places, 3 * LANES), BF16)
    for e, shifted in enumerate((from_right(grads, columns), grads, from_left(grads, columns))):
        shifted = shifted.astype(BF16).reshape(slab, places, LANES)
        grad_ref[1 : slab + 1, :, e * LANES : (e + 1) * LANES] = shifted

    for i, ref in enumerate(video_grad_refs):
        row = jnp.mod(own + i, slab)
        total = None
        for b in range(3):
            term = lax.dot_general(
                grad_ref[row + 2 - b],
                weights_ref[:, 384 * b : 384 * (b + 1)],
                (((1,), (1,)), ((), ())),
                preferred_element_type=F32,
            )
            total = term if total is None else total + term
        ref[...] = total.astype(ref.dtype)

    video_t = jnp.transpose(video_pad[1 : slab + 1].reshape(many, c_in))
    parts = []
    for b in range(3):
        moved = grad_ref[2 - b : 2 - b + slab].reshape(many, 3 * LANES)
        parts.append(jnp.dot(video_t, moved, preferred_element_type=F32).astype(BF16))
    native = lax.dot_general(
        jnp.concatenate(parts, axis=1),
        table_ref[...],
        (((1,), (1,)), ((), ())),
        preferred_element_type=F32,
    ).reshape(devs // 2, 2 * rows_in, table_ref.shape[0])
    low, high = native[:, :rows_in, :cols], native[:, rows_in:, :cols]
    odd = me % 2 == 1
    keep_ref[...] = jnp.where(odd, high, low)
    send_ref[...] = jnp.where(odd, low, high).astype(BF16)
    act_copy.wait()


def unfolded_to_lanes(values, unit):
    groups = LANES // values.shape[1]
    rows = round_up(-(-values.shape[0] // groups), unit)
    short = rows * groups - values.shape[0]
    if short:
        values = jnp.concatenate([values, jnp.zeros((short, values.shape[1]), F32)], axis=0)
    return jnp.concatenate([values[g * rows : (g + 1) * rows] for g in range(groups)], axis=1)


def pair_kernel(chips, keep_ref, other_ref, *outs):
    me = lax.axis_index("clips") // 2
    for t, ref in enumerate(outs):
        chip = partner(me, t, chips)
        ref[...] = (keep_ref[chip] + other_ref[chip].astype(F32)).astype(ref.dtype)


def finish_kernel(dims, blocks_hbm, order_hbm, act_in, *refs):
    devs, slab, slots, clips, held, och = dims
    chips = devs // 2
    kernel_refs, grad_refs = refs[:chips], refs[chips : chips + slab]
    kernel_grad_ref, video_grad_ref, act_ref, gain_ref, bias_ref = refs[chips + slab : -3]
    blocks_ref, order_ref, sems = refs[-3:]
    copies = fetch([(blocks_hbm, blocks_ref), (order_hbm, order_ref)], sems)
    total = kernel_refs[0][...]
    for ref in kernel_refs[1:]:
        total = total + ref[...].astype(F32)
    kernel_grad_ref[...] = total
    total = grad_refs[0][...]
    for ref in grad_refs[1:]:
        total = total + ref[...].astype(F32)
    video_grad_ref[...] = total.astype(BF16)
    groups = LANES // och
    rows = act_in.shape[1] - 8
    sums = []
    for s in range(slab):
        part = act_in[s].astype(F32)[rows:]
        for d in range(1, devs):
            part = part + act_in[d * slab + s].astype(F32)[rows:]
        sums.append(part[:, :och])
    sums = jnp.concatenate(sums, axis=1)
    gain_ref[...] = sums[0:1] + (sums[1:2] + sums[2:3])
    bias_ref[...] = sums[3:4] + (sums[4:5] + sums[5:6])
    for copy in copies:
        copy.wait()
    me = lax.axis_index("clips")
    holders = slot_holders(blocks_ref, order_ref, me, slots, clips, held, devs)
    for q in range(slots):
        parts = [act_in[holders[q] * slab + s].astype(F32)[:rows] for s in range(slab)]
        block = []
        for g in range(groups):
            block.append(jnp.concatenate([p[:, g * och : (g + 1) * och] for p in parts], axis=1))
        act_ref[q] = jnp.concatenate(block, axis=0)[: act_ref.shape[1]].astype(BF16)


def call(kernel, outs, specs, scratch=(), limit=4 * MIB, out_specs=None, cost=None):
    return pl.pallas_call(
        kernel,
        out_shape=outs,
        in_specs=specs,
        out_specs=out_specs or [VMEM] * len(outs),
        cost_estimate=cost,
        scratch_shapes=list(scratch),
        compiler_params=pltpu.CompilerParams(vmem_limit_bytes=limit),
    )


def partner(index, step, size):
    return index ^ step if size & (size - 1) == 0 else (index + step) % size


def shifts(arrays, axis):
    size = lax.axis_size(axis)
    moved = [arrays[0]]
    for i in range(1, size):
        moved.append(lax.ppermute(arrays[i], axis, [(j, (j + i) % size) for j in range(size)]))
    return moved


def chip_swaps(arrays, axis):
    size = lax.axis_size(axis)
    moved = [arrays[0]]
    for t in range(1, size // 2):
        pairs = [(j, 2 * partner(j // 2, t, size // 2) + j % 2) for j in range(size)]
        moved.append(lax.ppermute(arrays[t], axis, pairs))
    return moved


def core_swap(array, axis):
    return lax.ppermute(array, axis, [(j, j ^ 1) for j in range(lax.axis_size(axis))])


def body(video, clip_blocks, deal_order, kernel, gain, bias, cotangent):
    devs, slab = lax.axis_size("clips"), lax.axis_size("slab")
    held, frames, _, columns, c_in = video.shape
    slots, clips = cotangent.shape[0], clip_blocks.shape[0]
    c_out = gain.shape[0]
    rows_in, cols = kernel.shape
    och = c_out // slab
    per_group = c_out // GROUPS
    width = round_up(cols, LANES)
    places = held * frames * columns
    block_rows = FB * columns
    fold_rows = round_up(-(-block_rows // (LANES // och)), 8)
    chips = devs // 2
    everyone = ("clips", "slab")
    shape = jax.ShapeDtypeStruct
    smem = [pltpu.SMEM((clips,), jnp.int32), pltpu.SMEM((devs,), jnp.int32)]
    large = (6 + 3 * slab) * MIB
    gain, bias = gain.reshape(1, c_out), bias.reshape(1, c_out)
    clip_blocks = pltpu.with_memory_space_constraint(clip_blocks, pltpu.HBM)
    deal_order = pltpu.with_memory_space_constraint(deal_order, pltpu.HBM)
    kernel = pltpu.with_memory_space_constraint(kernel, pltpu.HBM)
    cotangent_blocks = pltpu.with_memory_space_constraint(
        cotangent.reshape(slots, block_rows, c_out), pltpu.HBM
    )

    videos = shifts([video.reshape(places, c_in)] * slab, "slab")
    cots, shard = call(
        functools.partial(send_kernel, (devs, slab, slots, clips, held, och)),
        [shape((devs * slab, fold_rows, LANES), BF16), shape((rows_in, cols), BF16)],
        [HBM, HBM, HBM, HBM],
        smem + [pltpu.VMEM((slots, block_rows, c_out), BF16), pltpu.SemaphoreType.DMA((4,))],
        cost=pl.CostEstimate(flops=FIRST, bytes_accessed=0, transcendentals=0),
    )(clip_blocks, deal_order, cotangent_blocks, kernel)
    cots = lax.all_to_all(cots, everyone, split_axis=0, concat_axis=0, tiled=True)
    shards = chip_swaps([shard] * chips, "clips")
    shards = shards + [core_swap(shard, "clips") for shard in shards]

    dims = (devs, slab, clips, held, frames, columns, rows_in, cols, och, per_group)
    video_pad = call(
        functools.partial(stage_kernel, slab),
        [shape((slab + 2, places, c_in), BF16)],
        [VMEM] * slab,
        cost=pl.CostEstimate(flops=STAGE, bytes_accessed=0, transcendentals=0),
    )(*videos)[0]
    weights, normed, inv_std = call(
        functools.partial(forward_kernel, dims),
        [
            shape((c_in, 9 * LANES), BF16),
            shape((slab, places, och), F32),
            shape((held, 8, och), F32),
        ],
        [HBM] + [VMEM] * (devs + 1),
        [
            pltpu.VMEM((width, 9 * LANES), BF16),
            pltpu.VMEM((devs, rows_in, width), F32),
            smem[0],
            pltpu.SemaphoreType.DMA((1,)),
        ],
        large,
    )(clip_blocks, *shards, video_pad)
    acts, keep, send, *video_grads = call(
        functools.partial(backward_kernel, dims),
        [
            pltpu.HBM((devs * slab, fold_rows + 8, LANES), BF16),
            shape((chips, rows_in, cols), F32),
            shape((chips, rows_in, cols), BF16),
        ]
        + [shape((places, c_in), F32 if i == 0 else BF16) for i in range(slab)],
        [HBM, HBM] + [VMEM] * 7,
        [
            pltpu.VMEM((width, 9 * LANES), BF16),
            pltpu.VMEM((devs * slab, fold_rows + 8, LANES), BF16),
            pltpu.VMEM((slab + 2, places, 3 * LANES), BF16),
        ]
        + smem
        + [pltpu.SemaphoreType.DMA((3,))],
        large,
        [HBM] + [VMEM] * (2 + slab),
    )(clip_blocks, deal_order, gain, bias, weights, video_pad, normed, inv_std, cots)
    video_grads = shifts(video_grads, "slab")
    send = core_swap(send, "clips")
    acts = lax.all_to_all(acts, everyone, split_axis=0, concat_axis=0, tiled=True)
    kernel_grads = call(
        functools.partial(pair_kernel, chips),
        [shape((rows_in, cols), F32 if t == 0 else BF16) for t in range(chips)],
        [VMEM, VMEM],
    )(keep, send)
    kernel_grads = chip_swaps(kernel_grads, "clips")

    kernel_grad, video_grad, act, gain_grad, bias_grad = call(
        functools.partial(finish_kernel, (devs, slab, slots, clips, held, och)),
        [
            shape((rows_in, cols), F32),
            shape((places, c_in), BF16),
            shape((slots, block_rows, c_out), BF16),
            shape((1, c_out), F32),
            shape((1, c_out), F32),
        ],
        [HBM, HBM] + [VMEM] * (1 + chips + slab),
        smem + [pltpu.SemaphoreType.DMA((2,))],
    )(clip_blocks, deal_order, acts, *kernel_grads, *video_grads)
    return (
        act.reshape(cotangent.shape),
        video_grad.reshape(video.shape),
        kernel_grad,
        gain_grad.reshape(c_out),
        bias_grad.reshape(c_out),
    )


def solution(mesh):
    return jax.shard_map(
        body,
        mesh=mesh,
        in_specs=(
            P("clips", None, "slab", None, None),
            P(),
            P(),
            P("clips", "slab"),
            P(),
            P(),
            P("clips", None, "slab", None, None),
        ),
        out_specs=(
            P("clips", None, "slab", None, None),
            P("clips", None, "slab", None, None),
            P("clips", "slab"),
            P(),
            P(),
        ),
        check_vma=False,
    )
```

```python
import functools

import jax
import jax.numpy as jnp
from jax import lax
from jax.experimental import pallas as pl
from jax.experimental.pallas import tpu as pltpu
from jax.sharding import PartitionSpec as P

GROUPS = 16
TAPS = 27
FB = 2
BMAX = 3
LANES = 128
F32 = jnp.float32
BF16 = jnp.bfloat16
HBM = pl.BlockSpec(memory_space=pltpu.HBM)
ANY = pl.BlockSpec(memory_space=pl.ANY)
VMEM = pl.BlockSpec(memory_space=pltpu.VMEM)
MIB = 1024 * 1024
FIRST = 10**6
STAGE = 10**10


def round_up(value, unit):
    return -(-value // unit) * unit


def fold(values, slice_index, och, unit):
    groups = LANES // och
    rows = round_up(-(-values.shape[0] // groups), unit)
    short = rows * groups - values.shape[0]
    if short:
        values = jnp.concatenate([values, jnp.zeros((short, LANES), values.dtype)], axis=0)
    lane_group = lax.broadcasted_iota(jnp.int32, (rows, LANES), 1) // och
    total = jnp.zeros((rows, LANES), F32)
    for g in range(groups):
        shift = (g - slice_index) * och % LANES
        moved = pltpu.roll(values[g * rows : (g + 1) * rows], shift, 1) if shift else values[g * rows : (g + 1) * rows]
        total = total + jnp.where(lane_group == g, moved, 0.0)
    return total


def first_block_of(blocks_ref, first_clip, clips):
    start = jnp.int32(0)
    for k in range(clips):
        start = start + jnp.where(k < first_clip, blocks_ref[k], 0)
    return start


def slot_holders(blocks_ref, order_ref, me, slots, clips, held, devs):
    residue = jnp.int32(0)
    for r in range(devs):
        residue = jnp.where(order_ref[r] == me, r, residue)
    clip_of = [jnp.int32(0)] * slots
    end = jnp.int32(0)
    for k in range(clips):
        end = end + blocks_ref[k]
        for q in range(slots):
            clip_of[q] = clip_of[q] + jnp.where(end <= q * devs + residue, 1, 0)
    return [jnp.minimum(c, clips - 1) // held for c in clip_of]


def split3(values):
    high = values.astype(BF16).astype(F32)
    rest = values - high
    middle = rest.astype(BF16).astype(F32)
    return [high, middle, rest - middle]


def fetch(pairs, sems):
    copies = [pltpu.make_async_copy(a, b, sems.at[i]) for i, (a, b) in enumerate(pairs)]
    for copy in copies:
        copy.start()
    return copies


def send_kernel(
    dims, blocks_hbm, order_hbm, cot_hbm, out_ref, holds_ref, blocks_ref, order_ref, cot_ref, sems
):
    devs, slab, slots, clips, held, och = dims
    pairs = [(blocks_hbm, blocks_ref), (order_hbm, order_ref), (cot_hbm, cot_ref)]
    for copy in fetch(pairs, sems):
        copy.wait()
    me = lax.axis_index("clips")
    holders = slot_holders(blocks_ref, order_ref, me, slots, clips, held, devs)
    for q in range(slots):
        block = cot_ref[q].astype(F32)
        for s in range(slab):
            out_ref[holders[q] * slab + s] = fold(block, s, och, 8).astype(BF16)
        for d in range(devs):
            holds_ref[q * devs + d] = jnp.full((1, LANES), jnp.where(holders[q] == d, 1.0, 0.0), F32)


def make_table(och, out_ref):
    rows = out_ref.shape[0]
    lane = lax.broadcasted_iota(jnp.int32, (8, LANES), 1)
    source = jnp.where(lane < 3 * och, 27 * (lane % och) + 9 * (2 - lane // och), -rows)
    ahead = source - lax.broadcasted_iota(jnp.int32, (8, LANES), 0)
    for group in range(9):
        for i in range(0, rows, 16):
            top = jnp.where(ahead == i - group, 1.0, 0.0)
            bottom = jnp.where(ahead == i + 8 - group, 1.0, 0.0)
            both = jnp.concatenate([top, bottom], axis=0).astype(BF16)
            out_ref[i : i + 16, group * LANES : (group + 1) * LANES] = both


def stage_kernel(slab, och, *refs):
    video_refs, video_pad, table_ref, sems = refs[1:slab], refs[slab], refs[slab + 1], refs[slab + 2]
    own = lax.axis_index("slab")
    copy = fetch([(refs[0], video_pad.at[own + 1])], sems)[0]
    make_table(och, table_ref)
    zeros = jnp.zeros(video_pad.shape[1:], BF16)
    video_pad[0] = zeros
    video_pad[slab + 1] = zeros
    for i in range(1, slab):
        video_pad[jnp.mod(own - i + slab, slab) + 1] = video_refs[i - 1][...]
    copy.wait()


def forward_kernel(dims, blocks_hbm, gain_ref, bias_ref, *refs):
    devs, slab, clips, held, frames, columns, rows_in, cols, och, per_group = dims
    shard_refs, video_pad, table_ref = refs[:devs], refs[devs], refs[devs + 1]
    weights_ref, video_t_ref, normed_ref, inv_ref, slope_ref, act_ref = refs[devs + 2 : devs + 8]
    shards, blocks_ref, sems = refs[devs + 8 :]
    copy = fetch([(blocks_hbm, blocks_ref)], sems)[0]
    me, own = lax.axis_index("clips"), lax.axis_index("slab")
    places = held * frames * columns
    per_clip = frames * columns
    c_in = video_pad.shape[2]
    many = slab * places
    width = table_ref.shape[0]
    chips = devs // 2
    for t in range(chips):
        for e in range(2):
            source = 2 * ((me // 2) ^ t) + (me % 2 + e) % 2
            shard = shard_refs[t + e * chips][...].astype(F32)
            shard = jnp.concatenate([shard, jnp.zeros((rows_in, width - cols), F32)], axis=1)
            shards[source] = shard.astype(shards.dtype)
    weights = shards[...].reshape(c_in, width).astype(BF16)
    weights = jnp.dot(weights, table_ref[...], preferred_element_type=F32).astype(BF16)

    total = None
    for b in range(3):
        rows = video_pad[b : b + slab].reshape(many, c_in)
        term = jnp.dot(rows, weights[:, 384 * b : 384 * (b + 1)], preferred_element_type=F32)
        total = term if total is None else total + term
    mixed = (
        from_left(total[:, 0:LANES], columns)
        + total[:, LANES : 2 * LANES]
        + from_right(total[:, 2 * LANES :], columns)
    ).reshape(slab, places, LANES)
    frame_shifts = [mixed[:, :, a * och : (a + 1) * och] for a in range(3)]
    frame_of = lax.broadcasted_iota(jnp.int32, (slab, per_clip, och), 1) // columns
    shift = jnp.mod(LANES - own * och, LANES)
    gain = pltpu.roll(jnp.broadcast_to(gain_ref[...], (8, LANES)), shift, 1)[0:1, :och]
    bias = pltpu.roll(jnp.broadcast_to(bias_ref[...], (8, LANES)), shift, 1)[0:1, :och]
    block_rows = FB * columns
    copy.wait()
    for k in range(held):
        blocks = blocks_ref[me * held + k]
        conv = frame_shifts[0][:, k * per_clip : (k + 1) * per_clip]
        for a in (1, 2):
            part = frame_shifts[a][:, k * per_clip : (k + 1) * per_clip - a * columns]
            conv = conv + jnp.concatenate([jnp.zeros((slab, a * columns, och), F32), part], axis=1)
        alive = frame_of < blocks * FB
        count = (blocks * (FB * slab * columns * per_group)).astype(F32)
        kept = jnp.where(alive, conv, 0.0)
        mean = group_mean_of(kept, count, per_group)
        var = group_mean_of(kept * conv, count, per_group) - mean * mean
        inv_std = lax.rsqrt(var + 1e-05)
        normed = (conv - mean) * inv_std
        normed_ref[:, k * per_clip : (k + 1) * per_clip, :] = normed
        inv_ref[k] = jnp.broadcast_to(inv_std[0], (8, och))
        affine = normed * gain[None] + bias[None]
        sigmoid = jax.nn.sigmoid(affine)
        act = affine * sigmoid
        slope = sigmoid * (1.0 + affine * (1.0 - sigmoid))
        slope_ref[:, k * per_clip : (k + 1) * per_clip, :] = slope
        for b in range(BMAX):
            for h in range(slab):
                block = act[h, b * block_rows : (b + 1) * block_rows]
                act_ref[k * BMAX + b, h] = unfolded_to_lanes(block, 8)
    weights_ref[...] = jnp.transpose(weights)
    video_t_ref[...] = jnp.transpose(video_pad[1 : slab + 1].reshape(many, c_in))


def from_left(values, columns):
    column = lax.broadcasted_iota(jnp.int32, values.shape, 0) % columns
    return jnp.where(column > 0, pltpu.roll(values, 1, 0), 0.0)


def from_right(values, columns):
    column = lax.broadcasted_iota(jnp.int32, values.shape, 0) % columns
    return jnp.where(column < columns - 1, pltpu.roll(values, values.shape[0] - 1, 0), 0.0)


def group_mean_of(values, count, per_group):
    och = values.shape[-1]
    same = lax.broadcasted_iota(jnp.int32, (och, och), 0) // per_group
    same = (same == lax.broadcasted_iota(jnp.int32, (och, och), 1) // per_group).astype(F32)
    sums = jnp.sum(jnp.sum(values, axis=0), axis=0, keepdims=True)
    sums = jnp.broadcast_to(sums, (8, och))
    sums = jnp.dot(sums, same, precision=lax.Precision.HIGHEST, preferred_element_type=F32)
    return (sums[0:1] / count)[None]


def backward_kernel(dims, blocks_hbm, order_hbm, gain_ref, weights_ref, *refs):
    devs, slab, clips, held, frames, columns, rows_in, cols, och, per_group = dims
    video_t_ref, normed_ref, inv_ref, slope_ref, act_in, cot_ref = refs[:6]
    act_hbm, keep_ref, send_ref = refs[6:9]
    video_grad_refs = refs[9 : 9 + slab]
    act_ref, grad_ref, rows_ref, blocks_ref, order_ref, sems = refs[9 + slab :]
    copies = fetch([(blocks_hbm, blocks_ref), (order_hbm, order_ref)], sems)
    me, own = lax.axis_index("clips"), lax.axis_index("slab")
    places = held * frames * columns
    per_clip = frames * columns
    block_rows = FB * columns
    c_in = video_t_ref.shape[0]
    groups = LANES // och
    many = slab * places
    shift = jnp.mod(LANES - own * och, LANES)
    gain = pltpu.roll(jnp.broadcast_to(gain_ref[...], (8, LANES)), shift, 1)[0:1, :och]
    frame_of = lax.broadcasted_iota(jnp.int32, (slab, per_clip, och), 1) // columns
    gain_part = jnp.zeros((1, och), F32)
    bias_part = jnp.zeros((1, och), F32)
    for copy in copies:
        copy.wait()
    start = first_block_of(blocks_ref, me * held, clips)
    conv_grads = []
    act_blocks = []
    for k in range(held):
        blocks = blocks_ref[me * held + k]
        cot = []
        for b in range(BMAX):
            device = order_ref[jnp.mod(start + b, devs)]
            rows = []
            for s in range(slab):
                folded = cot_ref[device * slab + s].astype(F32)
                parts = [folded[:, g * och : (g + 1) * och] for g in range(groups)]
                rows.append(jnp.concatenate(parts, axis=0)[:block_rows])
            cot.append(jnp.stack(rows, axis=0))
        cot = jnp.concatenate(cot, axis=1)
        alive = frame_of < blocks * FB
        count = (blocks * (FB * slab * columns * per_group)).astype(F32)
        inv_std = inv_ref[k][None, 0:1]
        normed = normed_ref[:, k * per_clip : (k + 1) * per_clip, :]
        slope = slope_ref[:, k * per_clip : (k + 1) * per_clip, :]
        grad_affine = jnp.where(alive, cot * slope, 0.0)
        gain_part += jnp.sum(jnp.sum(grad_affine * normed, axis=0), axis=0, keepdims=True)
        bias_part += jnp.sum(jnp.sum(grad_affine, axis=0), axis=0, keepdims=True)
        grad_normed = grad_affine * gain[None]
        mean_grad = group_mean_of(grad_normed, count, per_group)
        mean_cross = group_mean_of(grad_normed * normed, count, per_group)
        grad_conv = inv_std * (grad_normed - mean_grad - normed * mean_cross)
        grad_conv = jnp.where(alive, grad_conv, 0.0).astype(BF16).astype(F32)
        lanes = [grad_conv]
        for a in (1, 2):
            zeros = jnp.zeros((slab, a * columns, och), F32)
            lanes.append(jnp.concatenate([grad_conv[:, a * columns :], zeros], axis=1))
        if LANES > 3 * och:
            lanes.append(jnp.zeros((slab, per_clip, LANES - 3 * och), F32))
        conv_grads.append(jnp.concatenate(lanes, axis=2))
        for b in range(BMAX):
            device = order_ref[jnp.mod(start + b, devs)]
            for h in range(slab):
                act_blocks.append((b < blocks, device * slab + h, act_in[k * BMAX + b, h]))
        start = start + blocks

    sums = split3(gain_part) + split3(bias_part) + [jnp.zeros((2, och), F32)]
    sums = jnp.concatenate(sums, axis=0)
    sums = jnp.concatenate([sums, jnp.zeros((8, LANES - och), F32)], axis=1)
    nothing = jnp.concatenate([jnp.zeros_like(act_blocks[0][2]), sums], axis=0).astype(BF16)
    for d in range(devs * slab):
        act_ref[d] = nothing
    for alive, dest, block in act_blocks:

        @pl.when(alive)
        def _(dest=dest, block=block):
            act_ref[dest] = jnp.concatenate([block, sums], axis=0).astype(BF16)

    act_copy = pltpu.make_async_copy(act_ref, act_hbm, sems.at[2])
    act_copy.start()

    grads = jnp.concatenate(conv_grads, axis=1).reshape(many, LANES)
    grad_ref[0] = jnp.zeros((places, 3 * LANES), BF16)
    grad_ref[slab + 1] = jnp.zeros((places, 3 * LANES), BF16)
    for e, shifted in enumerate((from_right(grads, columns), grads, from_left(grads, columns))):
        shifted = shifted.astype(BF16).reshape(slab, places, LANES)
        grad_ref[1 : slab + 1, :, e * LANES : (e + 1) * LANES] = shifted

    total = None
    for b in range(3):
        term = jnp.dot(
            grad_ref[2 - b : 2 - b + slab].reshape(many, 3 * LANES),
            weights_ref[384 * b : 384 * (b + 1)],
            preferred_element_type=F32,
        )
        total = term if total is None else total + term
    rows_ref[...] = total.reshape(slab, places, c_in)
    for i, ref in enumerate(video_grad_refs):
        ref[...] = rows_ref[jnp.mod(own + i, slab)].astype(ref.dtype)

    parts = []
    for b in range(3):
        moved = grad_ref[2 - b : 2 - b + slab].reshape(many, 3 * LANES)
        parts.append(jnp.dot(video_t_ref[...], moved, preferred_element_type=F32))
    terms = jnp.concatenate(parts, axis=1).reshape(devs // 2, 2 * rows_in, 9 * LANES)
    low, high = terms[:, :rows_in], terms[:, rows_in:]
    odd = me % 2 == 1
    keep_ref[...] = jnp.where(odd, high, low)
    send_ref[...] = jnp.where(odd, low, high).astype(BF16)
    act_copy.wait()


def unfolded_to_lanes(values, unit):
    groups = LANES // values.shape[1]
    rows = round_up(-(-values.shape[0] // groups), unit)
    short = rows * groups - values.shape[0]
    if short:
        values = jnp.concatenate([values, jnp.zeros((short, values.shape[1]), F32)], axis=0)
    return jnp.concatenate([values[g * rows : (g + 1) * rows] for g in range(groups)], axis=1)


def pair_kernel(chips, keep_ref, other_ref, *outs):
    me = lax.axis_index("clips") // 2
    for t, ref in enumerate(outs):
        chip = partner(me, t, chips)
        ref[...] = (keep_ref[chip] + other_ref[chip].astype(F32)).astype(ref.dtype)


def sum_kernel(*refs):
    total = refs[0][...]
    for ref in refs[1:-1]:
        total = total + ref[...].astype(F32)
    refs[-1][...] = total.astype(refs[-1].dtype)


def table_kernel(och, after_ref, table_ref):
    rows, cols = table_ref.shape
    lane = lax.broadcasted_iota(jnp.int32, (LANES, LANES), 0)
    source = jnp.where(lane < 3 * och, 27 * (lane % och) + 9 * (2 - lane // och), -cols)
    ahead = source - lax.broadcasted_iota(jnp.int32, (LANES, LANES), 1)
    for group in range(rows // LANES):
        for j in range(0, cols, LANES):
            hit = jnp.where(ahead == j - group, 1.0, 0.0).astype(BF16)
            table_ref[group * LANES : (group + 1) * LANES, j : j + LANES] = hit


def weights_kernel(*refs):
    kernel_refs, table_ref, kernel_grad_ref = refs[:-2], refs[-2], refs[-1]
    total = kernel_refs[0][...]
    for ref in kernel_refs[1:]:
        total = total + ref[...].astype(F32)
    rows, cols = kernel_grad_ref.shape
    native = jnp.dot(
        jnp.concatenate(split3(total), axis=0).astype(BF16),
        table_ref[...],
        preferred_element_type=F32,
    )
    native = native[:rows] + (native[rows : 2 * rows] + native[2 * rows :])
    kernel_grad_ref[...] = native[:, :cols]


def finish_kernel(dims, holds_ref, act_in, after_ref, *refs):
    devs, slab, slots, och = dims
    hbm_refs, (act_ref, gain_ref, bias_ref), sems = refs[:3], refs[3:6], refs[6]
    groups = LANES // och
    rows = act_in.shape[1] - 8
    sums = []
    blocks = [[jnp.zeros((rows, LANES), F32)] * slab for _ in range(slots)]
    for s in range(slab):
        part = jnp.zeros((8, LANES), F32)
        for d in range(devs):
            both = act_in[d * slab + s].astype(F32)
            part = part + both[rows:]
            for q in range(slots):
                blocks[q][s] = blocks[q][s] + both[:rows] * holds_ref[q * devs + d]
        sums.append(part[:, :och])
    sums = jnp.concatenate(sums, axis=1)
    gain_ref[...] = sums[0:1] + (sums[1:2] + sums[2:3])
    bias_ref[...] = sums[3:4] + (sums[4:5] + sums[5:6])
    copies = [pltpu.make_async_copy(a, b, sems.at[i]) for i, (a, b) in enumerate(zip(refs[3:6], hbm_refs))]
    copies[1].start()
    copies[2].start()
    for q in range(slots):
        block = []
        for g in range(groups):
            parts = [p[:, g * och : (g + 1) * och] for p in blocks[q]]
            block.append(jnp.concatenate(parts, axis=1))
        act_ref[q] = jnp.concatenate(block, axis=0)[: act_ref.shape[1]].astype(BF16)
    copies[0].start()
    for copy in copies:
        copy.wait()


def call(kernel, outs, specs, scratch=(), limit=None, out_specs=None, cost=None):
    limit = limit or lax.axis_size("slab") * MIB
    return pl.pallas_call(
        kernel,
        out_shape=outs,
        in_specs=specs,
        out_specs=out_specs or [VMEM] * len(outs),
        cost_estimate=cost,
        scratch_shapes=list(scratch),
        compiler_params=pltpu.CompilerParams(vmem_limit_bytes=limit),
    )


def partner(index, step, size):
    return index ^ step if size & (size - 1) == 0 else (index + step) % size


def shifts(arrays, axis):
    size = lax.axis_size(axis)
    moved = [arrays[0]]
    for i in range(1, size):
        moved.append(lax.ppermute(arrays[i], axis, [(j, (j + i) % size) for j in range(size)]))
    return moved


def chip_swaps(arrays, axis):
    size = lax.axis_size(axis)
    moved = [arrays[0]]
    for t in range(1, size // 2):
        pairs = [(j, 2 * partner(j // 2, t, size // 2) + j % 2) for j in range(size)]
        moved.append(lax.ppermute(arrays[t], axis, pairs))
    return moved


def core_swap(array, axis):
    return lax.ppermute(array, axis, [(j, j ^ 1) for j in range(lax.axis_size(axis))])


def body(video, clip_blocks, deal_order, kernel, gain, bias, cotangent):
    devs, slab = lax.axis_size("clips"), lax.axis_size("slab")
    held, frames, _, columns, c_in = video.shape
    slots, clips = cotangent.shape[0], clip_blocks.shape[0]
    c_out = gain.shape[0]
    rows_in, cols = kernel.shape
    och = c_out // slab
    per_group = c_out // GROUPS
    width = round_up(cols, LANES)
    places = held * frames * columns
    block_rows = FB * columns
    fold_rows = round_up(-(-block_rows // (LANES // och)), 8)
    chips = devs // 2
    everyone = ("clips", "slab")
    shape = jax.ShapeDtypeStruct
    smem = [pltpu.SMEM((clips,), jnp.int32), pltpu.SMEM((devs,), jnp.int32)]
    large = (6 + 3 * slab) * MIB
    gain, bias = gain.reshape(1, c_out), bias.reshape(1, c_out)
    clip_blocks = pltpu.with_memory_space_constraint(clip_blocks, pltpu.HBM)
    deal_order = pltpu.with_memory_space_constraint(deal_order, pltpu.HBM)
    cotangent_blocks = pltpu.with_memory_space_constraint(
        cotangent.reshape(slots, block_rows, c_out), pltpu.HBM
    )

    videos = shifts([video.reshape(places, c_in)] * slab, "slab")
    cots, holds = call(
        functools.partial(send_kernel, (devs, slab, slots, clips, held, och)),
        [shape((devs * slab, fold_rows, LANES), BF16), shape((slots * devs, 1, LANES), F32)],
        [HBM, HBM, HBM],
        smem + [pltpu.VMEM((slots, block_rows, c_out), BF16), pltpu.SemaphoreType.DMA((3,))],
        cost=pl.CostEstimate(flops=FIRST, bytes_accessed=0, transcendentals=0),
    )(clip_blocks, deal_order, cotangent_blocks)
    cots = lax.all_to_all(cots, everyone, split_axis=0, concat_axis=0, tiled=True)
    shards = [kernel]
    while len(shards) < chips:
        pairs = [(j, j ^ (2 * len(shards))) for j in range(devs)]
        shards = shards + [lax.ppermute(shard, "clips", pairs) for shard in shards]
    shards = shards + [core_swap(shard, "clips") for shard in shards]

    dims = (devs, slab, clips, held, frames, columns, rows_in, cols, och, per_group)
    video_pad, table = call(
        functools.partial(stage_kernel, slab, och),
        [shape((slab + 2, places, c_in), BF16), shape((width, 9 * LANES), BF16)],
        [HBM] + [VMEM] * (slab - 1),
        [pltpu.SemaphoreType.DMA((1,))],
        cost=pl.CostEstimate(flops=STAGE, bytes_accessed=0, transcendentals=0),
    )(pltpu.with_memory_space_constraint(videos[0], pltpu.HBM), *videos[1:])
    weights, video_t, normed, inv_std, slope, act = call(
        functools.partial(forward_kernel, dims),
        [
            shape((9 * LANES, c_in), BF16),
            shape((c_in, slab * places), BF16),
            shape((slab, places, och), F32),
            shape((held, 8, och), F32),
            shape((slab, places, och), F32),
            shape((held * BMAX, slab, fold_rows, LANES), F32),
        ],
        [HBM] + [VMEM] * (devs + 4),
        [
            pltpu.VMEM((devs, rows_in, width), F32 if rows_in % 16 else BF16),
            smem[0],
            pltpu.SemaphoreType.DMA((1,)),
        ],
        large,
    )(clip_blocks, gain, bias, *shards, video_pad, table)
    acts, keep, send, *video_grads = call(
        functools.partial(backward_kernel, dims),
        [
            pltpu.HBM((devs * slab, fold_rows + 8, LANES), BF16),
            shape((chips, rows_in, 9 * LANES), F32),
            shape((chips, rows_in, 9 * LANES), BF16),
        ]
        + [shape((places, c_in), F32 if i == 0 else BF16) for i in range(slab)],
        [HBM, HBM] + [VMEM] * 8,
        [
            pltpu.VMEM((devs * slab, fold_rows + 8, LANES), BF16),
            pltpu.VMEM((slab + 2, places, 3 * LANES), BF16),
            pltpu.VMEM((slab, places, c_in), F32),
        ]
        + smem
        + [pltpu.SemaphoreType.DMA((3,))],
        large,
        [HBM] + [VMEM] * (2 + slab),
    )(clip_blocks, deal_order, gain, weights, video_t, normed, inv_std, slope, act, cots)
    video_grads = shifts(video_grads, "slab")
    send = core_swap(send, "clips")
    acts = lax.all_to_all(acts, everyone, split_axis=0, concat_axis=0, tiled=True)
    kernel_grads = call(
        functools.partial(pair_kernel, chips),
        [shape((rows_in, 9 * LANES), F32 if t == 0 else BF16) for t in range(chips)],
        [VMEM, VMEM],
    )(keep, send)
    table = call(
        functools.partial(table_kernel, och), [shape((9 * LANES, width), BF16)], [ANY]
    )(kernel_grads[1])[0]
    kernel_grads = chip_swaps(kernel_grads, "clips")

    video_grad = call(
        sum_kernel,
        [shape((places, c_in), BF16)],
        [VMEM] * slab,
        cost=pl.CostEstimate(flops=STAGE, bytes_accessed=0, transcendentals=0),
    )(*video_grads)[0]
    kernel_grad = call(
        weights_kernel,
        [shape((rows_in, cols), F32)],
        [VMEM] * (chips + 1),
        limit=2 * slab * MIB,
        cost=pl.CostEstimate(flops=STAGE, bytes_accessed=0, transcendentals=0),
    )(*kernel_grads, table)[0]
    act, gain_grad, bias_grad = call(
        functools.partial(finish_kernel, (devs, slab, slots, och)),
        [
            pltpu.HBM((slots, block_rows, c_out), BF16),
            pltpu.HBM((1, c_out), F32),
            pltpu.HBM((1, c_out), F32),
        ],
        [VMEM, VMEM, HBM],
        [
            pltpu.VMEM((slots, block_rows, c_out), BF16),
            pltpu.VMEM((1, c_out), F32),
            pltpu.VMEM((1, c_out), F32),
            pltpu.SemaphoreType.DMA((3,)),
        ],
        out_specs=[HBM] * 3,
    )(holds, acts, pltpu.with_memory_space_constraint(kernel_grad, pltpu.HBM))
    return (
        act.reshape(cotangent.shape),
        video_grad.reshape(video.shape),
        kernel_grad,
        gain_grad.reshape(c_out),
        bias_grad.reshape(c_out),
    )


def solution(mesh):
    return jax.shard_map(
        body,
        mesh=mesh,
        in_specs=(
            P("clips", None, "slab", None, None),
            P(),
            P(),
            P("clips", "slab"),
            P(),
            P(),
            P("clips", None, "slab", None, None),
        ),
        out_specs=(
            P("clips", None, "slab", None, None),
            P("clips", None, "slab", None, None),
            P("clips", "slab"),
            P(),
            P(),
        ),
        check_vma=False,
    )
```

```python
import functools

import jax
import jax.numpy as jnp
from jax import lax
from jax.experimental import pallas as pl
from jax.experimental.pallas import tpu as pltpu
from jax.sharding import PartitionSpec as P

GROUPS = 16
TAPS = 27
FB = 2
BMAX = 3
LANES = 128
F32 = jnp.float32
BF16 = jnp.bfloat16
HBM = pl.BlockSpec(memory_space=pltpu.HBM)
ANY = pl.BlockSpec(memory_space=pl.ANY)
VMEM = pl.BlockSpec(memory_space=pltpu.VMEM)
MIB = 1024 * 1024
FIRST = 10**6
STAGE = 10**10


def round_up(value, unit):
    return -(-value // unit) * unit


def fold(values, slice_index, och, unit):
    groups = LANES // och
    rows = round_up(-(-values.shape[0] // groups), unit)
    short = rows * groups - values.shape[0]
    if short:
        values = jnp.concatenate([values, jnp.zeros((short, LANES), values.dtype)], axis=0)
    lane_group = lax.broadcasted_iota(jnp.int32, (rows, LANES), 1) // och
    total = jnp.zeros((rows, LANES), F32)
    for g in range(groups):
        shift = (g - slice_index) * och % LANES
        moved = pltpu.roll(values[g * rows : (g + 1) * rows], shift, 1) if shift else values[g * rows : (g + 1) * rows]
        total = total + jnp.where(lane_group == g, moved, 0.0)
    return total


def first_block_of(blocks_ref, first_clip, clips):
    start = jnp.int32(0)
    for k in range(clips):
        start = start + jnp.where(k < first_clip, blocks_ref[k], 0)
    return start


def slot_holders(blocks_ref, order_ref, me, slots, clips, held, devs):
    residue = jnp.int32(0)
    for r in range(devs):
        residue = jnp.where(order_ref[r] == me, r, residue)
    clip_of = [jnp.int32(0)] * slots
    end = jnp.int32(0)
    for k in range(clips):
        end = end + blocks_ref[k]
        for q in range(slots):
            clip_of[q] = clip_of[q] + jnp.where(end <= q * devs + residue, 1, 0)
    return [jnp.minimum(c, clips - 1) // held for c in clip_of]


def split3(values):
    high = values.astype(BF16).astype(F32)
    rest = values - high
    middle = rest.astype(BF16).astype(F32)
    return [high, middle, rest - middle]


def fetch(pairs, sems):
    copies = [pltpu.make_async_copy(a, b, sems.at[i]) for i, (a, b) in enumerate(pairs)]
    for copy in copies:
        copy.start()
    return copies


def send_kernel(
    dims,
    blocks_hbm,
    order_hbm,
    cot_hbm,
    out_ref,
    holds_ref,
    slots_ref,
    blocks_ref,
    order_ref,
    cot_ref,
    sems,
):
    devs, slab, slots, clips, held, och = dims
    pairs = [(blocks_hbm, blocks_ref), (order_hbm, order_ref), (cot_hbm, cot_ref)]
    copies = fetch(pairs, sems)
    out_ref[...] = jnp.zeros_like(out_ref)
    for copy in copies:
        copy.wait()
    me = lax.axis_index("clips")
    start = first_block_of(blocks_ref, me * held, clips)
    for k in range(held):
        count = blocks_ref[me * held + k]
        for b in range(BMAX):
            device = jnp.where(b < count, order_ref[jnp.mod(start + b, devs)], devs)
            for d in range(devs):
                hit = jnp.where(device == d, 1.0, 0.0)
                slots_ref[(k * BMAX + b) * devs + d] = jnp.full((1, LANES), hit, F32)
        start = start + count
    holders = slot_holders(blocks_ref, order_ref, me, slots, clips, held, devs)
    for q in range(slots):
        block = cot_ref[q].astype(F32)
        for s in range(slab):
            out_ref[holders[q] * slab + s] = fold(block, s, och, 8).astype(BF16)
        for d in range(devs):
            holds_ref[q * devs + d] = jnp.full((1, LANES), jnp.where(holders[q] == d, 1.0, 0.0), F32)


def make_table(och, out_ref):
    rows = out_ref.shape[0]
    lane = lax.broadcasted_iota(jnp.int32, (8, LANES), 1)
    source = jnp.where(lane < 3 * och, 27 * (lane % och) + 9 * (2 - lane // och), -rows)
    ahead = source - lax.broadcasted_iota(jnp.int32, (8, LANES), 0)
    for group in range(9):
        for i in range(0, rows, 16):
            top = jnp.where(ahead == i - group, 1.0, 0.0)
            bottom = jnp.where(ahead == i + 8 - group, 1.0, 0.0)
            both = jnp.concatenate([top, bottom], axis=0).astype(BF16)
            out_ref[i : i + 16, group * LANES : (group + 1) * LANES] = both


def stage_kernel(slab, och, *refs):
    video_refs, video_pad, table_ref, sems = refs[1:slab], refs[slab], refs[slab + 1], refs[slab + 2]
    own = lax.axis_index("slab")
    copy = fetch([(refs[0], video_pad.at[own + 1])], sems)[0]
    make_table(och, table_ref)
    zeros = jnp.zeros(video_pad.shape[1:], BF16)
    video_pad[0] = zeros
    video_pad[slab + 1] = zeros
    for i in range(1, slab):
        video_pad[jnp.mod(own - i + slab, slab) + 1] = video_refs[i - 1][...]
    copy.wait()


def forward_kernel(dims, blocks_hbm, gain_ref, bias_ref, *refs):
    devs, slab, clips, held, frames, columns, rows_in, cols, och, per_group = dims
    shard_refs, video_pad, table_ref = refs[:devs], refs[devs], refs[devs + 1]
    weights_ref, video_t_ref, normed_ref, inv_ref, slope_ref, act_ref = refs[devs + 2 : devs + 8]
    shards, blocks_ref, sems = refs[devs + 8 :]
    copy = fetch([(blocks_hbm, blocks_ref)], sems)[0]
    me, own = lax.axis_index("clips"), lax.axis_index("slab")
    places = held * frames * columns
    per_clip = frames * columns
    c_in = video_pad.shape[2]
    many = slab * places
    width = table_ref.shape[0]
    chips = devs // 2
    for t in range(chips):
        for e in range(2):
            source = 2 * ((me // 2) ^ t) + (me % 2 + e) % 2
            shard = shard_refs[t + e * chips][...].astype(F32)
            shard = jnp.concatenate([shard, jnp.zeros((rows_in, width - cols), F32)], axis=1)
            shards[source] = shard.astype(shards.dtype)
    weights = shards[...].reshape(c_in, width).astype(BF16)
    weights = jnp.dot(weights, table_ref[...], preferred_element_type=F32).astype(BF16)

    total = jnp.dot(
        jnp.concatenate([video_pad[b : b + slab].reshape(many, c_in) for b in range(3)], axis=1),
        jnp.concatenate([weights[:, 384 * b : 384 * (b + 1)] for b in range(3)], axis=0),
        preferred_element_type=F32,
    )
    mixed = (
        from_left(total[:, 0:LANES], columns)
        + total[:, LANES : 2 * LANES]
        + from_right(total[:, 2 * LANES :], columns)
    ).reshape(slab, places, LANES)
    frame_shifts = [mixed[:, :, a * och : (a + 1) * och] for a in range(3)]
    frame_of = lax.broadcasted_iota(jnp.int32, (slab, per_clip, och), 1) // columns
    shift = jnp.mod(LANES - own * och, LANES)
    gain = pltpu.roll(jnp.broadcast_to(gain_ref[...], (8, LANES)), shift, 1)[0:1, :och]
    bias = pltpu.roll(jnp.broadcast_to(bias_ref[...], (8, LANES)), shift, 1)[0:1, :och]
    block_rows = FB * columns
    copy.wait()
    convs, kept, counts, limits = [], [], [], []
    for k in range(held):
        blocks = blocks_ref[me * held + k]
        conv = frame_shifts[0][:, k * per_clip : (k + 1) * per_clip]
        for a in (1, 2):
            part = frame_shifts[a][:, k * per_clip : (k + 1) * per_clip - a * columns]
            conv = conv + jnp.concatenate([jnp.zeros((slab, a * columns, och), F32), part], axis=1)
        convs.append(conv)
        kept.append(jnp.where(frame_of < blocks * FB, conv, 0.0))
        count = (blocks * (FB * slab * columns * per_group)).astype(F32)
        counts.append(jnp.full((1, och), count, F32))
        limits.append(jnp.full((1, och), (blocks * FB).astype(F32), F32))
    sums = group_sums(kept + [a * b for a, b in zip(kept, convs)], per_group)
    for k in range(held):
        conv = convs[k]
        mean = sums[k] / counts[k]
        inv_std = lax.rsqrt(sums[held + k] / counts[k] - mean * mean + 1e-05)
        inv_ref[k] = jnp.concatenate([inv_std, counts[k], limits[k], jnp.zeros((5, och), F32)], axis=0)
        mean, inv_std = mean[None], inv_std[None]
        normed = (conv - mean) * inv_std
        normed_ref[:, k * per_clip : (k + 1) * per_clip, :] = normed
        affine = normed * gain[None] + bias[None]
        sigmoid = jax.nn.sigmoid(affine)
        act = affine * sigmoid
        slope = sigmoid * (1.0 + affine * (1.0 - sigmoid))
        slope_ref[:, k * per_clip : (k + 1) * per_clip, :] = slope
        for b in range(BMAX):
            for h in range(slab):
                block = act[h, b * block_rows : (b + 1) * block_rows]
                act_ref[k * BMAX + b, h] = unfolded_to_lanes(block, 8)
    weights_ref[...] = jnp.transpose(weights)
    video_t_ref[...] = jnp.transpose(video_pad[1 : slab + 1].reshape(many, c_in))


def from_left(values, columns):
    column = lax.broadcasted_iota(jnp.int32, values.shape, 0) % columns
    return jnp.where(column > 0, pltpu.roll(values, 1, 0), 0.0)


def from_right(values, columns):
    column = lax.broadcasted_iota(jnp.int32, values.shape, 0) % columns
    return jnp.where(column < columns - 1, pltpu.roll(values, values.shape[0] - 1, 0), 0.0)


def group_sums(arrays, per_group):
    och = arrays[0].shape[-1]
    rows = [jnp.sum(jnp.sum(a, axis=0), axis=0, keepdims=True) for a in arrays]
    rows.append(jnp.zeros((-len(rows) % 8, och), F32))
    total = jnp.concatenate([r for r in rows if r.shape[0]], axis=0)
    if och < LANES:
        total = jnp.concatenate([total, jnp.zeros((total.shape[0], LANES - och), F32)], axis=1)
    lane = lax.broadcasted_iota(jnp.int32, total.shape, 1)
    step = 1
    while step < per_group:
        down, up = pltpu.roll(total, LANES - step, 1), pltpu.roll(total, step, 1)
        total = total + jnp.where((lane // step) % 2 == 0, down, up)
        step *= 2
    return [total[i : i + 1, :och] for i in range(len(arrays))]


def backward_kernel(dims, slots_ref, gain_ref, weights_ref, *refs):
    devs, slab, clips, held, frames, columns, rows_in, cols, och, per_group = dims
    video_t_ref, normed_ref, inv_ref, slope_ref, act_in, cot_ref = refs[:6]
    act_hbm, keep_ref, send_ref = refs[6:9]
    video_grad_refs = refs[9 : 9 + slab]
    act_ref, grad_ref, rows_ref, sems = refs[9 + slab :]
    me, own = lax.axis_index("clips"), lax.axis_index("slab")
    places = held * frames * columns
    per_clip = frames * columns
    block_rows = FB * columns
    c_in = video_t_ref.shape[0]
    groups = LANES // och
    many = slab * places
    shift = jnp.mod(LANES - own * och, LANES)
    gain = pltpu.roll(jnp.broadcast_to(gain_ref[...], (8, LANES)), shift, 1)[0:1, :och]
    frame_of = lax.broadcasted_iota(jnp.int32, (slab, per_clip, och), 1) // columns
    frame_of = frame_of.astype(F32)
    gain_part = jnp.zeros((1, och), F32)
    bias_part = jnp.zeros((1, och), F32)
    blocks = [[None] * slab for _ in range(held * BMAX)]
    for d in range(devs):
        for s in range(slab):
            folded = cot_ref[d * slab + s].astype(F32)
            for j in range(held * BMAX):
                term = folded * slots_ref[j * devs + d]
                blocks[j][s] = term if d == 0 else blocks[j][s] + term
    normeds, grads, alives = [], [], []
    for k in range(held):
        cot = []
        for b in range(BMAX):
            rows = []
            for folded in blocks[k * BMAX + b]:
                parts = [folded[:, g * och : (g + 1) * och] for g in range(groups)]
                rows.append(jnp.concatenate(parts, axis=0)[:block_rows])
            cot.append(jnp.stack(rows, axis=0))
        cot = jnp.concatenate(cot, axis=1)
        alive = frame_of < inv_ref[k][None, 2:3]
        normed = normed_ref[:, k * per_clip : (k + 1) * per_clip, :]
        slope = slope_ref[:, k * per_clip : (k + 1) * per_clip, :]
        grad_affine = jnp.where(alive, cot * slope, 0.0)
        gain_part += jnp.sum(jnp.sum(grad_affine * normed, axis=0), axis=0, keepdims=True)
        bias_part += jnp.sum(jnp.sum(grad_affine, axis=0), axis=0, keepdims=True)
        normeds.append(normed)
        grads.append(grad_affine * gain[None])
        alives.append(alive)
    sums = group_sums(grads + [a * b for a, b in zip(grads, normeds)], per_group)
    conv_grads = []
    for k in range(held):
        inv_std, count = inv_ref[k][None, 0:1], inv_ref[k][1:2]
        mean_grad, mean_cross = (sums[k] / count)[None], (sums[held + k] / count)[None]
        grad_conv = inv_std * (grads[k] - mean_grad - normeds[k] * mean_cross)
        grad_conv = jnp.where(alives[k], grad_conv, 0.0).astype(BF16).astype(F32)
        lanes = [grad_conv]
        for a in (1, 2):
            zeros = jnp.zeros((slab, a * columns, och), F32)
            lanes.append(jnp.concatenate([grad_conv[:, a * columns :], zeros], axis=1))
        if LANES > 3 * och:
            lanes.append(jnp.zeros((slab, per_clip, LANES - 3 * och), F32))
        conv_grads.append(jnp.concatenate(lanes, axis=2))

    sums = split3(gain_part) + split3(bias_part) + [jnp.zeros((2, och), F32)]
    sums = jnp.concatenate(sums, axis=0)
    sums = jnp.concatenate([sums, jnp.zeros((8, LANES - och), F32)], axis=1)
    for d in range(devs):
        for h in range(slab):
            total = None
            for j in range(held * BMAX):
                term = act_in[j, h] * slots_ref[j * devs + d]
                total = term if total is None else total + term
            act_ref[d * slab + h] = jnp.concatenate([total, sums], axis=0).astype(BF16)

    act_copy = pltpu.make_async_copy(act_ref, act_hbm, sems.at[0])
    act_copy.start()

    grads = jnp.concatenate(conv_grads, axis=1).reshape(many, LANES)
    grad_ref[0] = jnp.zeros((places, 3 * LANES), BF16)
    grad_ref[slab + 1] = jnp.zeros((places, 3 * LANES), BF16)
    for e, shifted in enumerate((from_right(grads, columns), grads, from_left(grads, columns))):
        shifted = shifted.astype(BF16).reshape(slab, places, LANES)
        grad_ref[1 : slab + 1, :, e * LANES : (e + 1) * LANES] = shifted

    moved = [grad_ref[2 - b : 2 - b + slab].reshape(many, 3 * LANES) for b in range(3)]
    moved = jnp.concatenate(moved, axis=1)
    total = jnp.dot(moved, weights_ref[...], preferred_element_type=F32)
    rows_ref[...] = total.reshape(slab, places, c_in)
    for i, ref in enumerate(video_grad_refs):
        ref[...] = rows_ref[jnp.mod(own + i, slab)].astype(ref.dtype)

    terms = jnp.dot(video_t_ref[...], moved, preferred_element_type=F32)
    terms = terms.reshape(devs // 2, 2 * rows_in, 9 * LANES)
    low, high = terms[:, :rows_in], terms[:, rows_in:]
    odd = me % 2 == 1
    keep_ref[...] = jnp.where(odd, high, low)
    send_ref[...] = jnp.where(odd, low, high).astype(BF16)
    act_copy.wait()


def unfolded_to_lanes(values, unit):
    groups = LANES // values.shape[1]
    rows = round_up(-(-values.shape[0] // groups), unit)
    short = rows * groups - values.shape[0]
    if short:
        values = jnp.concatenate([values, jnp.zeros((short, values.shape[1]), F32)], axis=0)
    return jnp.concatenate([values[g * rows : (g + 1) * rows] for g in range(groups)], axis=1)


def pair_kernel(chips, keep_ref, other_ref, *outs):
    me = lax.axis_index("clips") // 2
    cols = outs[0].shape[1]
    used = cols // 9
    for t, ref in enumerate(outs):
        chip = partner(me, t, chips)
        total = keep_ref[chip] + other_ref[chip].astype(F32)
        parts = [total[:, g * LANES : g * LANES + used] for g in range(9)]
        ref[...] = jnp.concatenate(parts, axis=1).astype(ref.dtype)


def sum_kernel(*refs):
    total = refs[0][...]
    for ref in refs[1:-1]:
        total = total + ref[...].astype(F32)
    refs[-1][...] = total.astype(refs[-1].dtype)


def table_kernel(och, after_ref, table_ref):
    rows, cols = table_ref.shape
    place = lax.broadcasted_iota(jnp.int32, (LANES, LANES), 0)
    column = lax.broadcasted_iota(jnp.int32, (LANES, LANES), 1)
    for i in range(0, rows, LANES):
        inner = (place + i) % (3 * och)
        source = 27 * (inner % och) + 9 * (2 - inner // och) + (place + i) // (3 * och)
        ahead = jnp.where(place + i < 27 * och, source, -cols) - column
        for j in range(0, cols, LANES):
            table_ref[i : i + LANES, j : j + LANES] = jnp.where(ahead == j, 1.0, 0.0).astype(BF16)


def finish_kernel(dims, holds_ref, act_in, table_ref, *refs):
    devs, slab, slots, och = dims
    chips = devs // 2
    kernel_refs, hbm_refs = refs[:chips], refs[chips : chips + 4]
    out_refs, sems = refs[chips + 4 : chips + 8], refs[chips + 8]
    kernel_grad_ref, act_ref, gain_ref, bias_ref = out_refs
    copies = [pltpu.make_async_copy(a, b, sems.at[i]) for i, (a, b) in enumerate(zip(out_refs, hbm_refs))]

    total = kernel_refs[0][...]
    for ref in kernel_refs[1:]:
        total = total + ref[...].astype(F32)
    rows, cols = total.shape
    width = table_ref.shape[0]
    if width > cols:
        total = jnp.concatenate([total, jnp.zeros((rows, width - cols), F32)], axis=1)
    native = jnp.dot(
        jnp.concatenate(split3(total), axis=0).astype(BF16),
        table_ref[...],
        preferred_element_type=F32,
    )
    native = native[:rows] + (native[rows : 2 * rows] + native[2 * rows :])
    kernel_grad_ref[...] = native[:, :cols]
    copies[0].start()

    groups = LANES // och
    rows = act_in.shape[1] - 8
    sums = []
    blocks = [[jnp.zeros((rows, LANES), F32)] * slab for _ in range(slots)]
    for s in range(slab):
        part = jnp.zeros((8, LANES), F32)
        for d in range(devs):
            both = act_in[d * slab + s].astype(F32)
            part = part + both[rows:]
            for q in range(slots):
                blocks[q][s] = blocks[q][s] + both[:rows] * holds_ref[q * devs + d]
        sums.append(part[:, :och])
    for q in range(slots):
        block = []
        for g in range(groups):
            parts = [p[:, g * och : (g + 1) * och] for p in blocks[q]]
            block.append(jnp.concatenate(parts, axis=1))
        act_ref[q] = jnp.concatenate(block, axis=0)[: act_ref.shape[1]].astype(BF16)
    copies[1].start()
    sums = jnp.concatenate(sums, axis=1)
    gain_ref[...] = sums[0:1] + (sums[1:2] + sums[2:3])
    bias_ref[...] = sums[3:4] + (sums[4:5] + sums[5:6])
    copies[2].start()
    copies[3].start()
    for copy in copies:
        copy.wait()


def call(kernel, outs, specs, scratch=(), limit=None, out_specs=None, cost=None):
    limit = limit or lax.axis_size("slab") * MIB
    return pl.pallas_call(
        kernel,
        out_shape=outs,
        in_specs=specs,
        out_specs=out_specs or [VMEM] * len(outs),
        cost_estimate=cost,
        scratch_shapes=list(scratch),
        compiler_params=pltpu.CompilerParams(vmem_limit_bytes=limit),
    )


def partner(index, step, size):
    return index ^ step if size & (size - 1) == 0 else (index + step) % size


def shifts(arrays, axis):
    size = lax.axis_size(axis)
    moved = [arrays[0]]
    for i in range(1, size):
        moved.append(lax.ppermute(arrays[i], axis, [(j, (j + i) % size) for j in range(size)]))
    return moved


def chip_swaps(arrays, axis):
    size = lax.axis_size(axis)
    moved = [arrays[0]]
    for t in range(1, size // 2):
        pairs = [(j, 2 * partner(j // 2, t, size // 2) + j % 2) for j in range(size)]
        moved.append(lax.ppermute(arrays[t], axis, pairs))
    return moved


def core_swap(array, axis):
    return lax.ppermute(array, axis, [(j, j ^ 1) for j in range(lax.axis_size(axis))])


def body(video, clip_blocks, deal_order, kernel, gain, bias, cotangent):
    devs, slab = lax.axis_size("clips"), lax.axis_size("slab")
    held, frames, _, columns, c_in = video.shape
    slots, clips = cotangent.shape[0], clip_blocks.shape[0]
    c_out = gain.shape[0]
    rows_in, cols = kernel.shape
    och = c_out // slab
    per_group = c_out // GROUPS
    width = round_up(cols, LANES)
    places = held * frames * columns
    block_rows = FB * columns
    fold_rows = round_up(-(-block_rows // (LANES // och)), 8)
    chips = devs // 2
    everyone = ("clips", "slab")
    shape = jax.ShapeDtypeStruct
    smem = [pltpu.SMEM((clips,), jnp.int32), pltpu.SMEM((devs,), jnp.int32)]
    large = (6 + 3 * slab) * MIB
    gain, bias = gain.reshape(1, c_out), bias.reshape(1, c_out)
    clip_blocks = pltpu.with_memory_space_constraint(clip_blocks, pltpu.HBM)
    deal_order = pltpu.with_memory_space_constraint(deal_order, pltpu.HBM)
    cotangent_blocks = pltpu.with_memory_space_constraint(
        cotangent.reshape(slots, block_rows, c_out), pltpu.HBM
    )

    videos = shifts([video.reshape(places, c_in)] * slab, "slab")
    cots, holds, slot_of = call(
        functools.partial(send_kernel, (devs, slab, slots, clips, held, och)),
        [shape((devs * slab, fold_rows, LANES), BF16), shape((slots * devs, 1, LANES), F32)]
        + [shape((held * BMAX * devs, 1, LANES), F32)],
        [HBM, HBM, HBM],
        smem + [pltpu.VMEM((slots, block_rows, c_out), BF16), pltpu.SemaphoreType.DMA((3,))],
        cost=pl.CostEstimate(flops=FIRST, bytes_accessed=0, transcendentals=0),
    )(clip_blocks, deal_order, cotangent_blocks)
    cots = lax.all_to_all(cots, everyone, split_axis=0, concat_axis=0, tiled=True)
    shards = [kernel]
    while len(shards) < chips:
        pairs = [(j, j ^ (2 * len(shards))) for j in range(devs)]
        shards = shards + [lax.ppermute(shard, "clips", pairs) for shard in shards]
    shards = shards + [core_swap(shard, "clips") for shard in shards]

    dims = (devs, slab, clips, held, frames, columns, rows_in, cols, och, per_group)
    video_pad, table = call(
        functools.partial(stage_kernel, slab, och),
        [shape((slab + 2, places, c_in), BF16), shape((width, 9 * LANES), BF16)],
        [HBM] + [VMEM] * (slab - 1),
        [pltpu.SemaphoreType.DMA((1,))],
        cost=pl.CostEstimate(flops=STAGE, bytes_accessed=0, transcendentals=0),
    )(pltpu.with_memory_space_constraint(videos[0], pltpu.HBM), *videos[1:])
    weights, video_t, normed, inv_std, slope, act = call(
        functools.partial(forward_kernel, dims),
        [
            shape((9 * LANES, c_in), BF16),
            shape((c_in, slab * places), BF16),
            shape((slab, places, och), F32),
            shape((held, 8, och), F32),
            shape((slab, places, och), F32),
            shape((held * BMAX, slab, fold_rows, LANES), F32),
        ],
        [HBM] + [VMEM] * (devs + 4),
        [
            pltpu.VMEM((devs, rows_in, width), F32 if rows_in % 16 else BF16),
            smem[0],
            pltpu.SemaphoreType.DMA((1,)),
        ],
        large,
    )(clip_blocks, gain, bias, *shards, video_pad, table)
    acts, keep, send, *video_grads = call(
        functools.partial(backward_kernel, dims),
        [
            pltpu.HBM((devs * slab, fold_rows + 8, LANES), BF16),
            shape((chips, rows_in, 9 * LANES), F32),
            shape((chips, rows_in, 9 * LANES), BF16),
        ]
        + [shape((places, c_in), F32 if i == 0 else BF16) for i in range(slab)],
        [VMEM] * 9,
        [
            pltpu.VMEM((devs * slab, fold_rows + 8, LANES), BF16),
            pltpu.VMEM((slab + 2, places, 3 * LANES), BF16),
            pltpu.VMEM((slab, places, c_in), F32),
            pltpu.SemaphoreType.DMA((1,)),
        ],
        large,
        [HBM] + [VMEM] * (2 + slab),
    )(slot_of, gain, weights, video_t, normed, inv_std, slope, act, cots)
    video_grads = shifts(video_grads, "slab")
    send = core_swap(send, "clips")
    acts = lax.all_to_all(acts, everyone, split_axis=0, concat_axis=0, tiled=True)
    kernel_grads = call(
        functools.partial(pair_kernel, chips),
        [shape((rows_in, cols), F32 if t == 0 else BF16) for t in range(chips)],
        [VMEM, VMEM],
    )(keep, send)
    table = call(
        functools.partial(table_kernel, och), [shape((width, width), BF16)], [ANY]
    )(kernel_grads[1])[0]
    kernel_grads = chip_swaps(kernel_grads, "clips")

    video_grad = call(
        sum_kernel,
        [shape((places, c_in), BF16)],
        [VMEM] * slab,
        cost=pl.CostEstimate(flops=STAGE, bytes_accessed=0, transcendentals=0),
    )(*video_grads)[0]
    outs = [
        ((rows_in, cols), F32),
        ((slots, block_rows, c_out), BF16),
        ((1, c_out), F32),
        ((1, c_out), F32),
    ]
    kernel_grad, act, gain_grad, bias_grad = call(
        functools.partial(finish_kernel, (devs, slab, slots, och)),
        [pltpu.HBM(*out) for out in outs],
        [VMEM] * (3 + chips),
        [pltpu.VMEM(*out) for out in outs] + [pltpu.SemaphoreType.DMA((4,))],
        2 * slab * MIB,
        [HBM] * 4,
    )(holds, acts, table, *kernel_grads)
    return (
        act.reshape(cotangent.shape),
        video_grad.reshape(video.shape),
        kernel_grad,
        gain_grad.reshape(c_out),
        bias_grad.reshape(c_out),
    )


def solution(mesh):
    return jax.shard_map(
        body,
        mesh=mesh,
        in_specs=(
            P("clips", None, "slab", None, None),
            P(),
            P(),
            P("clips", "slab"),
            P(),
            P(),
            P("clips", None, "slab", None, None),
        ),
        out_specs=(
            P("clips", None, "slab", None, None),
            P("clips", None, "slab", None, None),
            P("clips", "slab"),
            P(),
            P(),
        ),
        check_vma=False,
    )
```

```python
import functools

import jax
import jax.numpy as jnp
from jax import lax
from jax.experimental import pallas as pl
from jax.experimental.pallas import tpu as pltpu
from jax.sharding import PartitionSpec as P

GROUPS = 16
TAPS = 27
FB = 2
BMAX = 3
LANES = 128
F32 = jnp.float32
BF16 = jnp.bfloat16
HBM = pl.BlockSpec(memory_space=pltpu.HBM)
ANY = pl.BlockSpec(memory_space=pl.ANY)
VMEM = pl.BlockSpec(memory_space=pltpu.VMEM)
MIB = 1024 * 1024
FIRST = 10**6
STAGE = 10**10


def round_up(value, unit):
    return -(-value // unit) * unit


def fold(values, slice_index, och, unit):
    groups = LANES // och
    rows = round_up(-(-values.shape[0] // groups), unit)
    short = rows * groups - values.shape[0]
    if short:
        values = jnp.concatenate([values, jnp.zeros((short, LANES), values.dtype)], axis=0)
    lane_group = lax.broadcasted_iota(jnp.int32, (rows, LANES), 1) // och
    total = jnp.zeros((rows, LANES), F32)
    for g in range(groups):
        shift = (g - slice_index) * och % LANES
        moved = pltpu.roll(values[g * rows : (g + 1) * rows], shift, 1) if shift else values[g * rows : (g + 1) * rows]
        total = total + jnp.where(lane_group == g, moved, 0.0)
    return total


def first_block_of(blocks_ref, first_clip, clips):
    start = jnp.int32(0)
    for k in range(clips):
        start = start + jnp.where(k < first_clip, blocks_ref[k], 0)
    return start


def slot_holders(blocks_ref, order_ref, me, slots, clips, held, devs):
    residue = jnp.int32(0)
    for r in range(devs):
        residue = jnp.where(order_ref[r] == me, r, residue)
    clip_of = [jnp.int32(0)] * slots
    end = jnp.int32(0)
    for k in range(clips):
        end = end + blocks_ref[k]
        for q in range(slots):
            clip_of[q] = clip_of[q] + jnp.where(end <= q * devs + residue, 1, 0)
    return [jnp.minimum(c, clips - 1) // held for c in clip_of]


def split3(values):
    high = values.astype(BF16).astype(F32)
    rest = values - high
    middle = rest.astype(BF16).astype(F32)
    return [high, middle, rest - middle]


def fetch(pairs, sems):
    copies = [pltpu.make_async_copy(a, b, sems.at[i]) for i, (a, b) in enumerate(pairs)]
    for copy in copies:
        copy.start()
    return copies


def send_kernel(
    dims,
    blocks_hbm,
    order_hbm,
    cot_hbm,
    out_ref,
    holds_ref,
    slots_ref,
    blocks_ref,
    order_ref,
    cot_ref,
    sems,
):
    devs, slab, slots, clips, held, och = dims
    pairs = [(blocks_hbm, blocks_ref), (order_hbm, order_ref), (cot_hbm, cot_ref)]
    copies = fetch(pairs, sems)
    out_ref[...] = jnp.zeros_like(out_ref)
    for copy in copies:
        copy.wait()
    me = lax.axis_index("clips")
    start = first_block_of(blocks_ref, me * held, clips)
    for k in range(held):
        count = blocks_ref[me * held + k]
        for b in range(BMAX):
            device = jnp.where(b < count, order_ref[jnp.mod(start + b, devs)], devs)
            for d in range(devs):
                hit = jnp.where(device == d, 1.0, 0.0)
                slots_ref[(k * BMAX + b) * devs + d] = jnp.full((1, LANES), hit, F32)
        start = start + count
    holders = slot_holders(blocks_ref, order_ref, me, slots, clips, held, devs)
    for q in range(slots):
        block = cot_ref[q].astype(F32)
        for s in range(slab):
            out_ref[holders[q] * slab + s] = fold(block, s, och, 8).astype(BF16)
        for d in range(devs):
            holds_ref[q * devs + d] = jnp.full((1, LANES), jnp.where(holders[q] == d, 1.0, 0.0), F32)


def make_table(och, out_ref):
    rows = out_ref.shape[0]
    lane = lax.broadcasted_iota(jnp.int32, (8, LANES), 1)
    source = jnp.where(lane < 3 * och, 27 * (lane % och) + 9 * (2 - lane // och), -rows)
    ahead = source - lax.broadcasted_iota(jnp.int32, (8, LANES), 0)
    for group in range(9):
        for i in range(0, rows, 16):
            top = jnp.where(ahead == i - group, 1.0, 0.0)
            bottom = jnp.where(ahead == i + 8 - group, 1.0, 0.0)
            both = jnp.concatenate([top, bottom], axis=0).astype(BF16)
            out_ref[i : i + 16, group * LANES : (group + 1) * LANES] = both


def stage_kernel(slab, och, *refs):
    video_refs, video_pad, table_ref, sems = refs[1:slab], refs[slab], refs[slab + 1], refs[slab + 2]
    own = lax.axis_index("slab")
    copy = fetch([(refs[0], video_pad.at[own + 1])], sems)[0]
    make_table(och, table_ref)
    zeros = jnp.zeros(video_pad.shape[1:], BF16)
    video_pad[0] = zeros
    video_pad[slab + 1] = zeros
    for i in range(1, slab):
        video_pad[jnp.mod(own - i + slab, slab) + 1] = video_refs[-i][...]
    copy.wait()


def forward_kernel(dims, blocks_hbm, slots_ref, gain_ref, bias_ref, *refs):
    devs, slab, clips, held, frames, columns, rows_in, cols, och, per_group = dims
    shard_refs, video_pad, table_ref = refs[:devs], refs[devs], refs[devs + 1]
    weights_ref, video_t_ref, normed_ref, inv_ref, slope_ref, act_ref = refs[devs + 2 : devs + 8]
    act_hbm, act_ref = act_ref, refs[devs + 8]
    shards, blocks_ref, sems = refs[devs + 9 :]
    copy = fetch([(blocks_hbm, blocks_ref)], sems)[0]
    me, own = lax.axis_index("clips"), lax.axis_index("slab")
    places = held * frames * columns
    per_clip = frames * columns
    c_in = video_pad.shape[2]
    many = slab * places
    width = table_ref.shape[0]
    chips = devs // 2
    for t in range(chips):
        for e in range(2):
            source = 2 * ((me // 2) ^ t) + (me % 2 + e) % 2
            shard = shard_refs[t + e * chips][...].astype(F32)
            shard = jnp.concatenate([shard, jnp.zeros((rows_in, width - cols), F32)], axis=1)
            shards[source] = shard.astype(shards.dtype)
    weights = shards[...].reshape(c_in, width).astype(BF16)
    weights = jnp.dot(weights, table_ref[...], preferred_element_type=F32).astype(BF16)

    total = jnp.dot(
        jnp.concatenate([video_pad[b : b + slab].reshape(many, c_in) for b in range(3)], axis=1),
        jnp.concatenate([weights[:, 384 * b : 384 * (b + 1)] for b in range(3)], axis=0),
        preferred_element_type=F32,
    )
    mixed = (
        from_left(total[:, 0:LANES], columns)
        + total[:, LANES : 2 * LANES]
        + from_right(total[:, 2 * LANES :], columns)
    ).reshape(slab, places, LANES)
    frame_shifts = [mixed[:, :, a * och : (a + 1) * och] for a in range(3)]
    frame_of = lax.broadcasted_iota(jnp.int32, (slab, per_clip, och), 1) // columns
    shift = jnp.mod(LANES - own * och, LANES)
    gain = pltpu.roll(jnp.broadcast_to(gain_ref[...], (8, LANES)), shift, 1)[0:1, :och]
    bias = pltpu.roll(jnp.broadcast_to(bias_ref[...], (8, LANES)), shift, 1)[0:1, :och]
    block_rows = FB * columns
    copy.wait()
    convs, kept, counts, limits = [], [], [], []
    for k in range(held):
        blocks = blocks_ref[me * held + k]
        conv = frame_shifts[0][:, k * per_clip : (k + 1) * per_clip]
        for a in (1, 2):
            part = frame_shifts[a][:, k * per_clip : (k + 1) * per_clip - a * columns]
            conv = conv + jnp.concatenate([jnp.zeros((slab, a * columns, och), F32), part], axis=1)
        convs.append(conv)
        kept.append(jnp.where(frame_of < blocks * FB, conv, 0.0))
        count = (blocks * (FB * slab * columns * per_group)).astype(F32)
        counts.append(jnp.full((1, och), count, F32))
        limits.append(jnp.full((1, och), (blocks * FB).astype(F32), F32))
    sums = group_sums(kept + [a * b for a, b in zip(kept, convs)], per_group)
    act_blocks = []
    for k in range(held):
        conv = convs[k]
        mean = sums[k] / counts[k]
        inv_std = lax.rsqrt(sums[held + k] / counts[k] - mean * mean + 1e-05)
        inv_ref[k] = jnp.concatenate([inv_std, counts[k], limits[k], jnp.zeros((5, och), F32)], axis=0)
        mean, inv_std = mean[None], inv_std[None]
        normed = (conv - mean) * inv_std
        normed_ref[:, k * per_clip : (k + 1) * per_clip, :] = normed
        affine = normed * gain[None] + bias[None]
        sigmoid = jax.nn.sigmoid(affine)
        act = affine * sigmoid
        slope = sigmoid * (1.0 + affine * (1.0 - sigmoid))
        slope_ref[:, k * per_clip : (k + 1) * per_clip, :] = slope
        for b in range(BMAX):
            for h in range(slab):
                block = act[h, b * block_rows : (b + 1) * block_rows]
                act_blocks.append(unfolded_to_lanes(block, 8))
    for d in range(devs):
        for h in range(slab):
            total = None
            for j in range(held * BMAX):
                term = act_blocks[j * slab + h] * slots_ref[j * devs + d]
                total = term if total is None else total + term
            pairs = [total[i : i + 2] for i in range(0, total.shape[0], 2)] + [jnp.zeros((2, LANES), F32)]
            act_ref[d * slab + h] = jnp.concatenate(pairs, axis=1).astype(BF16)
    act_copy = pltpu.make_async_copy(act_ref, act_hbm, sems.at[1])
    act_copy.start()
    weights_ref[...] = jnp.transpose(weights)
    video_t_ref[...] = jnp.transpose(video_pad[1 : slab + 1].reshape(many, c_in))
    act_copy.wait()


def from_left(values, columns):
    column = lax.broadcasted_iota(jnp.int32, values.shape, 0) % columns
    return jnp.where(column > 0, pltpu.roll(values, 1, 0), 0.0)


def from_right(values, columns):
    column = lax.broadcasted_iota(jnp.int32, values.shape, 0) % columns
    return jnp.where(column < columns - 1, pltpu.roll(values, values.shape[0] - 1, 0), 0.0)


def group_sums(arrays, per_group):
    och = arrays[0].shape[-1]
    rows = [jnp.sum(jnp.sum(a, axis=0), axis=0, keepdims=True) for a in arrays]
    rows.append(jnp.zeros((-len(rows) % 8, och), F32))
    total = jnp.concatenate([r for r in rows if r.shape[0]], axis=0)
    if och < LANES:
        total = jnp.concatenate([total, jnp.zeros((total.shape[0], LANES - och), F32)], axis=1)
    lane = lax.broadcasted_iota(jnp.int32, total.shape, 1)
    step = 1
    while step < per_group:
        down, up = pltpu.roll(total, LANES - step, 1), pltpu.roll(total, step, 1)
        total = total + jnp.where((lane // step) % 2 == 0, down, up)
        step *= 2
    return [total[i : i + 1, :och] for i in range(len(arrays))]


def backward_kernel(dims, slots_ref, gain_ref, weights_ref, *refs):
    devs, slab, clips, held, frames, columns, rows_in, cols, och, per_group = dims
    video_t_ref, normed_ref, inv_ref, slope_ref, act_in, cot_ref = refs[:6]
    act_hbm, keep_ref, send_ref = refs[6:9]
    video_grad_refs = refs[9 : 9 + slab]
    sums_ref, grad_ref, rows_ref, sems = refs[9 + slab :]
    me, own = lax.axis_index("clips"), lax.axis_index("slab")
    places = held * frames * columns
    per_clip = frames * columns
    block_rows = FB * columns
    c_in = video_t_ref.shape[0]
    groups = LANES // och
    many = slab * places
    shift = jnp.mod(LANES - own * och, LANES)
    gain = pltpu.roll(jnp.broadcast_to(gain_ref[...], (8, LANES)), shift, 1)[0:1, :och]
    frame_of = lax.broadcasted_iota(jnp.int32, (slab, per_clip, och), 1) // columns
    frame_of = frame_of.astype(F32)
    gain_part = jnp.zeros((1, och), F32)
    bias_part = jnp.zeros((1, och), F32)
    blocks = [[None] * slab for _ in range(held * BMAX)]
    for d in range(devs):
        for s in range(slab):
            folded = cot_ref[d * slab + s].astype(F32)
            for j in range(held * BMAX):
                term = folded * slots_ref[j * devs + d]
                blocks[j][s] = term if d == 0 else blocks[j][s] + term
    normeds, grads, alives = [], [], []
    for k in range(held):
        cot = []
        for b in range(BMAX):
            rows = []
            for folded in blocks[k * BMAX + b]:
                parts = [folded[:, g * och : (g + 1) * och] for g in range(groups)]
                rows.append(jnp.concatenate(parts, axis=0)[:block_rows])
            cot.append(jnp.stack(rows, axis=0))
        cot = jnp.concatenate(cot, axis=1)
        alive = frame_of < inv_ref[k][None, 2:3]
        normed = normed_ref[:, k * per_clip : (k + 1) * per_clip, :]
        slope = slope_ref[:, k * per_clip : (k + 1) * per_clip, :]
        grad_affine = jnp.where(alive, cot * slope, 0.0)
        gain_part += jnp.sum(jnp.sum(grad_affine * normed, axis=0), axis=0, keepdims=True)
        bias_part += jnp.sum(jnp.sum(grad_affine, axis=0), axis=0, keepdims=True)
        normeds.append(normed)
        grads.append(grad_affine * gain[None])
        alives.append(alive)
    sums = group_sums(grads + [a * b for a, b in zip(grads, normeds)], per_group)
    conv_grads = []
    for k in range(held):
        inv_std, count = inv_ref[k][None, 0:1], inv_ref[k][1:2]
        mean_grad, mean_cross = (sums[k] / count)[None], (sums[held + k] / count)[None]
        grad_conv = inv_std * (grads[k] - mean_grad - normeds[k] * mean_cross)
        grad_conv = jnp.where(alives[k], grad_conv, 0.0).astype(BF16).astype(F32)
        lanes = [grad_conv]
        for a in (1, 2):
            zeros = jnp.zeros((slab, a * columns, och), F32)
            lanes.append(jnp.concatenate([grad_conv[:, a * columns :], zeros], axis=1))
        if LANES > 3 * och:
            lanes.append(jnp.zeros((slab, per_clip, LANES - 3 * och), F32))
        conv_grads.append(jnp.concatenate(lanes, axis=2))

    sums = split3(gain_part) + split3(bias_part)
    sums = [jnp.concatenate(sums[:4], axis=1), jnp.concatenate(sums[4:] + [jnp.zeros((1, 2 * och), F32)], axis=1)]
    sums = jnp.concatenate(sums, axis=0)
    if LANES > 4 * och:
        sums = jnp.concatenate([sums, jnp.zeros((2, LANES - 4 * och), F32)], axis=1)
    sums_ref[...] = jnp.broadcast_to(sums.astype(BF16)[None], sums_ref.shape)
    last = act_hbm.shape[2] - LANES
    sums_copy = pltpu.make_async_copy(sums_ref, act_hbm.at[:, :, last : last + LANES], sems.at[0])
    sums_copy.start()

    grads = jnp.concatenate(conv_grads, axis=1).reshape(many, LANES)
    grad_ref[0] = jnp.zeros((places, 3 * LANES), BF16)
    grad_ref[slab + 1] = jnp.zeros((places, 3 * LANES), BF16)
    for e, shifted in enumerate((from_right(grads, columns), grads, from_left(grads, columns))):
        shifted = shifted.astype(BF16).reshape(slab, places, LANES)
        grad_ref[1 : slab + 1, :, e * LANES : (e + 1) * LANES] = shifted

    moved = [grad_ref[2 - b : 2 - b + slab].reshape(many, 3 * LANES) for b in range(3)]
    moved = jnp.concatenate(moved, axis=1)
    total = jnp.dot(moved, weights_ref[...], preferred_element_type=F32)
    rows_ref[...] = total.reshape(slab, places, c_in)
    for i, ref in enumerate(video_grad_refs):
        ref[...] = rows_ref[jnp.mod(own + i, slab)].astype(ref.dtype)

    terms = jnp.dot(video_t_ref[...], moved, preferred_element_type=F32)
    terms = terms.reshape(devs // 2, 2 * rows_in, 9 * LANES)
    low, high = terms[:, :rows_in], terms[:, rows_in:]
    odd = me % 2 == 1
    keep_ref[...] = jnp.where(odd, high, low)
    send_ref[...] = jnp.where(odd, low, high).astype(BF16)
    sums_copy.wait()


def unfolded_to_lanes(values, unit):
    groups = LANES // values.shape[1]
    rows = round_up(-(-values.shape[0] // groups), unit)
    short = rows * groups - values.shape[0]
    if short:
        values = jnp.concatenate([values, jnp.zeros((short, values.shape[1]), F32)], axis=0)
    return jnp.concatenate([values[g * rows : (g + 1) * rows] for g in range(groups)], axis=1)


def pair_kernel(chips, keep_ref, other_ref, *outs):
    me = lax.axis_index("clips") // 2
    cols = outs[0].shape[1]
    used = cols // 9
    for t, ref in enumerate(outs):
        chip = partner(me, t, chips)
        total = keep_ref[chip] + other_ref[chip].astype(F32)
        parts = [total[:, g * LANES : g * LANES + used] for g in range(9)]
        ref[...] = jnp.concatenate(parts, axis=1).astype(ref.dtype)


def sum_kernel(*refs):
    total = refs[0][...]
    for ref in refs[1:-1]:
        total = total + ref[...].astype(F32)
    refs[-1][...] = total.astype(refs[-1].dtype)


def table_kernel(och, after_ref, table_ref):
    rows, cols = table_ref.shape
    place = lax.broadcasted_iota(jnp.int32, (LANES, LANES), 0)
    column = lax.broadcasted_iota(jnp.int32, (LANES, LANES), 1)
    for i in range(0, rows, LANES):
        inner = (place + i) % (3 * och)
        source = 27 * (inner % och) + 9 * (2 - inner // och) + (place + i) // (3 * och)
        ahead = jnp.where(place + i < 27 * och, source, -cols) - column
        for j in range(0, cols, LANES):
            table_ref[i : i + LANES, j : j + LANES] = jnp.where(ahead == j, 1.0, 0.0).astype(BF16)


def finish_kernel(dims, holds_ref, act_in, table_ref, *refs):
    devs, slab, slots, och = dims
    chips = devs // 2
    kernel_refs, hbm_refs = refs[:chips], refs[chips : chips + 4]
    out_refs, sems = refs[chips + 4 : chips + 8], refs[chips + 8]
    kernel_grad_ref, act_ref, gain_ref, bias_ref = out_refs
    copies = [pltpu.make_async_copy(a, b, sems.at[i]) for i, (a, b) in enumerate(zip(out_refs, hbm_refs))]

    total = kernel_refs[0][...]
    for ref in kernel_refs[1:]:
        total = total + ref[...].astype(F32)
    rows, cols = total.shape
    width = table_ref.shape[0]
    if width > cols:
        total = jnp.concatenate([total, jnp.zeros((rows, width - cols), F32)], axis=1)
    native = jnp.dot(
        jnp.concatenate(split3(total), axis=0).astype(BF16),
        table_ref[...],
        preferred_element_type=F32,
    )
    native = native[:rows] + (native[rows : 2 * rows] + native[2 * rows :])
    kernel_grad_ref[...] = native[:, :cols]
    copies[0].start()

    groups = LANES // och
    pairs = act_in.shape[2] // LANES - 1
    sums = []
    blocks = [[jnp.zeros((2 * pairs, LANES), F32)] * slab for _ in range(slots)]
    for s in range(slab):
        part = jnp.zeros((2, LANES), F32)
        for d in range(devs):
            both = act_in[d * slab + s].astype(F32)
            part = part + both[:, pairs * LANES :]
            both = [both[:, i * LANES : (i + 1) * LANES] for i in range(pairs)]
            both = jnp.concatenate(both, axis=0)
            for q in range(slots):
                blocks[q][s] = blocks[q][s] + both * holds_ref[q * devs + d]
        sums.append(part)
    for q in range(slots):
        block = []
        for g in range(groups):
            parts = [p[:, g * och : (g + 1) * och] for p in blocks[q]]
            block.append(jnp.concatenate(parts, axis=1))
        act_ref[q] = jnp.concatenate(block, axis=0)[: act_ref.shape[1]].astype(BF16)
    copies[1].start()
    gains = [p[0:1, :och] + (p[0:1, och : 2 * och] + p[0:1, 2 * och : 3 * och]) for p in sums]
    gain_ref[...] = jnp.concatenate(gains, axis=1)
    biases = [p[0:1, 3 * och : 4 * och] + (p[1:2, :och] + p[1:2, och : 2 * och]) for p in sums]
    bias_ref[...] = jnp.concatenate(biases, axis=1)
    copies[2].start()
    copies[3].start()
    for copy in copies:
        copy.wait()


def call(kernel, outs, specs, scratch=(), limit=None, out_specs=None, cost=None, alias=None):
    limit = limit or lax.axis_size("slab") * MIB
    return pl.pallas_call(
        kernel,
        out_shape=outs,
        in_specs=specs,
        out_specs=out_specs or [VMEM] * len(outs),
        cost_estimate=cost,
        input_output_aliases=alias or {},
        scratch_shapes=list(scratch),
        compiler_params=pltpu.CompilerParams(vmem_limit_bytes=limit),
    )


def partner(index, step, size):
    return index ^ step if size & (size - 1) == 0 else (index + step) % size


def shifts(arrays, axis):
    size = lax.axis_size(axis)
    moved = [arrays[0]]
    for i in range(1, size):
        moved.append(lax.ppermute(arrays[i], axis, [(j, (j + i) % size) for j in range(size)]))
    return moved


def chip_swaps(arrays, axis):
    size = lax.axis_size(axis)
    moved = [arrays[0]]
    for t in range(1, size // 2):
        pairs = [(j, 2 * partner(j // 2, t, size // 2) + j % 2) for j in range(size)]
        moved.append(lax.ppermute(arrays[t], axis, pairs))
    return moved


def core_swap(array, axis):
    return lax.ppermute(array, axis, [(j, j ^ 1) for j in range(lax.axis_size(axis))])


def body(video, clip_blocks, deal_order, kernel, gain, bias, cotangent):
    devs, slab = lax.axis_size("clips"), lax.axis_size("slab")
    held, frames, _, columns, c_in = video.shape
    slots, clips = cotangent.shape[0], clip_blocks.shape[0]
    c_out = gain.shape[0]
    rows_in, cols = kernel.shape
    och = c_out // slab
    per_group = c_out // GROUPS
    width = round_up(cols, LANES)
    places = held * frames * columns
    block_rows = FB * columns
    fold_rows = round_up(-(-block_rows // (LANES // och)), 8)
    chips = devs // 2
    everyone = ("clips", "slab")
    act_shape = (devs * slab, 2, fold_rows // 2 * LANES + LANES)
    shape = jax.ShapeDtypeStruct
    smem = [pltpu.SMEM((clips,), jnp.int32), pltpu.SMEM((devs,), jnp.int32)]
    large = (6 + 3 * slab) * MIB
    gain, bias = gain.reshape(1, c_out), bias.reshape(1, c_out)
    clip_blocks = pltpu.with_memory_space_constraint(clip_blocks, pltpu.HBM)
    deal_order = pltpu.with_memory_space_constraint(deal_order, pltpu.HBM)
    cotangent_blocks = pltpu.with_memory_space_constraint(
        cotangent.reshape(slots, block_rows, c_out), pltpu.HBM
    )

    videos = shifts([video.reshape(places, c_in)] * slab, "slab")
    cots, holds, slot_of = call(
        functools.partial(send_kernel, (devs, slab, slots, clips, held, och)),
        [shape((devs * slab, fold_rows, LANES), BF16), shape((slots * devs, 1, LANES), F32)]
        + [shape((held * BMAX * devs, 1, LANES), F32)],
        [HBM, HBM, HBM],
        smem + [pltpu.VMEM((slots, block_rows, c_out), BF16), pltpu.SemaphoreType.DMA((3,))],
        cost=pl.CostEstimate(flops=FIRST, bytes_accessed=0, transcendentals=0),
    )(clip_blocks, deal_order, cotangent_blocks)
    cots = lax.all_to_all(cots, everyone, split_axis=0, concat_axis=0, tiled=True)
    shards = [kernel]
    while len(shards) < chips:
        pairs = [(j, j ^ (2 * len(shards))) for j in range(devs)]
        shards = shards + [lax.ppermute(shard, "clips", pairs) for shard in shards]
    shards = shards + [core_swap(shard, "clips") for shard in shards]

    dims = (devs, slab, clips, held, frames, columns, rows_in, cols, och, per_group)
    video_pad, table = call(
        functools.partial(stage_kernel, slab, och),
        [shape((slab + 2, places, c_in), BF16), shape((width, 9 * LANES), BF16)],
        [HBM] + [VMEM] * (slab - 1),
        [pltpu.SemaphoreType.DMA((1,))],
        cost=pl.CostEstimate(flops=STAGE, bytes_accessed=0, transcendentals=0),
    )(pltpu.with_memory_space_constraint(videos[0], pltpu.HBM), *videos[:0:-1])
    weights, video_t, normed, inv_std, slope, act = call(
        functools.partial(forward_kernel, dims),
        [
            shape((9 * LANES, c_in), BF16),
            shape((c_in, slab * places), BF16),
            shape((slab, places, och), F32),
            shape((held, 8, och), F32),
            shape((slab, places, och), F32),
            pltpu.HBM(act_shape, BF16),
        ],
        [HBM] + [VMEM] * (devs + 5),
        [
            pltpu.VMEM(act_shape, BF16),
            pltpu.VMEM((devs, rows_in, width), F32 if rows_in % 16 else BF16),
            smem[0],
            pltpu.SemaphoreType.DMA((2,)),
        ],
        large,
        [VMEM] * 5 + [HBM],
    )(clip_blocks, slot_of, gain, bias, *shards, video_pad, table)
    acts, keep, send, *video_grads = call(
        functools.partial(backward_kernel, dims),
        [
            pltpu.HBM(act_shape, BF16),
            shape((chips, rows_in, 9 * LANES), F32),
            shape((chips, rows_in, 9 * LANES), BF16),
        ]
        + [shape((places, c_in), F32 if i == 0 else BF16) for i in range(slab)],
        [VMEM] * 7 + [HBM, VMEM],
        [
            pltpu.VMEM((devs * slab, 2, LANES), BF16),
            pltpu.VMEM((slab + 2, places, 3 * LANES), BF16),
            pltpu.VMEM((slab, places, c_in), F32),
            pltpu.SemaphoreType.DMA((1,)),
        ],
        large,
        [HBM] + [VMEM] * (2 + slab),
        alias={7: 0},
    )(slot_of, gain, weights, video_t, normed, inv_std, slope, act, cots)
    video_grads = shifts(video_grads, "slab")
    send = core_swap(send, "clips")
    acts = lax.all_to_all(acts, everyone, split_axis=0, concat_axis=0, tiled=True)
    kernel_grads = call(
        functools.partial(pair_kernel, chips),
        [shape((rows_in, cols), F32 if t == 0 else BF16) for t in range(chips)],
        [VMEM, VMEM],
    )(keep, send)
    table = call(
        functools.partial(table_kernel, och), [shape((width, width), BF16)], [ANY]
    )(kernel_grads[1])[0]
    kernel_grads = chip_swaps(kernel_grads, "clips")

    video_grad = call(
        sum_kernel,
        [shape((places, c_in), BF16)],
        [VMEM] * slab,
        cost=pl.CostEstimate(flops=STAGE, bytes_accessed=0, transcendentals=0),
    )(*video_grads)[0]
    outs = [
        ((rows_in, cols), F32),
        ((slots, block_rows, c_out), BF16),
        ((1, c_out), F32),
        ((1, c_out), F32),
    ]
    kernel_grad, act, gain_grad, bias_grad = call(
        functools.partial(finish_kernel, (devs, slab, slots, och)),
        [pltpu.HBM(*out) for out in outs],
        [VMEM] * (3 + chips),
        [pltpu.VMEM(*out) for out in outs] + [pltpu.SemaphoreType.DMA((4,))],
        2 * slab * MIB,
        [HBM] * 4,
    )(holds, acts, table, kernel_grads[0], *kernel_grads[:0:-1])
    return (
        act.reshape(cotangent.shape),
        video_grad.reshape(video.shape),
        kernel_grad,
        gain_grad.reshape(c_out),
        bias_grad.reshape(c_out),
    )


def solution(mesh):
    return jax.shard_map(
        body,
        mesh=mesh,
        in_specs=(
            P("clips", None, "slab", None, None),
            P(),
            P(),
            P("clips", "slab"),
            P(),
            P(),
            P("clips", None, "slab", None, None),
        ),
        out_specs=(
            P("clips", None, "slab", None, None),
            P("clips", None, "slab", None, None),
            P("clips", "slab"),
            P(),
            P(),
        ),
        check_vma=False,
    )
```

```python
import functools

import jax
import jax.numpy as jnp
from jax import lax
from jax.experimental import pallas as pl
from jax.experimental.pallas import tpu as pltpu
from jax.sharding import PartitionSpec as P

GROUPS = 16
TAPS = 27
FB = 2
BMAX = 3
LANES = 128
F32 = jnp.float32
BF16 = jnp.bfloat16
HBM = pl.BlockSpec(memory_space=pltpu.HBM)
ANY = pl.BlockSpec(memory_space=pl.ANY)
VMEM = pl.BlockSpec(memory_space=pltpu.VMEM)
MIB = 1024 * 1024
FIRST = 10**6
STAGE = 10**10


def round_up(value, unit):
    return -(-value // unit) * unit


def fold(values, slice_index, och, unit):
    groups = LANES // och
    rows = round_up(-(-values.shape[0] // groups), unit)
    short = rows * groups - values.shape[0]
    if short:
        values = jnp.concatenate([values, jnp.zeros((short, LANES), values.dtype)], axis=0)
    lane_group = lax.broadcasted_iota(jnp.int32, (rows, LANES), 1) // och
    total = jnp.zeros((rows, LANES), F32)
    for g in range(groups):
        shift = (g - slice_index) * och % LANES
        moved = pltpu.roll(values[g * rows : (g + 1) * rows], shift, 1) if shift else values[g * rows : (g + 1) * rows]
        total = total + jnp.where(lane_group == g, moved, 0.0)
    return total


def first_block_of(blocks_ref, first_clip, clips):
    start = jnp.int32(0)
    for k in range(clips):
        start = start + jnp.where(k < first_clip, blocks_ref[k], 0)
    return start


def slot_holders(blocks_ref, order_ref, me, slots, clips, held, devs):
    residue = jnp.int32(0)
    for r in range(devs):
        residue = jnp.where(order_ref[r] == me, r, residue)
    clip_of = [jnp.int32(0)] * slots
    end = jnp.int32(0)
    for k in range(clips):
        end = end + blocks_ref[k]
        for q in range(slots):
            clip_of[q] = clip_of[q] + jnp.where(end <= q * devs + residue, 1, 0)
    return [jnp.minimum(c, clips - 1) // held for c in clip_of]


def split3(values):
    high = values.astype(BF16).astype(F32)
    rest = values - high
    middle = rest.astype(BF16).astype(F32)
    return [high, middle, rest - middle]


def fetch(pairs, sems):
    copies = [pltpu.make_async_copy(a, b, sems.at[i]) for i, (a, b) in enumerate(pairs)]
    for copy in copies:
        copy.start()
    return copies


def send_kernel(
    dims,
    blocks_hbm,
    order_hbm,
    cot_hbm,
    out_hbm,
    holds_ref,
    slots_ref,
    blocks_ref,
    order_ref,
    cot_ref,
    out_ref,
    sems,
):
    devs, slab, slots, clips, held, och = dims
    pairs = [(blocks_hbm, blocks_ref), (order_hbm, order_ref), (cot_hbm, cot_ref)]
    copies = fetch(pairs, sems)
    out_ref[...] = jnp.zeros_like(out_ref)
    for copy in copies:
        copy.wait()
    me = lax.axis_index("clips")
    holders = slot_holders(blocks_ref, order_ref, me, slots, clips, held, devs)
    for q in range(slots):
        block = cot_ref[q].astype(F32)
        for s in range(slab):
            out_ref[holders[q] * slab + s] = fold(block, s, och, 8).astype(BF16)
    out_copy = pltpu.make_async_copy(out_ref, out_hbm, sems.at[3])
    out_copy.start()
    for q in range(slots):
        for d in range(devs):
            holds_ref[q * devs + d] = jnp.full((1, LANES), jnp.where(holders[q] == d, 1.0, 0.0), F32)
    start = first_block_of(blocks_ref, me * held, clips)
    for k in range(held):
        count = blocks_ref[me * held + k]
        for b in range(BMAX):
            device = jnp.where(b < count, order_ref[jnp.mod(start + b, devs)], devs)
            for d in range(devs):
                hit = jnp.where(device == d, 1.0, 0.0)
                slots_ref[(k * BMAX + b) * devs + d] = jnp.full((1, LANES), hit, F32)
        start = start + count
    out_copy.wait()


def make_table(och, out_ref):
    rows = out_ref.shape[0]
    lane = lax.broadcasted_iota(jnp.int32, (8, LANES), 1)
    source = jnp.where(lane < 3 * och, 27 * (lane % och) + 9 * (2 - lane // och), -rows)
    ahead = source - lax.broadcasted_iota(jnp.int32, (8, LANES), 0)
    for group in range(9):
        for i in range(0, rows, 16):
            top = jnp.where(ahead == i - group, 1.0, 0.0)
            bottom = jnp.where(ahead == i + 8 - group, 1.0, 0.0)
            both = jnp.concatenate([top, bottom], axis=0).astype(BF16)
            out_ref[i : i + 16, group * LANES : (group + 1) * LANES] = both


def stage_kernel(slab, och, *refs):
    video_refs, video_pad, table_ref, sems = refs[1:slab], refs[slab], refs[slab + 1], refs[slab + 2]
    own = lax.axis_index("slab")
    copy = fetch([(refs[0], video_pad.at[own + 1])], sems)[0]
    make_table(och, table_ref)
    zeros = jnp.zeros(video_pad.shape[1:], BF16)
    video_pad[0] = zeros
    video_pad[slab + 1] = zeros
    for i in range(1, slab):
        video_pad[jnp.mod(own - i + slab, slab) + 1] = video_refs[-i][...]
    copy.wait()


def forward_kernel(dims, blocks_hbm, slots_ref, gain_ref, bias_ref, *refs):
    devs, slab, clips, held, frames, columns, rows_in, cols, och, per_group = dims
    shard_refs, video_pad, table_ref = refs[:devs], refs[devs], refs[devs + 1]
    weights_ref, video_t_ref, normed_ref, inv_ref, slope_ref, act_ref = refs[devs + 2 : devs + 8]
    act_hbm, act_ref = act_ref, refs[devs + 8]
    shards, blocks_ref, sems = refs[devs + 9 :]
    copy = fetch([(blocks_hbm, blocks_ref)], sems)[0]
    me, own = lax.axis_index("clips"), lax.axis_index("slab")
    places = held * frames * columns
    per_clip = frames * columns
    c_in = video_pad.shape[2]
    many = slab * places
    width = table_ref.shape[0]
    chips = devs // 2
    for t in range(chips):
        for e in range(2):
            source = 2 * ((me // 2) ^ t) + (me % 2 + e) % 2
            shard = shard_refs[t + e * chips][...].astype(F32)
            shard = jnp.concatenate([shard, jnp.zeros((rows_in, width - cols), F32)], axis=1)
            shards[source] = shard.astype(shards.dtype)
    weights = shards[...].reshape(c_in, width).astype(BF16)
    weights = jnp.dot(weights, table_ref[...], preferred_element_type=F32).astype(BF16)

    total = jnp.dot(
        jnp.concatenate([video_pad[b : b + slab].reshape(many, c_in) for b in range(3)], axis=1),
        jnp.concatenate([weights[:, 384 * b : 384 * (b + 1)] for b in range(3)], axis=0),
        preferred_element_type=F32,
    )
    mixed = (
        from_left(total[:, 0:LANES], columns)
        + total[:, LANES : 2 * LANES]
        + from_right(total[:, 2 * LANES :], columns)
    ).reshape(slab, places, LANES)
    frame_shifts = [mixed[:, :, a * och : (a + 1) * och] for a in range(3)]
    frame_of = lax.broadcasted_iota(jnp.int32, (slab, per_clip, och), 1) // columns
    shift = jnp.mod(LANES - own * och, LANES)
    gain = pltpu.roll(jnp.broadcast_to(gain_ref[...], (8, LANES)), shift, 1)[0:1, :och]
    bias = pltpu.roll(jnp.broadcast_to(bias_ref[...], (8, LANES)), shift, 1)[0:1, :och]
    block_rows = FB * columns
    copy.wait()
    convs, kept, counts, limits = [], [], [], []
    for k in range(held):
        blocks = blocks_ref[me * held + k]
        conv = frame_shifts[0][:, k * per_clip : (k + 1) * per_clip]
        for a in (1, 2):
            part = frame_shifts[a][:, k * per_clip : (k + 1) * per_clip - a * columns]
            conv = conv + jnp.concatenate([jnp.zeros((slab, a * columns, och), F32), part], axis=1)
        convs.append(conv)
        kept.append(jnp.where(frame_of < blocks * FB, conv, 0.0))
        count = (blocks * (FB * slab * columns * per_group)).astype(F32)
        counts.append(jnp.full((1, och), count, F32))
        limits.append(jnp.full((1, och), (blocks * FB).astype(F32), F32))
    sums = group_sums(kept + [a * b for a, b in zip(kept, convs)], per_group)
    act_blocks = []
    for k in range(held):
        conv = convs[k]
        mean = sums[k] / counts[k]
        inv_std = lax.rsqrt(sums[held + k] / counts[k] - mean * mean + 1e-05)
        inv_ref[k] = jnp.concatenate([inv_std, counts[k], limits[k], jnp.zeros((5, och), F32)], axis=0)
        mean, inv_std = mean[None], inv_std[None]
        normed = (conv - mean) * inv_std
        normed_ref[:, k * per_clip : (k + 1) * per_clip, :] = normed
        affine = normed * gain[None] + bias[None]
        sigmoid = jax.nn.sigmoid(affine)
        act = affine * sigmoid
        slope = sigmoid * (1.0 + affine * (1.0 - sigmoid))
        slope_ref[:, k * per_clip : (k + 1) * per_clip, :] = slope
        for b in range(BMAX):
            for h in range(slab):
                block = act[h, b * block_rows : (b + 1) * block_rows]
                act_blocks.append(unfolded_to_lanes(block, 8))
    for d in range(devs):
        for h in range(slab):
            total = None
            for j in range(held * BMAX):
                term = act_blocks[j * slab + h] * slots_ref[j * devs + d]
                total = term if total is None else total + term
            pairs = [total[i : i + 2] for i in range(0, total.shape[0], 2)] + [jnp.zeros((2, LANES), F32)]
            act_ref[d * slab + h] = jnp.concatenate(pairs, axis=1).astype(BF16)
    act_copy = pltpu.make_async_copy(act_ref, act_hbm, sems.at[1])
    act_copy.start()
    weights_ref[...] = jnp.transpose(weights)
    video_t_ref[...] = jnp.transpose(video_pad[1 : slab + 1].reshape(many, c_in))
    act_copy.wait()


def from_left(values, columns):
    column = lax.broadcasted_iota(jnp.int32, values.shape, 0) % columns
    return jnp.where(column > 0, pltpu.roll(values, 1, 0), 0.0)


def from_right(values, columns):
    column = lax.broadcasted_iota(jnp.int32, values.shape, 0) % columns
    return jnp.where(column < columns - 1, pltpu.roll(values, values.shape[0] - 1, 0), 0.0)


def group_sums(arrays, per_group):
    och = arrays[0].shape[-1]
    rows = [jnp.sum(jnp.sum(a, axis=0), axis=0, keepdims=True) for a in arrays]
    rows.append(jnp.zeros((-len(rows) % 8, och), F32))
    total = jnp.concatenate([r for r in rows if r.shape[0]], axis=0)
    if och < LANES:
        total = jnp.concatenate([total, jnp.zeros((total.shape[0], LANES - och), F32)], axis=1)
    lane = lax.broadcasted_iota(jnp.int32, total.shape, 1)
    step = 1
    while step < per_group:
        down, up = pltpu.roll(total, LANES - step, 1), pltpu.roll(total, step, 1)
        total = total + jnp.where((lane // step) % 2 == 0, down, up)
        step *= 2
    return [total[i : i + 1, :och] for i in range(len(arrays))]


def backward_kernel(dims, slots_ref, gain_ref, weights_ref, *refs):
    devs, slab, clips, held, frames, columns, rows_in, cols, och, per_group = dims
    video_t_ref, normed_ref, inv_ref, slope_ref, act_in, cot_ref = refs[:6]
    act_hbm, keep_ref, send_ref = refs[6:9]
    video_grad_refs = refs[9 : 9 + slab]
    sums_ref, grad_ref, rows_ref, sems = refs[9 + slab :]
    me, own = lax.axis_index("clips"), lax.axis_index("slab")
    places = held * frames * columns
    per_clip = frames * columns
    block_rows = FB * columns
    c_in = video_t_ref.shape[0]
    groups = LANES // och
    many = slab * places
    shift = jnp.mod(LANES - own * och, LANES)
    gain = pltpu.roll(jnp.broadcast_to(gain_ref[...], (8, LANES)), shift, 1)[0:1, :och]
    frame_of = lax.broadcasted_iota(jnp.int32, (slab, per_clip, och), 1) // columns
    frame_of = frame_of.astype(F32)
    gain_part = jnp.zeros((1, och), F32)
    bias_part = jnp.zeros((1, och), F32)
    blocks = [[None] * slab for _ in range(held * BMAX)]
    for d in range(devs):
        for s in range(slab):
            folded = cot_ref[d * slab + s].astype(F32)
            for j in range(held * BMAX):
                term = folded * slots_ref[j * devs + d]
                blocks[j][s] = term if d == 0 else blocks[j][s] + term
    normeds, grads, alives = [], [], []
    for k in range(held):
        cot = []
        for b in range(BMAX):
            rows = []
            for folded in blocks[k * BMAX + b]:
                parts = [folded[:, g * och : (g + 1) * och] for g in range(groups)]
                rows.append(jnp.concatenate(parts, axis=0)[:block_rows])
            cot.append(jnp.stack(rows, axis=0))
        cot = jnp.concatenate(cot, axis=1)
        alive = frame_of < inv_ref[k][None, 2:3]
        normed = normed_ref[:, k * per_clip : (k + 1) * per_clip, :]
        slope = slope_ref[:, k * per_clip : (k + 1) * per_clip, :]
        grad_affine = jnp.where(alive, cot * slope, 0.0)
        gain_part += jnp.sum(jnp.sum(grad_affine * normed, axis=0), axis=0, keepdims=True)
        bias_part += jnp.sum(jnp.sum(grad_affine, axis=0), axis=0, keepdims=True)
        normeds.append(normed)
        grads.append(grad_affine * gain[None])
        alives.append(alive)
    sums = group_sums(grads + [a * b for a, b in zip(grads, normeds)], per_group)
    conv_grads = []
    for k in range(held):
        inv_std, count = inv_ref[k][None, 0:1], inv_ref[k][1:2]
        mean_grad, mean_cross = (sums[k] / count)[None], (sums[held + k] / count)[None]
        grad_conv = inv_std * (grads[k] - mean_grad - normeds[k] * mean_cross)
        grad_conv = jnp.where(alives[k], grad_conv, 0.0).astype(BF16).astype(F32)
        lanes = [grad_conv]
        for a in (1, 2):
            zeros = jnp.zeros((slab, a * columns, och), F32)
            lanes.append(jnp.concatenate([grad_conv[:, a * columns :], zeros], axis=1))
        if LANES > 3 * och:
            lanes.append(jnp.zeros((slab, per_clip, LANES - 3 * och), F32))
        conv_grads.append(jnp.concatenate(lanes, axis=2))

    sums = split3(gain_part) + split3(bias_part)
    sums = [jnp.concatenate(sums[:4], axis=1), jnp.concatenate(sums[4:] + [jnp.zeros((1, 2 * och), F32)], axis=1)]
    sums = jnp.concatenate(sums, axis=0)
    if LANES > 4 * och:
        sums = jnp.concatenate([sums, jnp.zeros((2, LANES - 4 * och), F32)], axis=1)
    sums_ref[...] = jnp.broadcast_to(sums.astype(BF16)[None], sums_ref.shape)
    last = act_hbm.shape[2] - LANES
    sums_copy = pltpu.make_async_copy(sums_ref, act_hbm.at[:, :, last : last + LANES], sems.at[0])
    sums_copy.start()

    grads = jnp.concatenate(conv_grads, axis=1).reshape(many, LANES)
    grad_ref[0] = jnp.zeros((places, 3 * LANES), BF16)
    grad_ref[slab + 1] = jnp.zeros((places, 3 * LANES), BF16)
    for e, shifted in enumerate((from_right(grads, columns), grads, from_left(grads, columns))):
        shifted = shifted.astype(BF16).reshape(slab, places, LANES)
        grad_ref[1 : slab + 1, :, e * LANES : (e + 1) * LANES] = shifted

    moved = [grad_ref[2 - b : 2 - b + slab].reshape(many, 3 * LANES) for b in range(3)]
    moved = jnp.concatenate(moved, axis=1)
    total = jnp.dot(moved, weights_ref[...], preferred_element_type=F32)
    rows_ref[...] = total.reshape(slab, places, c_in)
    for i, ref in enumerate(video_grad_refs):
        ref[...] = rows_ref[jnp.mod(own + i, slab)].astype(ref.dtype)

    terms = jnp.dot(video_t_ref[...], moved, preferred_element_type=F32)
    terms = terms.reshape(devs // 2, 2 * rows_in, 9 * LANES)
    low, high = terms[:, :rows_in], terms[:, rows_in:]
    odd = me % 2 == 1
    keep_ref[...] = jnp.where(odd, high, low)
    send_ref[...] = jnp.where(odd, low, high).astype(BF16)
    sums_copy.wait()


def unfolded_to_lanes(values, unit):
    groups = LANES // values.shape[1]
    rows = round_up(-(-values.shape[0] // groups), unit)
    short = rows * groups - values.shape[0]
    if short:
        values = jnp.concatenate([values, jnp.zeros((short, values.shape[1]), F32)], axis=0)
    return jnp.concatenate([values[g * rows : (g + 1) * rows] for g in range(groups)], axis=1)


def pair_kernel(chips, keep_ref, other_ref, *outs):
    me = lax.axis_index("clips") // 2
    cols = outs[0].shape[1]
    used = cols // 9
    for t, ref in enumerate(outs):
        chip = partner(me, t, chips)
        total = keep_ref[chip] + other_ref[chip].astype(F32)
        parts = [total[:, g * LANES : g * LANES + used] for g in range(9)]
        ref[...] = jnp.concatenate(parts, axis=1).astype(ref.dtype)


def sum_kernel(*refs):
    total = refs[0][...]
    for ref in refs[1:-1]:
        total = total + ref[...].astype(F32)
    refs[-1][...] = total.astype(refs[-1].dtype)


def table_kernel(och, after_ref, table_ref):
    rows, cols = table_ref.shape
    place = lax.broadcasted_iota(jnp.int32, (LANES, LANES), 0)
    column = lax.broadcasted_iota(jnp.int32, (LANES, LANES), 1)
    for i in range(0, rows, LANES):
        inner = (place + i) % (3 * och)
        source = 27 * (inner % och) + 9 * (2 - inner // och) + (place + i) // (3 * och)
        ahead = jnp.where(place + i < 27 * och, source, -cols) - column
        for j in range(0, cols, LANES):
            table_ref[i : i + LANES, j : j + LANES] = jnp.where(ahead == j, 1.0, 0.0).astype(BF16)


def finish_kernel(dims, holds_ref, act_in, table_ref, *refs):
    devs, slab, slots, och = dims
    chips = devs // 2
    kernel_refs, hbm_refs = refs[:chips], refs[chips : chips + 4]
    out_refs, sems = refs[chips + 4 : chips + 8], refs[chips + 8]
    kernel_grad_ref, act_ref, gain_ref, bias_ref = out_refs
    copies = [pltpu.make_async_copy(a, b, sems.at[i]) for i, (a, b) in enumerate(zip(out_refs, hbm_refs))]

    groups = LANES // och
    pairs = act_in.shape[2] // LANES - 1
    sums = []
    blocks = [[jnp.zeros((2 * pairs, LANES), F32)] * slab for _ in range(slots)]
    for s in range(slab):
        part = jnp.zeros((2, LANES), F32)
        for d in range(devs):
            both = act_in[d * slab + s].astype(F32)
            part = part + both[:, pairs * LANES :]
            both = [both[:, i * LANES : (i + 1) * LANES] for i in range(pairs)]
            both = jnp.concatenate(both, axis=0)
            for q in range(slots):
                blocks[q][s] = blocks[q][s] + both * holds_ref[q * devs + d]
        sums.append(part)
    for q in range(slots):
        block = []
        for g in range(groups):
            parts = [p[:, g * och : (g + 1) * och] for p in blocks[q]]
            block.append(jnp.concatenate(parts, axis=1))
        act_ref[q] = jnp.concatenate(block, axis=0)[: act_ref.shape[1]].astype(BF16)
    copies[1].start()
    gains = [p[0:1, :och] + (p[0:1, och : 2 * och] + p[0:1, 2 * och : 3 * och]) for p in sums]
    gain_ref[...] = jnp.concatenate(gains, axis=1)
    biases = [p[0:1, 3 * och : 4 * och] + (p[1:2, :och] + p[1:2, och : 2 * och]) for p in sums]
    bias_ref[...] = jnp.concatenate(biases, axis=1)
    copies[2].start()
    copies[3].start()
    total = kernel_refs[0][...]
    for ref in kernel_refs[1:]:
        total = total + ref[...].astype(F32)
    rows, cols = total.shape
    width = table_ref.shape[0]
    if width > cols:
        total = jnp.concatenate([total, jnp.zeros((rows, width - cols), F32)], axis=1)
    native = jnp.dot(
        jnp.concatenate(split3(total), axis=0).astype(BF16),
        table_ref[...],
        preferred_element_type=F32,
    )
    native = native[:rows] + (native[rows : 2 * rows] + native[2 * rows :])
    kernel_grad_ref[...] = native[:, :cols]
    copies[0].start()

    for copy in copies:
        copy.wait()


def call(kernel, outs, specs, scratch=(), limit=None, out_specs=None, cost=None, alias=None):
    limit = limit or lax.axis_size("slab") * MIB
    return pl.pallas_call(
        kernel,
        out_shape=outs,
        in_specs=specs,
        out_specs=out_specs or [VMEM] * len(outs),
        cost_estimate=cost,
        input_output_aliases=alias or {},
        scratch_shapes=list(scratch),
        compiler_params=pltpu.CompilerParams(vmem_limit_bytes=limit),
    )


def partner(index, step, size):
    return index ^ step if size & (size - 1) == 0 else (index + step) % size


def shifts(arrays, axis):
    size = lax.axis_size(axis)
    moved = [arrays[0]]
    for i in range(1, size):
        moved.append(lax.ppermute(arrays[i], axis, [(j, (j + i) % size) for j in range(size)]))
    return moved


def chip_swaps(arrays, axis):
    size = lax.axis_size(axis)
    moved = [arrays[0]]
    for t in range(1, size // 2):
        pairs = [(j, 2 * partner(j // 2, t, size // 2) + j % 2) for j in range(size)]
        moved.append(lax.ppermute(arrays[t], axis, pairs))
    return moved


def core_swap(array, axis):
    return lax.ppermute(array, axis, [(j, j ^ 1) for j in range(lax.axis_size(axis))])


def body(video, clip_blocks, deal_order, kernel, gain, bias, cotangent):
    devs, slab = lax.axis_size("clips"), lax.axis_size("slab")
    held, frames, _, columns, c_in = video.shape
    slots, clips = cotangent.shape[0], clip_blocks.shape[0]
    c_out = gain.shape[0]
    rows_in, cols = kernel.shape
    och = c_out // slab
    per_group = c_out // GROUPS
    width = round_up(cols, LANES)
    places = held * frames * columns
    block_rows = FB * columns
    fold_rows = round_up(-(-block_rows // (LANES // och)), 8)
    chips = devs // 2
    everyone = ("clips", "slab")
    act_shape = (devs * slab, 2, fold_rows // 2 * LANES + LANES)
    shape = jax.ShapeDtypeStruct
    smem = [pltpu.SMEM((clips,), jnp.int32), pltpu.SMEM((devs,), jnp.int32)]
    large = (6 + 3 * slab) * MIB
    gain, bias = gain.reshape(1, c_out), bias.reshape(1, c_out)
    clip_blocks = pltpu.with_memory_space_constraint(clip_blocks, pltpu.HBM)
    deal_order = pltpu.with_memory_space_constraint(deal_order, pltpu.HBM)
    cotangent_blocks = pltpu.with_memory_space_constraint(
        cotangent.reshape(slots, block_rows, c_out), pltpu.HBM
    )

    videos = shifts([video.reshape(places, c_in)] * slab, "slab")
    cots, holds, slot_of = call(
        functools.partial(send_kernel, (devs, slab, slots, clips, held, och)),
        [pltpu.HBM((devs * slab, fold_rows, LANES), BF16), shape((slots * devs, 1, LANES), F32)]
        + [shape((held * BMAX * devs, 1, LANES), F32)],
        [HBM, HBM, HBM],
        smem
        + [
            pltpu.VMEM((slots, block_rows, c_out), BF16),
            pltpu.VMEM((devs * slab, fold_rows, LANES), BF16),
            pltpu.SemaphoreType.DMA((4,)),
        ],
        out_specs=[HBM, VMEM, VMEM],
        cost=pl.CostEstimate(flops=FIRST, bytes_accessed=0, transcendentals=0),
    )(clip_blocks, deal_order, cotangent_blocks)
    cots = lax.all_to_all(cots, everyone, split_axis=0, concat_axis=0, tiled=True)
    shards = [kernel]
    while len(shards) < chips:
        pairs = [(j, j ^ (2 * len(shards))) for j in range(devs)]
        shards = shards + [lax.ppermute(shard, "clips", pairs) for shard in shards]
    shards = shards + [core_swap(shard, "clips") for shard in shards]

    dims = (devs, slab, clips, held, frames, columns, rows_in, cols, och, per_group)
    video_pad, table = call(
        functools.partial(stage_kernel, slab, och),
        [shape((slab + 2, places, c_in), BF16), shape((width, 9 * LANES), BF16)],
        [HBM] + [VMEM] * (slab - 1),
        [pltpu.SemaphoreType.DMA((1,))],
        cost=pl.CostEstimate(flops=STAGE, bytes_accessed=0, transcendentals=0),
    )(pltpu.with_memory_space_constraint(videos[0], pltpu.HBM), *videos[:0:-1])
    weights, video_t, normed, inv_std, slope, act = call(
        functools.partial(forward_kernel, dims),
        [
            shape((9 * LANES, c_in), BF16),
            shape((c_in, slab * places), BF16),
            shape((slab, places, och), F32),
            shape((held, 8, och), F32),
            shape((slab, places, och), F32),
            pltpu.HBM(act_shape, BF16),
        ],
        [HBM] + [VMEM] * (devs + 5),
        [
            pltpu.VMEM(act_shape, BF16),
            pltpu.VMEM((devs, rows_in, width), F32 if rows_in % 16 else BF16),
            smem[0],
            pltpu.SemaphoreType.DMA((2,)),
        ],
        large,
        [VMEM] * 5 + [HBM],
    )(clip_blocks, slot_of, gain, bias, *shards, video_pad, table)
    acts, keep, send, *video_grads = call(
        functools.partial(backward_kernel, dims),
        [
            pltpu.HBM(act_shape, BF16),
            shape((chips, rows_in, 9 * LANES), F32),
            shape((chips, rows_in, 9 * LANES), BF16),
        ]
        + [shape((places, c_in), F32 if i == 0 else BF16) for i in range(slab)],
        [VMEM] * 7 + [HBM, VMEM],
        [
            pltpu.VMEM((devs * slab, 2, LANES), BF16),
            pltpu.VMEM((slab + 2, places, 3 * LANES), BF16),
            pltpu.VMEM((slab, places, c_in), F32),
            pltpu.SemaphoreType.DMA((1,)),
        ],
        large,
        [HBM] + [VMEM] * (2 + slab),
        alias={7: 0},
    )(slot_of, gain, weights, video_t, normed, inv_std, slope, act, cots)
    video_grads = shifts(video_grads, "slab")
    send = core_swap(send, "clips")
    acts = lax.all_to_all(acts, everyone, split_axis=0, concat_axis=0, tiled=True)
    kernel_grads = call(
        functools.partial(pair_kernel, chips),
        [shape((rows_in, cols), F32 if t == 0 else BF16) for t in range(chips)],
        [VMEM, VMEM],
    )(keep, send)
    table = call(
        functools.partial(table_kernel, och), [shape((width, width), BF16)], [ANY]
    )(kernel_grads[1])[0]
    kernel_grads = chip_swaps(kernel_grads, "clips")

    video_grad = call(
        sum_kernel,
        [shape((places, c_in), BF16)],
        [VMEM] * slab,
        cost=pl.CostEstimate(flops=STAGE, bytes_accessed=0, transcendentals=0),
    )(*video_grads)[0]
    outs = [
        ((rows_in, cols), F32),
        ((slots, block_rows, c_out), BF16),
        ((1, c_out), F32),
        ((1, c_out), F32),
    ]
    kernel_grad, act, gain_grad, bias_grad = call(
        functools.partial(finish_kernel, (devs, slab, slots, och)),
        [pltpu.HBM(*out) for out in outs],
        [VMEM] * (3 + chips),
        [pltpu.VMEM(*out) for out in outs] + [pltpu.SemaphoreType.DMA((4,))],
        2 * slab * MIB,
        [HBM] * 4,
    )(holds, acts, table, kernel_grads[0], *kernel_grads[:0:-1])
    return (
        act.reshape(cotangent.shape),
        video_grad.reshape(video.shape),
        kernel_grad,
        gain_grad.reshape(c_out),
        bias_grad.reshape(c_out),
    )


def solution(mesh):
    return jax.shard_map(
        body,
        mesh=mesh,
        in_specs=(
            P("clips", None, "slab", None, None),
            P(),
            P(),
            P("clips", "slab"),
            P(),
            P(),
            P("clips", None, "slab", None, None),
        ),
        out_specs=(
            P("clips", None, "slab", None, None),
            P("clips", None, "slab", None, None),
            P("clips", "slab"),
            P(),
            P(),
        ),
        check_vma=False,
    )
```

```python
import functools

import jax
import jax.numpy as jnp
from jax import lax
from jax.experimental import pallas as pl
from jax.experimental.pallas import tpu as pltpu
from jax.sharding import PartitionSpec as P

GROUPS = 16
TAPS = 27
FB = 2
BMAX = 3
LANES = 128
F32 = jnp.float32
BF16 = jnp.bfloat16
HBM = pl.BlockSpec(memory_space=pltpu.HBM)
ANY = pl.BlockSpec(memory_space=pl.ANY)
VMEM = pl.BlockSpec(memory_space=pltpu.VMEM)
MIB = 1024 * 1024
FIRST = 10**6
STAGE = 10**10


def round_up(value, unit):
    return -(-value // unit) * unit


def fold(values, slice_index, och, unit):
    groups = LANES // och
    rows = round_up(-(-values.shape[0] // groups), unit)
    short = rows * groups - values.shape[0]
    if short:
        values = jnp.concatenate([values, jnp.zeros((short, LANES), values.dtype)], axis=0)
    lane_group = lax.broadcasted_iota(jnp.int32, (rows, LANES), 1) // och
    total = jnp.zeros((rows, LANES), F32)
    for g in range(groups):
        shift = (g - slice_index) * och % LANES
        moved = pltpu.roll(values[g * rows : (g + 1) * rows], shift, 1) if shift else values[g * rows : (g + 1) * rows]
        total = total + jnp.where(lane_group == g, moved, 0.0)
    return total


def first_block_of(blocks_ref, first_clip, clips):
    start = jnp.int32(0)
    for k in range(clips):
        start = start + jnp.where(k < first_clip, blocks_ref[k], 0)
    return start


def slot_holders(blocks_ref, order_ref, me, slots, clips, held, devs):
    residue = jnp.int32(0)
    for r in range(devs):
        residue = jnp.where(order_ref[r] == me, r, residue)
    clip_of = [jnp.int32(0)] * slots
    end = jnp.int32(0)
    for k in range(clips):
        end = end + blocks_ref[k]
        for q in range(slots):
            clip_of[q] = clip_of[q] + jnp.where(end <= q * devs + residue, 1, 0)
    return [jnp.minimum(c, clips - 1) // held for c in clip_of]


def split3(values):
    high = values.astype(BF16).astype(F32)
    rest = values - high
    middle = rest.astype(BF16).astype(F32)
    return [high, middle, rest - middle]


def fetch(pairs, sems):
    copies = [pltpu.make_async_copy(a, b, sems.at[i]) for i, (a, b) in enumerate(pairs)]
    for copy in copies:
        copy.start()
    return copies


def send_kernel(
    dims,
    blocks_hbm,
    order_hbm,
    cot_hbm,
    out_ref,
    holds_ref,
    slots_ref,
    blocks_ref,
    order_ref,
    cot_ref,
    sems,
):
    devs, slab, slots, clips, held, och = dims
    pairs = [(blocks_hbm, blocks_ref), (order_hbm, order_ref), (cot_hbm, cot_ref)]
    copies = fetch(pairs, sems)
    out_ref[...] = jnp.zeros_like(out_ref)
    for copy in copies:
        copy.wait()
    me = lax.axis_index("clips")
    start = first_block_of(blocks_ref, me * held, clips)
    for k in range(held):
        count = blocks_ref[me * held + k]
        for b in range(BMAX):
            device = jnp.where(b < count, order_ref[jnp.mod(start + b, devs)], devs)
            for d in range(devs):
                hit = jnp.where(device == d, 1.0, 0.0)
                slots_ref[(k * BMAX + b) * devs + d] = jnp.full((1, LANES), hit, F32)
        start = start + count
    holders = slot_holders(blocks_ref, order_ref, me, slots, clips, held, devs)
    for q in range(slots):
        block = cot_ref[q].astype(F32)
        for s in range(slab):
            out_ref[holders[q] * slab + s] = fold(block, s, och, 8).astype(BF16)
        for d in range(devs):
            holds_ref[q * devs + d] = jnp.full((1, LANES), jnp.where(holders[q] == d, 1.0, 0.0), F32)


def make_table(och, out_ref):
    rows = out_ref.shape[0]
    lane = lax.broadcasted_iota(jnp.int32, (8, LANES), 1)
    source = jnp.where(lane < 3 * och, 27 * (lane % och) + 9 * (2 - lane // och), -rows)
    ahead = source - lax.broadcasted_iota(jnp.int32, (8, LANES), 0)
    for group in range(9):
        for i in range(0, rows, 16):
            top = jnp.where(ahead == i - group, 1.0, 0.0)
            bottom = jnp.where(ahead == i + 8 - group, 1.0, 0.0)
            both = jnp.concatenate([top, bottom], axis=0).astype(BF16)
            out_ref[i : i + 16, group * LANES : (group + 1) * LANES] = both


def stage_kernel(slab, och, *refs):
    video_refs, video_pad, table_ref, sems = refs[1:slab], refs[slab], refs[slab + 1], refs[slab + 2]
    own = lax.axis_index("slab")
    copy = fetch([(refs[0], video_pad.at[own + 1])], sems)[0]
    make_table(och, table_ref)
    zeros = jnp.zeros(video_pad.shape[1:], BF16)
    video_pad[0] = zeros
    video_pad[slab + 1] = zeros
    for i in range(1, slab):
        video_pad[jnp.mod(own - i + slab, slab) + 1] = video_refs[-i][...]
    copy.wait()


def forward_kernel(dims, blocks_hbm, slots_ref, gain_ref, bias_ref, *refs):
    devs, slab, clips, held, frames, columns, rows_in, cols, och, per_group = dims
    shard_refs, video_pad, table_ref = refs[:devs], refs[devs], refs[devs + 1]
    weights_ref, video_t_ref, normed_ref, inv_ref, slope_ref, act_ref = refs[devs + 2 : devs + 8]
    act_hbm, act_ref = act_ref, refs[devs + 8]
    shards, blocks_ref, sems = refs[devs + 9 :]
    copy = fetch([(blocks_hbm, blocks_ref)], sems)[0]
    me, own = lax.axis_index("clips"), lax.axis_index("slab")
    places = held * frames * columns
    per_clip = frames * columns
    c_in = video_pad.shape[2]
    many = slab * places
    width = table_ref.shape[0]
    chips = devs // 2
    for t in range(chips):
        for e in range(2):
            source = 2 * ((me // 2) ^ t) + (me % 2 + e) % 2
            shard = shard_refs[t + e * chips][...].astype(F32)
            shard = jnp.concatenate([shard, jnp.zeros((rows_in, width - cols), F32)], axis=1)
            shards[source] = shard.astype(shards.dtype)
    weights = shards[...].reshape(c_in, width).astype(BF16)
    weights = jnp.dot(weights, table_ref[...], preferred_element_type=F32).astype(BF16)

    total = jnp.dot(
        jnp.concatenate([video_pad[b : b + slab].reshape(many, c_in) for b in range(3)], axis=1),
        jnp.concatenate([weights[:, 384 * b : 384 * (b + 1)] for b in range(3)], axis=0),
        preferred_element_type=F32,
    )
    mixed = (
        from_left(total[:, 0:LANES], columns)
        + total[:, LANES : 2 * LANES]
        + from_right(total[:, 2 * LANES :], columns)
    ).reshape(slab, places, LANES)
    frame_shifts = [mixed[:, :, a * och : (a + 1) * och] for a in range(3)]
    frame_of = lax.broadcasted_iota(jnp.int32, (slab, per_clip, och), 1) // columns
    shift = jnp.mod(LANES - own * och, LANES)
    gain = pltpu.roll(jnp.broadcast_to(gain_ref[...], (8, LANES)), shift, 1)[0:1, :och]
    bias = pltpu.roll(jnp.broadcast_to(bias_ref[...], (8, LANES)), shift, 1)[0:1, :och]
    block_rows = FB * columns
    copy.wait()
    convs, kept, counts, limits = [], [], [], []
    for k in range(held):
        blocks = blocks_ref[me * held + k]
        conv = frame_shifts[0][:, k * per_clip : (k + 1) * per_clip]
        for a in (1, 2):
            part = frame_shifts[a][:, k * per_clip : (k + 1) * per_clip - a * columns]
            conv = conv + jnp.concatenate([jnp.zeros((slab, a * columns, och), F32), part], axis=1)
        convs.append(conv)
        kept.append(jnp.where(frame_of < blocks * FB, conv, 0.0))
        count = (blocks * (FB * slab * columns * per_group)).astype(F32)
        counts.append(jnp.full((1, och), count, F32))
        limits.append(jnp.full((1, och), (blocks * FB).astype(F32), F32))
    sums = group_sums(kept + [a * b for a, b in zip(kept, convs)], per_group)
    act_blocks = []
    for k in range(held):
        conv = convs[k]
        mean = sums[k] / counts[k]
        inv_std = lax.rsqrt(sums[held + k] / counts[k] - mean * mean + 1e-05)
        inv_ref[k] = jnp.concatenate([inv_std, counts[k], limits[k], jnp.zeros((5, och), F32)], axis=0)
        mean, inv_std = mean[None], inv_std[None]
        normed = (conv - mean) * inv_std
        normed_ref[:, k * per_clip : (k + 1) * per_clip, :] = normed
        affine = normed * gain[None] + bias[None]
        sigmoid = jax.nn.sigmoid(affine)
        act = affine * sigmoid
        slope = sigmoid * (1.0 + affine * (1.0 - sigmoid))
        slope_ref[:, k * per_clip : (k + 1) * per_clip, :] = slope
        for b in range(BMAX):
            for h in range(slab):
                block = act[h, b * block_rows : (b + 1) * block_rows]
                act_blocks.append(unfolded_to_lanes(block, 8))
    for d in range(devs):
        for h in range(slab):
            total = None
            for j in range(held * BMAX):
                term = act_blocks[j * slab + h] * slots_ref[j * devs + d]
                total = term if total is None else total + term
            pairs = [total[i : i + 2] for i in range(0, total.shape[0], 2)] + [jnp.zeros((2, LANES), F32)]
            act_ref[d * slab + h] = jnp.concatenate(pairs, axis=1).astype(BF16)
    act_copy = pltpu.make_async_copy(act_ref, act_hbm, sems.at[1])
    act_copy.start()
    weights_ref[...] = jnp.transpose(weights)
    video_t_ref[...] = jnp.transpose(video_pad[1 : slab + 1].reshape(many, c_in))
    act_copy.wait()


def from_left(values, columns):
    column = lax.broadcasted_iota(jnp.int32, values.shape, 0) % columns
    return jnp.where(column > 0, pltpu.roll(values, 1, 0), 0.0)


def from_right(values, columns):
    column = lax.broadcasted_iota(jnp.int32, values.shape, 0) % columns
    return jnp.where(column < columns - 1, pltpu.roll(values, values.shape[0] - 1, 0), 0.0)


def group_sums(arrays, per_group):
    och = arrays[0].shape[-1]
    rows = [jnp.sum(jnp.sum(a, axis=0), axis=0, keepdims=True) for a in arrays]
    rows.append(jnp.zeros((-len(rows) % 8, och), F32))
    total = jnp.concatenate([r for r in rows if r.shape[0]], axis=0)
    if och < LANES:
        total = jnp.concatenate([total, jnp.zeros((total.shape[0], LANES - och), F32)], axis=1)
    lane = lax.broadcasted_iota(jnp.int32, total.shape, 1)
    step = 1
    while step < per_group:
        down, up = pltpu.roll(total, LANES - step, 1), pltpu.roll(total, step, 1)
        total = total + jnp.where((lane // step) % 2 == 0, down, up)
        step *= 2
    return [total[i : i + 1, :och] for i in range(len(arrays))]


def backward_kernel(dims, slots_ref, gain_ref, weights_ref, *refs):
    devs, slab, clips, held, frames, columns, rows_in, cols, och, per_group = dims
    video_t_ref, normed_ref, inv_ref, slope_ref, act_in, cot_ref = refs[:6]
    act_hbm, keep_ref, send_ref = refs[6:9]
    video_grad_refs = refs[9 : 9 + slab]
    sums_ref, grad_ref, rows_ref, sems = refs[9 + slab :]
    me, own = lax.axis_index("clips"), lax.axis_index("slab")
    places = held * frames * columns
    per_clip = frames * columns
    block_rows = FB * columns
    c_in = video_t_ref.shape[0]
    groups = LANES // och
    many = slab * places
    shift = jnp.mod(LANES - own * och, LANES)
    gain = pltpu.roll(jnp.broadcast_to(gain_ref[...], (8, LANES)), shift, 1)[0:1, :och]
    frame_of = lax.broadcasted_iota(jnp.int32, (slab, per_clip, och), 1) // columns
    frame_of = frame_of.astype(F32)
    gain_part = jnp.zeros((1, och), F32)
    bias_part = jnp.zeros((1, och), F32)
    blocks = [[None] * slab for _ in range(held * BMAX)]
    for d in range(devs):
        for s in range(slab):
            folded = cot_ref[d * slab + s].astype(F32)
            for j in range(held * BMAX):
                term = folded * slots_ref[j * devs + d]
                blocks[j][s] = term if d == 0 else blocks[j][s] + term
    normeds, grads, alives = [], [], []
    for k in range(held):
        cot = []
        for b in range(BMAX):
            rows = []
            for folded in blocks[k * BMAX + b]:
                parts = [folded[:, g * och : (g + 1) * och] for g in range(groups)]
                rows.append(jnp.concatenate(parts, axis=0)[:block_rows])
            cot.append(jnp.stack(rows, axis=0))
        cot = jnp.concatenate(cot, axis=1)
        alive = frame_of < inv_ref[k][None, 2:3]
        normed = normed_ref[:, k * per_clip : (k + 1) * per_clip, :]
        slope = slope_ref[:, k * per_clip : (k + 1) * per_clip, :]
        grad_affine = jnp.where(alive, cot * slope, 0.0)
        gain_part += jnp.sum(jnp.sum(grad_affine * normed, axis=0), axis=0, keepdims=True)
        bias_part += jnp.sum(jnp.sum(grad_affine, axis=0), axis=0, keepdims=True)
        normeds.append(normed)
        grads.append(grad_affine * gain[None])
        alives.append(alive)
    sums = group_sums(grads + [a * b for a, b in zip(grads, normeds)], per_group)
    conv_grads = []
    for k in range(held):
        inv_std, count = inv_ref[k][None, 0:1], inv_ref[k][1:2]
        mean_grad, mean_cross = (sums[k] / count)[None], (sums[held + k] / count)[None]
        grad_conv = inv_std * (grads[k] - mean_grad - normeds[k] * mean_cross)
        grad_conv = jnp.where(alives[k], grad_conv, 0.0).astype(BF16).astype(F32)
        lanes = [grad_conv]
        for a in (1, 2):
            zeros = jnp.zeros((slab, a * columns, och), F32)
            lanes.append(jnp.concatenate([grad_conv[:, a * columns :], zeros], axis=1))
        if LANES > 3 * och:
            lanes.append(jnp.zeros((slab, per_clip, LANES - 3 * och), F32))
        conv_grads.append(jnp.concatenate(lanes, axis=2))

    sums = split3(gain_part) + split3(bias_part)
    sums = [jnp.concatenate(sums[:4], axis=1), jnp.concatenate(sums[4:] + [jnp.zeros((1, 2 * och), F32)], axis=1)]
    sums = jnp.concatenate(sums, axis=0)
    if LANES > 4 * och:
        sums = jnp.concatenate([sums, jnp.zeros((2, LANES - 4 * och), F32)], axis=1)
    sums_ref[...] = jnp.broadcast_to(sums.astype(BF16)[None], sums_ref.shape)
    last = act_hbm.shape[2] - LANES
    sums_copy = pltpu.make_async_copy(sums_ref, act_hbm.at[:, :, last : last + LANES], sems.at[0])
    sums_copy.start()

    grads = jnp.concatenate(conv_grads, axis=1).reshape(many, LANES)
    grad_ref[0] = jnp.zeros((places, 3 * LANES), BF16)
    grad_ref[slab + 1] = jnp.zeros((places, 3 * LANES), BF16)
    for e, shifted in enumerate((from_right(grads, columns), grads, from_left(grads, columns))):
        shifted = shifted.astype(BF16).reshape(slab, places, LANES)
        grad_ref[1 : slab + 1, :, e * LANES : (e + 1) * LANES] = shifted

    moved = [grad_ref[2 - b : 2 - b + slab].reshape(many, 3 * LANES) for b in range(3)]
    moved = jnp.concatenate(moved, axis=1)
    total = jnp.dot(moved, weights_ref[...], preferred_element_type=F32)
    rows_ref[...] = total.reshape(slab, places, c_in)
    for i, ref in enumerate(video_grad_refs):
        ref[...] = rows_ref[jnp.mod(own + i, slab)].astype(ref.dtype)

    terms = jnp.dot(video_t_ref[...], moved, preferred_element_type=F32)
    terms = terms.reshape(devs // 2, 2 * rows_in, 9 * LANES)
    low, high = terms[:, :rows_in], terms[:, rows_in:]
    odd = me % 2 == 1
    keep_ref[...] = jnp.where(odd, high, low)
    send_ref[...] = jnp.where(odd, low, high).astype(BF16)
    sums_copy.wait()


def unfolded_to_lanes(values, unit):
    groups = LANES // values.shape[1]
    rows = round_up(-(-values.shape[0] // groups), unit)
    short = rows * groups - values.shape[0]
    if short:
        values = jnp.concatenate([values, jnp.zeros((short, values.shape[1]), F32)], axis=0)
    return jnp.concatenate([values[g * rows : (g + 1) * rows] for g in range(groups)], axis=1)


def pair_kernel(chips, keep_ref, other_ref, *outs):
    me = lax.axis_index("clips") // 2
    cols = outs[0].shape[1]
    used = cols // 9
    for t, ref in enumerate(outs):
        chip = partner(me, t, chips)
        total = keep_ref[chip] + other_ref[chip].astype(F32)
        parts = [total[:, g * LANES : g * LANES + used] for g in range(9)]
        ref[...] = jnp.concatenate(parts, axis=1).astype(ref.dtype)


def sum_kernel(*refs):
    total = refs[0][...]
    for ref in refs[1:-1]:
        total = total + ref[...].astype(F32)
    refs[-1][...] = total.astype(refs[-1].dtype)


def table_kernel(och, after_ref, table_ref):
    rows, cols = table_ref.shape
    place = lax.broadcasted_iota(jnp.int32, (LANES, LANES), 0)
    column = lax.broadcasted_iota(jnp.int32, (LANES, LANES), 1)
    for i in range(0, rows, LANES):
        inner = (place + i) % (3 * och)
        source = 27 * (inner % och) + 9 * (2 - inner // och) + (place + i) // (3 * och)
        ahead = jnp.where(place + i < 27 * och, source, -cols) - column
        for j in range(0, cols, LANES):
            table_ref[i : i + LANES, j : j + LANES] = jnp.where(ahead == j, 1.0, 0.0).astype(BF16)


def finish_kernel(dims, holds_ref, act_in, table_ref, *refs):
    devs, slab, slots, och = dims
    chips = devs // 2
    kernel_refs, hbm_refs = refs[:chips], refs[chips : chips + 4]
    out_refs, sems = refs[chips + 4 : chips + 8], refs[chips + 8]
    kernel_grad_ref, act_ref, gain_ref, bias_ref = out_refs
    copies = [pltpu.make_async_copy(a, b, sems.at[i]) for i, (a, b) in enumerate(zip(out_refs, hbm_refs))]

    total = kernel_refs[0][...]
    for ref in kernel_refs[1:]:
        total = total + ref[...].astype(F32)
    rows, cols = total.shape
    width = table_ref.shape[0]
    if width > cols:
        total = jnp.concatenate([total, jnp.zeros((rows, width - cols), F32)], axis=1)
    native = jnp.dot(
        jnp.concatenate(split3(total), axis=0).astype(BF16),
        table_ref[...],
        preferred_element_type=F32,
    )
    native = native[:rows] + (native[rows : 2 * rows] + native[2 * rows :])
    kernel_grad_ref[...] = native[:, :cols]
    copies[0].start()

    groups = LANES // och
    pairs = act_in.shape[2] // LANES - 1
    sums = []
    blocks = [[jnp.zeros((2 * pairs, LANES), F32)] * slab for _ in range(slots)]
    for s in range(slab):
        part = jnp.zeros((2, LANES), F32)
        for d in range(devs):
            both = act_in[d * slab + s].astype(F32)
            part = part + both[:, pairs * LANES :]
            both = [both[:, i * LANES : (i + 1) * LANES] for i in range(pairs)]
            both = jnp.concatenate(both, axis=0)
            for q in range(slots):
                blocks[q][s] = blocks[q][s] + both * holds_ref[q * devs + d]
        sums.append(part)
    for q in range(slots):
        block = []
        for g in range(groups):
            parts = [p[:, g * och : (g + 1) * och] for p in blocks[q]]
            block.append(jnp.concatenate(parts, axis=1))
        act_ref[q] = jnp.concatenate(block, axis=0)[: act_ref.shape[1]].astype(BF16)
    copies[1].start()
    gains = [p[0:1, :och] + (p[0:1, och : 2 * och] + p[0:1, 2 * och : 3 * och]) for p in sums]
    gain_ref[...] = jnp.concatenate(gains, axis=1)
    biases = [p[0:1, 3 * och : 4 * och] + (p[1:2, :och] + p[1:2, och : 2 * och]) for p in sums]
    bias_ref[...] = jnp.concatenate(biases, axis=1)
    copies[2].start()
    copies[3].start()
    for copy in copies:
        copy.wait()


def call(kernel, outs, specs, scratch=(), limit=None, out_specs=None, cost=None, alias=None):
    limit = limit or lax.axis_size("slab") * MIB
    return pl.pallas_call(
        kernel,
        out_shape=outs,
        in_specs=specs,
        out_specs=out_specs or [VMEM] * len(outs),
        cost_estimate=cost,
        input_output_aliases=alias or {},
        scratch_shapes=list(scratch),
        compiler_params=pltpu.CompilerParams(vmem_limit_bytes=limit),
    )


def partner(index, step, size):
    return index ^ step if size & (size - 1) == 0 else (index + step) % size


def shifts(arrays, axis):
    size = lax.axis_size(axis)
    moved = [arrays[0]]
    for i in range(1, size):
        moved.append(lax.ppermute(arrays[i], axis, [(j, (j + i) % size) for j in range(size)]))
    return moved


def chip_swaps(arrays, axis):
    size = lax.axis_size(axis)
    moved = [arrays[0]]
    for t in range(1, size // 2):
        pairs = [(j, 2 * partner(j // 2, t, size // 2) + j % 2) for j in range(size)]
        moved.append(lax.ppermute(arrays[t], axis, pairs))
    return moved


def core_swap(array, axis):
    return lax.ppermute(array, axis, [(j, j ^ 1) for j in range(lax.axis_size(axis))])


def body(video, clip_blocks, deal_order, kernel, gain, bias, cotangent):
    devs, slab = lax.axis_size("clips"), lax.axis_size("slab")
    held, frames, _, columns, c_in = video.shape
    slots, clips = cotangent.shape[0], clip_blocks.shape[0]
    c_out = gain.shape[0]
    rows_in, cols = kernel.shape
    och = c_out // slab
    per_group = c_out // GROUPS
    width = round_up(cols, LANES)
    places = held * frames * columns
    block_rows = FB * columns
    fold_rows = round_up(-(-block_rows // (LANES // och)), 8)
    chips = devs // 2
    everyone = ("clips", "slab")
    act_shape = (devs * slab, 2, fold_rows // 2 * LANES + LANES)
    shape = jax.ShapeDtypeStruct
    smem = [pltpu.SMEM((clips,), jnp.int32), pltpu.SMEM((devs,), jnp.int32)]
    large = (6 + 3 * slab) * MIB
    gain, bias = gain.reshape(1, c_out), bias.reshape(1, c_out)
    clip_blocks = pltpu.with_memory_space_constraint(clip_blocks, pltpu.HBM)
    deal_order = pltpu.with_memory_space_constraint(deal_order, pltpu.HBM)
    cotangent_blocks = pltpu.with_memory_space_constraint(
        cotangent.reshape(slots, block_rows, c_out), pltpu.HBM
    )

    videos = shifts([video.reshape(places, c_in)] * slab, "slab")
    cots, holds, slot_of = call(
        functools.partial(send_kernel, (devs, slab, slots, clips, held, och)),
        [shape((devs * slab, fold_rows, LANES), BF16), shape((slots * devs, 1, LANES), F32)]
        + [shape((held * BMAX * devs, 1, LANES), F32)],
        [HBM, HBM, HBM],
        smem + [pltpu.VMEM((slots, block_rows, c_out), BF16), pltpu.SemaphoreType.DMA((3,))],
        cost=pl.CostEstimate(flops=FIRST, bytes_accessed=0, transcendentals=0),
    )(clip_blocks, deal_order, cotangent_blocks)
    cots = lax.all_to_all(cots, everyone, split_axis=0, concat_axis=0, tiled=True)
    shards = [kernel]
    while len(shards) < chips:
        pairs = [(j, j ^ (2 * len(shards))) for j in range(devs)]
        shards = shards + [lax.ppermute(shard, "clips", pairs) for shard in shards]
    shards = shards + [core_swap(shard, "clips") for shard in shards]

    dims = (devs, slab, clips, held, frames, columns, rows_in, cols, och, per_group)
    video_pad, table = call(
        functools.partial(stage_kernel, slab, och),
        [shape((slab + 2, places, c_in), BF16), shape((width, 9 * LANES), BF16)],
        [HBM] + [VMEM] * (slab - 1),
        [pltpu.SemaphoreType.DMA((1,))],
        cost=pl.CostEstimate(flops=STAGE, bytes_accessed=0, transcendentals=0),
    )(pltpu.with_memory_space_constraint(videos[0], pltpu.HBM), *videos[:0:-1])
    weights, video_t, normed, inv_std, slope, act = call(
        functools.partial(forward_kernel, dims),
        [
            shape((9 * LANES, c_in), BF16),
            shape((c_in, slab * places), BF16),
            shape((slab, places, och), F32),
            shape((held, 8, och), F32),
            shape((slab, places, och), F32),
            pltpu.HBM(act_shape, BF16),
        ],
        [HBM] + [VMEM] * (devs + 5),
        [
            pltpu.VMEM(act_shape, BF16),
            pltpu.VMEM((devs, rows_in, width), F32 if rows_in % 16 else BF16),
            smem[0],
            pltpu.SemaphoreType.DMA((2,)),
        ],
        large,
        [VMEM] * 5 + [HBM],
    )(clip_blocks, slot_of, gain, bias, *shards, video_pad, table)
    acts, keep, send, *video_grads = call(
        functools.partial(backward_kernel, dims),
        [
            pltpu.HBM(act_shape, BF16),
            shape((chips, rows_in, 9 * LANES), F32),
            shape((chips, rows_in, 9 * LANES), BF16),
        ]
        + [shape((places, c_in), F32 if i == 0 else BF16) for i in range(slab)],
        [VMEM] * 7 + [HBM, VMEM],
        [
            pltpu.VMEM((devs * slab, 2, LANES), BF16),
            pltpu.VMEM((slab + 2, places, 3 * LANES), BF16),
            pltpu.VMEM((slab, places, c_in), F32),
            pltpu.SemaphoreType.DMA((1,)),
        ],
        large,
        [HBM] + [VMEM] * (2 + slab),
        alias={7: 0},
    )(slot_of, gain, weights, video_t, normed, inv_std, slope, act, cots)
    video_grads = shifts(video_grads, "slab")
    send = core_swap(send, "clips")
    acts = lax.all_to_all(acts, everyone, split_axis=0, concat_axis=0, tiled=True)
    kernel_grads = call(
        functools.partial(pair_kernel, chips),
        [shape((rows_in, cols), F32 if t == 0 else BF16) for t in range(chips)],
        [VMEM, VMEM],
    )(keep, send)
    table = call(
        functools.partial(table_kernel, och), [shape((width, width), BF16)], [ANY]
    )(kernel_grads[1])[0]
    kernel_grads = chip_swaps(kernel_grads, "clips")

    video_grad = call(
        sum_kernel,
        [shape((places, c_in), BF16)],
        [VMEM] * slab,
        cost=pl.CostEstimate(flops=STAGE, bytes_accessed=0, transcendentals=0),
    )(*video_grads)[0]
    outs = [
        ((rows_in, cols), F32),
        ((slots, block_rows, c_out), BF16),
        ((1, c_out), F32),
        ((1, c_out), F32),
    ]
    kernel_grad, act, gain_grad, bias_grad = call(
        functools.partial(finish_kernel, (devs, slab, slots, och)),
        [pltpu.HBM(*out) for out in outs],
        [VMEM] * (3 + chips),
        [pltpu.VMEM(*out) for out in outs] + [pltpu.SemaphoreType.DMA((4,))],
        2 * slab * MIB,
        [HBM] * 4,
    )(holds, acts, table, kernel_grads[0], *kernel_grads[2:], kernel_grads[1])
    return (
        act.reshape(cotangent.shape),
        video_grad.reshape(video.shape),
        kernel_grad,
        gain_grad.reshape(c_out),
        bias_grad.reshape(c_out),
    )


def solution(mesh):
    return jax.shard_map(
        body,
        mesh=mesh,
        in_specs=(
            P("clips", None, "slab", None, None),
            P(),
            P(),
            P("clips", "slab"),
            P(),
            P(),
            P("clips", None, "slab", None, None),
        ),
        out_specs=(
            P("clips", None, "slab", None, None),
            P("clips", None, "slab", None, None),
            P("clips", "slab"),
            P(),
            P(),
        ),
        check_vma=False,
    )
```

```python
import functools

import jax
import jax.numpy as jnp
from jax import lax
from jax.experimental import pallas as pl
from jax.experimental.pallas import tpu as pltpu
from jax.sharding import PartitionSpec as P

GROUPS = 16
TAPS = 27
FB = 2
BMAX = 3
LANES = 128
F32 = jnp.float32
BF16 = jnp.bfloat16
HBM = pl.BlockSpec(memory_space=pltpu.HBM)
ANY = pl.BlockSpec(memory_space=pl.ANY)
VMEM = pl.BlockSpec(memory_space=pltpu.VMEM)
MIB = 1024 * 1024
FIRST = 10**6
STAGE = 10**10


def round_up(value, unit):
    return -(-value // unit) * unit


def fold(values, slice_index, och, unit):
    groups = LANES // och
    rows = round_up(-(-values.shape[0] // groups), unit)
    short = rows * groups - values.shape[0]
    if short:
        values = jnp.concatenate([values, jnp.zeros((short, LANES), values.dtype)], axis=0)
    lane_group = lax.broadcasted_iota(jnp.int32, (rows, LANES), 1) // och
    total = jnp.zeros((rows, LANES), F32)
    for g in range(groups):
        shift = (g - slice_index) * och % LANES
        moved = pltpu.roll(values[g * rows : (g + 1) * rows], shift, 1) if shift else values[g * rows : (g + 1) * rows]
        total = total + jnp.where(lane_group == g, moved, 0.0)
    return total


def first_block_of(blocks_ref, first_clip, clips):
    start = jnp.int32(0)
    for k in range(clips):
        start = start + jnp.where(k < first_clip, blocks_ref[k], 0)
    return start


def slot_holders(blocks_ref, order_ref, me, slots, clips, held, devs):
    residue = jnp.int32(0)
    for r in range(devs):
        residue = jnp.where(order_ref[r] == me, r, residue)
    clip_of = [jnp.int32(0)] * slots
    end = jnp.int32(0)
    for k in range(clips):
        end = end + blocks_ref[k]
        for q in range(slots):
            clip_of[q] = clip_of[q] + jnp.where(end <= q * devs + residue, 1, 0)
    return [jnp.minimum(c, clips - 1) // held for c in clip_of]


def split3(values):
    high = values.astype(BF16).astype(F32)
    rest = values - high
    middle = rest.astype(BF16).astype(F32)
    return [high, middle, rest - middle]


def fetch(pairs, sems):
    copies = [pltpu.make_async_copy(a, b, sems.at[i]) for i, (a, b) in enumerate(pairs)]
    for copy in copies:
        copy.start()
    return copies


def send_kernel(
    dims,
    blocks_hbm,
    order_hbm,
    cot_hbm,
    out_ref,
    holds_ref,
    slots_ref,
    blocks_ref,
    order_ref,
    cot_ref,
    sems,
):
    devs, slab, slots, clips, held, och = dims
    pairs = [(blocks_hbm, blocks_ref), (order_hbm, order_ref), (cot_hbm, cot_ref)]
    copies = fetch(pairs, sems)
    out_ref[...] = jnp.zeros_like(out_ref)
    copies[0].wait()
    copies[1].wait()
    me = lax.axis_index("clips")
    start = first_block_of(blocks_ref, me * held, clips)
    for k in range(held):
        count = blocks_ref[me * held + k]
        for b in range(BMAX):
            device = jnp.where(b < count, order_ref[jnp.mod(start + b, devs)], devs)
            for d in range(devs):
                hit = jnp.where(device == d, 1.0, 0.0)
                slots_ref[(k * BMAX + b) * devs + d] = jnp.full((1, LANES), hit, F32)
        start = start + count
    holders = slot_holders(blocks_ref, order_ref, me, slots, clips, held, devs)
    copies[2].wait()
    for q in range(slots):
        block = cot_ref[q].astype(F32)
        for s in range(slab):
            out_ref[holders[q] * slab + s] = fold(block, s, och, 8).astype(BF16)
        for d in range(devs):
            holds_ref[q * devs + d] = jnp.full((1, LANES), jnp.where(holders[q] == d, 1.0, 0.0), F32)


def make_table(och, out_ref):
    rows = out_ref.shape[0]
    lane = lax.broadcasted_iota(jnp.int32, (8, LANES), 1)
    source = jnp.where(lane < 3 * och, 27 * (lane % och) + 9 * (2 - lane // och), -rows)
    ahead = source - lax.broadcasted_iota(jnp.int32, (8, LANES), 0)
    for group in range(9):
        for i in range(0, rows, 16):
            top = jnp.where(ahead == i - group, 1.0, 0.0)
            bottom = jnp.where(ahead == i + 8 - group, 1.0, 0.0)
            both = jnp.concatenate([top, bottom], axis=0).astype(BF16)
            out_ref[i : i + 16, group * LANES : (group + 1) * LANES] = both


def stage_kernel(slab, och, *refs):
    video_refs, video_pad, table_ref, sems = refs[1:slab], refs[slab], refs[slab + 1], refs[slab + 2]
    own = lax.axis_index("slab")
    copy = fetch([(refs[0], video_pad.at[own + 1])], sems)[0]
    make_table(och, table_ref)
    zeros = jnp.zeros(video_pad.shape[1:], BF16)
    video_pad[0] = zeros
    video_pad[slab + 1] = zeros
    for i in range(1, slab):
        video_pad[jnp.mod(own - i + slab, slab) + 1] = video_refs[-i][...]
    copy.wait()


def forward_kernel(dims, blocks_hbm, slots_ref, gain_ref, bias_ref, *refs):
    devs, slab, clips, held, frames, columns, rows_in, cols, och, per_group = dims
    shard_refs, video_pad, table_ref = refs[:devs], refs[devs], refs[devs + 1]
    weights_ref, video_t_ref, normed_ref, inv_ref, slope_ref, act_ref = refs[devs + 2 : devs + 8]
    act_hbm, act_ref = act_ref, refs[devs + 8]
    shards, blocks_ref, sems = refs[devs + 9 :]
    copy = fetch([(blocks_hbm, blocks_ref)], sems)[0]
    me, own = lax.axis_index("clips"), lax.axis_index("slab")
    places = held * frames * columns
    per_clip = frames * columns
    c_in = video_pad.shape[2]
    many = slab * places
    width = table_ref.shape[0]
    chips = devs // 2
    for t in range(chips):
        for e in range(2):
            source = 2 * ((me // 2) ^ t) + (me % 2 + e) % 2
            shard = shard_refs[t + e * chips][...].astype(F32)
            shard = jnp.concatenate([shard, jnp.zeros((rows_in, width - cols), F32)], axis=1)
            shards[source] = shard.astype(shards.dtype)
    weights = shards[...].reshape(c_in, width).astype(BF16)
    weights = jnp.dot(weights, table_ref[...], preferred_element_type=F32).astype(BF16)

    total = jnp.dot(
        jnp.concatenate([video_pad[b : b + slab].reshape(many, c_in) for b in range(3)], axis=1),
        jnp.concatenate([weights[:, 384 * b : 384 * (b + 1)] for b in range(3)], axis=0),
        preferred_element_type=F32,
    )
    mixed = (
        from_left(total[:, 0:LANES], columns)
        + total[:, LANES : 2 * LANES]
        + from_right(total[:, 2 * LANES :], columns)
    ).reshape(slab, places, LANES)
    frame_shifts = [mixed[:, :, a * och : (a + 1) * och] for a in range(3)]
    frame_of = lax.broadcasted_iota(jnp.int32, (slab, per_clip, och), 1) // columns
    shift = jnp.mod(LANES - own * och, LANES)
    gain = pltpu.roll(jnp.broadcast_to(gain_ref[...], (8, LANES)), shift, 1)[0:1, :och]
    bias = pltpu.roll(jnp.broadcast_to(bias_ref[...], (8, LANES)), shift, 1)[0:1, :och]
    block_rows = FB * columns
    copy.wait()
    convs, kept, counts, limits = [], [], [], []
    for k in range(held):
        blocks = blocks_ref[me * held + k]
        conv = frame_shifts[0][:, k * per_clip : (k + 1) * per_clip]
        for a in (1, 2):
            part = frame_shifts[a][:, k * per_clip : (k + 1) * per_clip - a * columns]
            conv = conv + jnp.concatenate([jnp.zeros((slab, a * columns, och), F32), part], axis=1)
        convs.append(conv)
        kept.append(jnp.where(frame_of < blocks * FB, conv, 0.0))
        count = (blocks * (FB * slab * columns * per_group)).astype(F32)
        counts.append(jnp.full((1, och), count, F32))
        limits.append(jnp.full((1, och), (blocks * FB).astype(F32), F32))
    sums = group_sums(kept + [a * b for a, b in zip(kept, convs)], per_group)
    act_blocks = []
    for k in range(held):
        conv = convs[k]
        mean = sums[k] / counts[k]
        inv_std = lax.rsqrt(sums[held + k] / counts[k] - mean * mean + 1e-05)
        inv_ref[k] = jnp.concatenate([inv_std, counts[k], limits[k], jnp.zeros((5, och), F32)], axis=0)
        mean, inv_std = mean[None], inv_std[None]
        normed = (conv - mean) * inv_std
        normed_ref[:, k * per_clip : (k + 1) * per_clip, :] = normed
        affine = normed * gain[None] + bias[None]
        sigmoid = jax.nn.sigmoid(affine)
        act = affine * sigmoid
        slope = sigmoid * (1.0 + affine * (1.0 - sigmoid))
        slope_ref[:, k * per_clip : (k + 1) * per_clip, :] = slope
        for b in range(BMAX):
            for h in range(slab):
                block = act[h, b * block_rows : (b + 1) * block_rows]
                act_blocks.append(unfolded_to_lanes(block, 8))
    for d in range(devs):
        for h in range(slab):
            total = None
            for j in range(held * BMAX):
                term = act_blocks[j * slab + h] * slots_ref[j * devs + d]
                total = term if total is None else total + term
            pairs = [total[i : i + 2] for i in range(0, total.shape[0], 2)] + [jnp.zeros((2, LANES), F32)]
            act_ref[d * slab + h] = jnp.concatenate(pairs, axis=1).astype(BF16)
    act_copy = pltpu.make_async_copy(act_ref, act_hbm, sems.at[1])
    act_copy.start()
    weights_ref[...] = jnp.transpose(weights)
    video_t_ref[...] = jnp.transpose(video_pad[1 : slab + 1].reshape(many, c_in))
    act_copy.wait()


def from_left(values, columns):
    column = lax.broadcasted_iota(jnp.int32, values.shape, 0) % columns
    return jnp.where(column > 0, pltpu.roll(values, 1, 0), 0.0)


def from_right(values, columns):
    column = lax.broadcasted_iota(jnp.int32, values.shape, 0) % columns
    return jnp.where(column < columns - 1, pltpu.roll(values, values.shape[0] - 1, 0), 0.0)


def group_sums(arrays, per_group):
    och = arrays[0].shape[-1]
    rows = [jnp.sum(jnp.sum(a, axis=0), axis=0, keepdims=True) for a in arrays]
    rows.append(jnp.zeros((-len(rows) % 8, och), F32))
    total = jnp.concatenate([r for r in rows if r.shape[0]], axis=0)
    if och < LANES:
        total = jnp.concatenate([total, jnp.zeros((total.shape[0], LANES - och), F32)], axis=1)
    lane = lax.broadcasted_iota(jnp.int32, total.shape, 1)
    step = 1
    while step < per_group:
        down, up = pltpu.roll(total, LANES - step, 1), pltpu.roll(total, step, 1)
        total = total + jnp.where((lane // step) % 2 == 0, down, up)
        step *= 2
    return [total[i : i + 1, :och] for i in range(len(arrays))]


def backward_kernel(dims, slots_ref, gain_ref, weights_ref, *refs):
    devs, slab, clips, held, frames, columns, rows_in, cols, och, per_group = dims
    video_t_ref, normed_ref, inv_ref, slope_ref, act_in, cot_ref = refs[:6]
    act_hbm, keep_ref, send_ref = refs[6:9]
    video_grad_refs = refs[9 : 9 + slab]
    sums_ref, grad_ref, rows_ref, sems = refs[9 + slab :]
    me, own = lax.axis_index("clips"), lax.axis_index("slab")
    places = held * frames * columns
    per_clip = frames * columns
    block_rows = FB * columns
    c_in = video_t_ref.shape[0]
    groups = LANES // och
    many = slab * places
    shift = jnp.mod(LANES - own * och, LANES)
    gain = pltpu.roll(jnp.broadcast_to(gain_ref[...], (8, LANES)), shift, 1)[0:1, :och]
    frame_of = lax.broadcasted_iota(jnp.int32, (slab, per_clip, och), 1) // columns
    frame_of = frame_of.astype(F32)
    gain_part = jnp.zeros((1, och), F32)
    bias_part = jnp.zeros((1, och), F32)
    blocks = [[None] * slab for _ in range(held * BMAX)]
    for d in range(devs):
        for s in range(slab):
            folded = cot_ref[d * slab + s].astype(F32)
            for j in range(held * BMAX):
                term = folded * slots_ref[j * devs + d]
                blocks[j][s] = term if d == 0 else blocks[j][s] + term
    normeds, grads, alives = [], [], []
    for k in range(held):
        cot = []
        for b in range(BMAX):
            rows = []
            for folded in blocks[k * BMAX + b]:
                parts = [folded[:, g * och : (g + 1) * och] for g in range(groups)]
                rows.append(jnp.concatenate(parts, axis=0)[:block_rows])
            cot.append(jnp.stack(rows, axis=0))
        cot = jnp.concatenate(cot, axis=1)
        alive = frame_of < inv_ref[k][None, 2:3]
        normed = normed_ref[:, k * per_clip : (k + 1) * per_clip, :]
        slope = slope_ref[:, k * per_clip : (k + 1) * per_clip, :]
        grad_affine = jnp.where(alive, cot * slope, 0.0)
        gain_part += jnp.sum(jnp.sum(grad_affine * normed, axis=0), axis=0, keepdims=True)
        bias_part += jnp.sum(jnp.sum(grad_affine, axis=0), axis=0, keepdims=True)
        normeds.append(normed)
        grads.append(grad_affine * gain[None])
        alives.append(alive)
    sums = group_sums(grads + [a * b for a, b in zip(grads, normeds)], per_group)
    conv_grads = []
    for k in range(held):
        inv_std, count = inv_ref[k][None, 0:1], inv_ref[k][1:2]
        mean_grad, mean_cross = (sums[k] / count)[None], (sums[held + k] / count)[None]
        grad_conv = inv_std * (grads[k] - mean_grad - normeds[k] * mean_cross)
        grad_conv = jnp.where(alives[k], grad_conv, 0.0).astype(BF16).astype(F32)
        lanes = [grad_conv]
        for a in (1, 2):
            zeros = jnp.zeros((slab, a * columns, och), F32)
            lanes.append(jnp.concatenate([grad_conv[:, a * columns :], zeros], axis=1))
        if LANES > 3 * och:
            lanes.append(jnp.zeros((slab, per_clip, LANES - 3 * och), F32))
        conv_grads.append(jnp.concatenate(lanes, axis=2))

    sums = split3(gain_part) + split3(bias_part)
    sums = [jnp.concatenate(sums[:4], axis=1), jnp.concatenate(sums[4:] + [jnp.zeros((1, 2 * och), F32)], axis=1)]
    sums = jnp.concatenate(sums, axis=0)
    if LANES > 4 * och:
        sums = jnp.concatenate([sums, jnp.zeros((2, LANES - 4 * och), F32)], axis=1)
    sums_ref[...] = jnp.broadcast_to(sums.astype(BF16)[None], sums_ref.shape)
    last = act_hbm.shape[2] - LANES
    sums_copy = pltpu.make_async_copy(sums_ref, act_hbm.at[:, :, last : last + LANES], sems.at[0])
    sums_copy.start()

    grads = jnp.concatenate(conv_grads, axis=1).reshape(many, LANES)
    grad_ref[0] = jnp.zeros((places, 3 * LANES), BF16)
    grad_ref[slab + 1] = jnp.zeros((places, 3 * LANES), BF16)
    for e, shifted in enumerate((from_right(grads, columns), grads, from_left(grads, columns))):
        shifted = shifted.astype(BF16).reshape(slab, places, LANES)
        grad_ref[1 : slab + 1, :, e * LANES : (e + 1) * LANES] = shifted

    moved = [grad_ref[2 - b : 2 - b + slab].reshape(many, 3 * LANES) for b in range(3)]
    moved = jnp.concatenate(moved, axis=1)
    total = jnp.dot(moved, weights_ref[...], preferred_element_type=F32)
    rows_ref[...] = total.reshape(slab, places, c_in)
    for i, ref in enumerate(video_grad_refs):
        ref[...] = rows_ref[jnp.mod(own + i, slab)].astype(ref.dtype)

    terms = jnp.dot(video_t_ref[...], moved, preferred_element_type=F32)
    terms = terms.reshape(devs // 2, 2 * rows_in, 9 * LANES)
    low, high = terms[:, :rows_in], terms[:, rows_in:]
    odd = me % 2 == 1
    keep_ref[...] = jnp.where(odd, high, low)
    send_ref[...] = jnp.where(odd, low, high).astype(BF16)
    sums_copy.wait()


def unfolded_to_lanes(values, unit):
    groups = LANES // values.shape[1]
    rows = round_up(-(-values.shape[0] // groups), unit)
    short = rows * groups - values.shape[0]
    if short:
        values = jnp.concatenate([values, jnp.zeros((short, values.shape[1]), F32)], axis=0)
    return jnp.concatenate([values[g * rows : (g + 1) * rows] for g in range(groups)], axis=1)


def pair_kernel(chips, keep_ref, other_ref, *outs):
    me = lax.axis_index("clips") // 2
    cols = outs[0].shape[1]
    used = cols // 9
    for t, ref in enumerate(outs):
        chip = partner(me, t, chips)
        total = keep_ref[chip] + other_ref[chip].astype(F32)
        parts = [total[:, g * LANES : g * LANES + used] for g in range(9)]
        ref[...] = jnp.concatenate(parts, axis=1).astype(ref.dtype)


def sum_kernel(*refs):
    total = refs[0][...]
    for ref in refs[1:-1]:
        total = total + ref[...].astype(F32)
    refs[-1][...] = total.astype(refs[-1].dtype)


def table_kernel(och, after_ref, table_ref):
    rows, cols = table_ref.shape
    place = lax.broadcasted_iota(jnp.int32, (LANES, LANES), 0)
    column = lax.broadcasted_iota(jnp.int32, (LANES, LANES), 1)
    for i in range(0, rows, LANES):
        inner = (place + i) % (3 * och)
        source = 27 * (inner % och) + 9 * (2 - inner // och) + (place + i) // (3 * och)
        ahead = jnp.where(place + i < 27 * och, source, -cols) - column
        for j in range(0, cols, LANES):
            table_ref[i : i + LANES, j : j + LANES] = jnp.where(ahead == j, 1.0, 0.0).astype(BF16)


def finish_kernel(dims, holds_ref, act_in, table_ref, *refs):
    devs, slab, slots, och = dims
    chips = devs // 2
    kernel_refs, hbm_refs = refs[:chips], refs[chips : chips + 4]
    out_refs, sems = refs[chips + 4 : chips + 8], refs[chips + 8]
    kernel_grad_ref, act_ref, gain_ref, bias_ref = out_refs
    copies = [pltpu.make_async_copy(a, b, sems.at[i]) for i, (a, b) in enumerate(zip(out_refs, hbm_refs))]

    total = kernel_refs[0][...]
    for ref in kernel_refs[1:]:
        total = total + ref[...].astype(F32)
    rows, cols = total.shape
    width = table_ref.shape[0]
    if width > cols:
        total = jnp.concatenate([total, jnp.zeros((rows, width - cols), F32)], axis=1)
    native = jnp.dot(
        jnp.concatenate(split3(total), axis=0).astype(BF16),
        table_ref[...],
        preferred_element_type=F32,
    )
    native = native[:rows] + (native[rows : 2 * rows] + native[2 * rows :])
    kernel_grad_ref[...] = native[:, :cols]
    copies[0].start()

    groups = LANES // och
    pairs = act_in.shape[2] // LANES - 1
    sums = []
    blocks = [[jnp.zeros((2 * pairs, LANES), F32)] * slab for _ in range(slots)]
    for s in range(slab):
        part = jnp.zeros((2, LANES), F32)
        for d in range(devs):
            both = act_in[d * slab + s].astype(F32)
            part = part + both[:, pairs * LANES :]
            both = [both[:, i * LANES : (i + 1) * LANES] for i in range(pairs)]
            both = jnp.concatenate(both, axis=0)
            for q in range(slots):
                blocks[q][s] = blocks[q][s] + both * holds_ref[q * devs + d]
        sums.append(part)
    for q in range(slots):
        block = []
        for g in range(groups):
            parts = [p[:, g * och : (g + 1) * och] for p in blocks[q]]
            block.append(jnp.concatenate(parts, axis=1))
        act_ref[q] = jnp.concatenate(block, axis=0)[: act_ref.shape[1]].astype(BF16)
    copies[1].start()
    gains = [p[0:1, :och] + (p[0:1, och : 2 * och] + p[0:1, 2 * och : 3 * och]) for p in sums]
    gain_ref[...] = jnp.concatenate(gains, axis=1)
    biases = [p[0:1, 3 * och : 4 * och] + (p[1:2, :och] + p[1:2, och : 2 * och]) for p in sums]
    bias_ref[...] = jnp.concatenate(biases, axis=1)
    copies[2].start()
    copies[3].start()
    for copy in copies:
        copy.wait()


def call(kernel, outs, specs, scratch=(), limit=None, out_specs=None, cost=None, alias=None):
    limit = limit or lax.axis_size("slab") * MIB
    return pl.pallas_call(
        kernel,
        out_shape=outs,
        in_specs=specs,
        out_specs=out_specs or [VMEM] * len(outs),
        cost_estimate=cost,
        input_output_aliases=alias or {},
        scratch_shapes=list(scratch),
        compiler_params=pltpu.CompilerParams(vmem_limit_bytes=limit),
    )


def partner(index, step, size):
    return index ^ step if size & (size - 1) == 0 else (index + step) % size


def shifts(arrays, axis):
    size = lax.axis_size(axis)
    moved = [arrays[0]]
    for i in range(1, size):
        moved.append(lax.ppermute(arrays[i], axis, [(j, (j + i) % size) for j in range(size)]))
    return moved


def chip_swaps(arrays, axis):
    size = lax.axis_size(axis)
    moved = [arrays[0]]
    for t in range(1, size // 2):
        pairs = [(j, 2 * partner(j // 2, t, size // 2) + j % 2) for j in range(size)]
        moved.append(lax.ppermute(arrays[t], axis, pairs))
    return moved


def core_swap(array, axis):
    return lax.ppermute(array, axis, [(j, j ^ 1) for j in range(lax.axis_size(axis))])


def body(video, clip_blocks, deal_order, kernel, gain, bias, cotangent):
    devs, slab = lax.axis_size("clips"), lax.axis_size("slab")
    held, frames, _, columns, c_in = video.shape
    slots, clips = cotangent.shape[0], clip_blocks.shape[0]
    c_out = gain.shape[0]
    rows_in, cols = kernel.shape
    och = c_out // slab
    per_group = c_out // GROUPS
    width = round_up(cols, LANES)
    places = held * frames * columns
    block_rows = FB * columns
    fold_rows = round_up(-(-block_rows // (LANES // och)), 8)
    chips = devs // 2
    everyone = ("clips", "slab")
    act_shape = (devs * slab, 2, fold_rows // 2 * LANES + LANES)
    shape = jax.ShapeDtypeStruct
    smem = [pltpu.SMEM((clips,), jnp.int32), pltpu.SMEM((devs,), jnp.int32)]
    large = (6 + 3 * slab) * MIB
    gain, bias = gain.reshape(1, c_out), bias.reshape(1, c_out)
    clip_blocks = pltpu.with_memory_space_constraint(clip_blocks, pltpu.HBM)
    deal_order = pltpu.with_memory_space_constraint(deal_order, pltpu.HBM)
    cotangent_blocks = pltpu.with_memory_space_constraint(
        cotangent.reshape(slots, block_rows, c_out), pltpu.HBM
    )

    videos = shifts([video.reshape(places, c_in)] * slab, "slab")
    cots, holds, slot_of = call(
        functools.partial(send_kernel, (devs, slab, slots, clips, held, och)),
        [shape((devs * slab, fold_rows, LANES), BF16), shape((slots * devs, 1, LANES), F32)]
        + [shape((held * BMAX * devs, 1, LANES), F32)],
        [HBM, HBM, HBM],
        smem + [pltpu.VMEM((slots, block_rows, c_out), BF16), pltpu.SemaphoreType.DMA((3,))],
        cost=pl.CostEstimate(flops=FIRST, bytes_accessed=0, transcendentals=0),
    )(clip_blocks, deal_order, cotangent_blocks)
    cots = lax.all_to_all(cots, everyone, split_axis=0, concat_axis=0, tiled=True)
    shards = [kernel]
    while len(shards) < chips:
        pairs = [(j, j ^ (2 * len(shards))) for j in range(devs)]
        shards = shards + [lax.ppermute(shard, "clips", pairs) for shard in shards]
    shards = shards + [core_swap(shard, "clips") for shard in shards]

    dims = (devs, slab, clips, held, frames, columns, rows_in, cols, och, per_group)
    video_pad, table = call(
        functools.partial(stage_kernel, slab, och),
        [shape((slab + 2, places, c_in), BF16), shape((width, 9 * LANES), BF16)],
        [HBM] + [VMEM] * (slab - 1),
        [pltpu.SemaphoreType.DMA((1,))],
        cost=pl.CostEstimate(flops=STAGE, bytes_accessed=0, transcendentals=0),
    )(pltpu.with_memory_space_constraint(videos[0], pltpu.HBM), *videos[:0:-1])
    weights, video_t, normed, inv_std, slope, act = call(
        functools.partial(forward_kernel, dims),
        [
            shape((9 * LANES, c_in), BF16),
            shape((c_in, slab * places), BF16),
            shape((slab, places, och), F32),
            shape((held, 8, och), F32),
            shape((slab, places, och), F32),
            pltpu.HBM(act_shape, BF16),
        ],
        [HBM] + [VMEM] * (devs + 5),
        [
            pltpu.VMEM(act_shape, BF16),
            pltpu.VMEM((devs, rows_in, width), F32 if rows_in % 16 else BF16),
            smem[0],
            pltpu.SemaphoreType.DMA((2,)),
        ],
        large,
        [VMEM] * 5 + [HBM],
    )(clip_blocks, slot_of, gain, bias, *shards, video_pad, table)
    acts, keep, send, *video_grads = call(
        functools.partial(backward_kernel, dims),
        [
            pltpu.HBM(act_shape, BF16),
            shape((chips, rows_in, 9 * LANES), F32),
            shape((chips, rows_in, 9 * LANES), BF16),
        ]
        + [shape((places, c_in), F32 if i == 0 else BF16) for i in range(slab)],
        [VMEM] * 7 + [HBM, VMEM],
        [
            pltpu.VMEM((devs * slab, 2, LANES), BF16),
            pltpu.VMEM((slab + 2, places, 3 * LANES), BF16),
            pltpu.VMEM((slab, places, c_in), F32),
            pltpu.SemaphoreType.DMA((1,)),
        ],
        large,
        [HBM] + [VMEM] * (2 + slab),
        alias={7: 0},
    )(slot_of, gain, weights, video_t, normed, inv_std, slope, act, cots)
    video_grads = shifts(video_grads, "slab")
    send = core_swap(send, "clips")
    acts = lax.all_to_all(acts, everyone, split_axis=0, concat_axis=0, tiled=True)
    kernel_grads = call(
        functools.partial(pair_kernel, chips),
        [shape((rows_in, cols), F32 if t == 0 else BF16) for t in range(chips)],
        [VMEM, VMEM],
    )(keep, send)
    table = call(
        functools.partial(table_kernel, och), [shape((width, width), BF16)], [ANY]
    )(kernel_grads[1])[0]
    kernel_grads = chip_swaps(kernel_grads, "clips")

    video_grad = call(
        sum_kernel,
        [shape((places, c_in), BF16)],
        [VMEM] * slab,
        cost=pl.CostEstimate(flops=STAGE, bytes_accessed=0, transcendentals=0),
    )(*video_grads)[0]
    outs = [
        ((rows_in, cols), F32),
        ((slots, block_rows, c_out), BF16),
        ((1, c_out), F32),
        ((1, c_out), F32),
    ]
    kernel_grad, act, gain_grad, bias_grad = call(
        functools.partial(finish_kernel, (devs, slab, slots, och)),
        [pltpu.HBM(*out) for out in outs],
        [VMEM] * (3 + chips),
        [pltpu.VMEM(*out) for out in outs] + [pltpu.SemaphoreType.DMA((4,))],
        2 * slab * MIB,
        [HBM] * 4,
    )(holds, acts, table, kernel_grads[0], *kernel_grads[:0:-1])
    return (
        act.reshape(cotangent.shape),
        video_grad.reshape(video.shape),
        kernel_grad,
        gain_grad.reshape(c_out),
        bias_grad.reshape(c_out),
    )


def solution(mesh):
    return jax.shard_map(
        body,
        mesh=mesh,
        in_specs=(
            P("clips", None, "slab", None, None),
            P(),
            P(),
            P("clips", "slab"),
            P(),
            P(),
            P("clips", None, "slab", None, None),
        ),
        out_specs=(
            P("clips", None, "slab", None, None),
            P("clips", None, "slab", None, None),
            P("clips", "slab"),
            P(),
            P(),
        ),
        check_vma=False,
    )
```
